32 devices in a mesh: row: 4 (over y, x), col: 8 (over z, core).
Axes of the slice: x: 2, y: 2, z: 4, core: 2. Of those that a mesh axis runs over, the one named last changes fastest.
Arguments:
- film_embeds: float32 [4096, 1024], P(('row', 'col')), may hold values from -120 to 120
- text_embeds: float32 [4096, 1024], P(('col', 'row')), may hold values from -150 to 150
- matched_text_index: int32 [4096], replicated, may hold values from 0 to 4095, as said below
- sharpness_factor: float32 [1], replicated, may hold values from 20 to 60
- affinity_offset: float32 [1], replicated, may hold values from -12 to -6
Outputs:
- clip_loss: float32 [4096], P(('row', 'col'))
- grad_videos: float32 [4096, 1024], P(('row', 'col'))
- grad_captions: float32 [4096, 1024], P(('col', 'row'))
The draws below stay inside these ranges and needn't reach their ends.
Inputs may be any that keep to these rules, and one draw needn't show every extreme that they name: `matched_text_index`: each caption is the positive of exactly one clip.
All inputs are finite; a program needn't handle non-finite values.
Results may differ from the reference program's by a relative error of at most 0.0037.
Values may be sent and summed in bfloat16 or wider, within the bound.
No kernel may reach another device: no remote copies, remote signals or barrier semaphores. Data moves between devices by JAX's collectives and lax.ppermute only.
A program may use at most 128 MiB of HBM per device.

```python
import math
import jax
import jax.numpy as jnp
from jax import lax

D = 1024
ROWS_PER_DEVICE = 128
CLIPS = 4096
N_COL = 8


def pairing(key):
    return jax.random.permutation(jax.random.fold_in(key, 101), CLIPS).astype(jnp.int32)


def rough_noise(key, shape):
    values = jnp.clip(jax.random.normal(key, shape, jnp.float32), -4.0, 4.0)
    return values / D ** 0.5


def video_unit_vectors(key):
    device_groups = max(CLIPS // 16, 1)
    members = jax.random.randint(jax.random.fold_in(key, 102), (CLIPS,), 0, device_groups)
    centres = rough_noise(jax.random.fold_in(key, 103), (device_groups, D))
    noise = rough_noise(jax.random.fold_in(key, 104), (CLIPS, D))
    share = jax.random.uniform(jax.random.fold_in(key, 105), (CLIPS, 1), jnp.float32, 0.1, 0.4)
    directions = jnp.sqrt(share) * centres[members] + jnp.sqrt(1.0 - share) * noise
    return directions


def row_scales(key):
    logs = jax.random.uniform(key, (CLIPS, 1), jnp.float32, jnp.log(10.0), jnp.log(100.0))
    return jnp.exp(logs)


def draw_matched_text_index(key, part):
    return pairing(key)


def draw_film_embeds(key, part):
    directions = video_unit_vectors(key)
    return (directions * row_scales(jax.random.fold_in(key, 106))).astype(jnp.float32)


def draw_text_embeds(key, part):
    directions = video_unit_vectors(key)
    order = pairing(key)
    keep = jax.random.uniform(jax.random.fold_in(key, 107), (CLIPS, 1), jnp.float32, 0.2, 0.8)
    noise = rough_noise(jax.random.fold_in(key, 108), (CLIPS, D))
    by_clip = jnp.sqrt(keep) * directions + jnp.sqrt(1.0 - keep) * noise
    placed = jnp.zeros((CLIPS, D), jnp.float32).at[order].set(by_clip)
    return (placed * row_scales(jax.random.fold_in(key, 109))).astype(jnp.float32)


def setup_inputs(seed: int = 0) -> dict:
    key_list = jax.random.split(jax.random.key(seed), 6)
    return {
        "film_embeds": draw_film_embeds(jax.random.fold_in(key_list[5], 71), 0),
        "text_embeds": draw_text_embeds(jax.random.fold_in(key_list[5], 71), 0),
        "matched_text_index": draw_matched_text_index(jax.random.fold_in(key_list[5], 71), 0),
        "sharpness_factor": jnp.clip(jnp.exp(jax.random.uniform(key_list[3], (1,), jnp.float32, math.log(20.0), math.log(60.0))), 20.0, 60.0),
        "affinity_offset": jnp.clip(jax.random.uniform(key_list[4], (1,), jnp.float32, -12.0, -6.0), -12.0, -6.0),
    }


def normalize(embed):
    inverse = lax.rsqrt(lax.optimization_barrier(jnp.sum(embed * embed, axis=1, keepdims=True)) + 1e-06)
    return (embed * inverse, inverse)

def backward_norm(hat, inverse, grad_hat):
    return inverse * (grad_hat - hat * lax.optimization_barrier(jnp.sum(hat * grad_hat, axis=1, keepdims=True)))

def reference(film_embeds, text_embeds, matched_text_index, sharpness_factor, affinity_offset):
    vhat, vnorm = normalize(film_embeds)
    chat, cnorm = normalize(text_embeds)
    v16 = vhat.astype(jnp.bfloat16)
    c16 = chat.astype(jnp.bfloat16)
    similarity_multiplier = sharpness_factor[0]
    shift = affinity_offset[0]
    total = CLIPS
    block = ROWS_PER_DEVICE * N_COL
    count = total // block
    matching_text_indices = jnp.arange(total, dtype=jnp.int32)

    def step(acc, index):
        start = (index * block).astype(jnp.int32)
        vblock = lax.dynamic_slice_in_dim(v16, start, block, 0)
        lblock = lax.dynamic_slice_in_dim(matched_text_index, start, block, 0)
        logits = jnp.dot(vblock, c16.T, preferred_element_type=jnp.float32) * similarity_multiplier + shift
        match = lblock[:, None] == matching_text_indices[None, :]
        sign = jnp.where(match, 1.0, -1.0).astype(jnp.float32)
        losses = lax.optimization_barrier(jnp.sum(jax.nn.softplus(-sign * logits), axis=1))
        coef = (jax.nn.sigmoid(logits) - match.astype(jnp.float32)).astype(jnp.bfloat16)
        dv = similarity_multiplier * jnp.dot(coef, c16, preferred_element_type=jnp.float32)
        acc = acc + jnp.dot(coef.T, vblock, preferred_element_type=jnp.float32)
        return (acc, (losses, dv))
    init = jnp.zeros((total, film_embeds.shape[1]), jnp.float32)
    acc, (losses, dvs) = lax.scan(step, init, jnp.arange(count, dtype=jnp.int32))
    clip_loss = losses.reshape(total)
    dvhat = dvs.reshape(total, film_embeds.shape[1])
    dchat = similarity_multiplier * acc
    return (clip_loss, backward_norm(vhat, vnorm, dvhat), backward_norm(chat, cnorm, dchat))
```

```python
import jax
import jax.numpy as jnp
from jax import lax
from jax.experimental import pallas as pl
from jax.experimental.pallas import tpu as pltpu
from jax.sharding import PartitionSpec as P

F32, BF16 = jnp.float32, jnp.bfloat16
LANES = 128
VMEM_LIMIT = 56 * 1024 * 1024


def params():
    return pltpu.CompilerParams(vmem_limit_bytes=VMEM_LIMIT)


def in_vmem(count):
    return [pl.BlockSpec(memory_space=pltpu.VMEM)] * count


def unit_rows(rows):
    inverse = lax.rsqrt(jnp.sum(rows * rows, axis=1, keepdims=True) + 1e-06)
    return rows * inverse, inverse


def normalize_kernel(film_ref, text_ref, v_ref, c_ref):
    c_ref[...] = unit_rows(text_ref[...])[0].astype(BF16)
    v_ref[...] = unit_rows(film_ref[...])[0].astype(BF16)


def log1p_unit(e):
    series = e * (1.0 - e * (0.5 - e * (1.0 / 3.0 - e * 0.25)))
    return jnp.where(e < 0.01, series, jnp.log(1.0 + e))


def pair_kernel(clip_blocks, caption_blocks, own_blocks, scalars, bases, labels, *refs):
    v_refs = refs[:clip_blocks]
    c_refs = refs[clip_blocks : clip_blocks + caption_blocks]
    rest = refs[clip_blocks + caption_blocks :]
    dv_refs = rest[:clip_blocks]
    dc_refs = rest[clip_blocks : clip_blocks + own_blocks]
    away, loss_ref, v_all, c_all, coef = rest[clip_blocks + own_blocks :]
    rows, width = v_refs[0].shape
    clips = clip_blocks * rows
    captions = caption_blocks * rows
    for i, ref in enumerate(v_refs):
        v_all[pl.ds(i * rows, rows), :] = ref[...]
    for i, ref in enumerate(c_refs):
        c_all[pl.ds(i * rows, rows), :] = ref[...]
    scale, shift = scalars[0], scalars[1]
    loss_ref[...] = jnp.zeros_like(loss_ref)

    @pl.loop(0, caption_blocks // 2)
    def _(pair):
        start = pl.multiple_of(pair * 2 * rows, 2 * rows)
        dots = lax.dot_general(
            c_all[pl.ds(start, 2 * rows), :],
            v_all[...],
            (((1,), (1,)), ((), ())),
            preferred_element_type=F32,
        )
        for half in range(2):
            logits = dots[half * rows : (half + 1) * rows] * scale + shift
            ids = lax.broadcasted_iota(jnp.int32, (rows, clips), 0) + bases[pair * 2 + half]
            match = ids == labels[...]
            e = jnp.exp(-jnp.abs(logits))
            over = 1.0 / (1.0 + e)
            sigmoid = jnp.where(logits >= 0.0, over, e * over)
            signed = jnp.where(match, -logits, logits)
            losses = jnp.maximum(signed, 0.0) + log1p_unit(e)
            loss_ref[...] += jnp.sum(losses, axis=0, keepdims=True)
            coef[pl.ds(start + half * rows, rows), :] = (
                sigmoid - jnp.where(match, 1.0, 0.0)
            ).astype(BF16)

    chunk = 256

    for i in range(width // chunk):
        columns = pl.ds(i * chunk, chunk)
        part = lax.dot_general(
            coef[...], c_all[:, columns], (((0,), (0,)), ((), ())), preferred_element_type=F32
        )
        for b, ref in enumerate(dv_refs):
            ref[:, columns] = part[b * rows : (b + 1) * rows].astype(ref.dtype)
        part = jnp.dot(coef[...], v_all[:, columns], preferred_element_type=F32)
        for b, ref in enumerate(dc_refs):
            ref[:, columns] = part[b * rows : (b + 1) * rows].astype(ref.dtype)
        away[:, columns] = part[own_blocks * rows :].astype(away.dtype)


def finish_kernel(scalars, film, text, dv, dv_x, dv_z, dc, dc_y, dc_z, loss, loss_x, loss_z, out, gv, gc):
    scale = scalars[0]

    def back(rows, total):
        hat, inverse = unit_rows(rows)
        total = total * scale
        return inverse * (total - hat * jnp.sum(hat * total, axis=1, keepdims=True))

    gv[...] = back(film[...], dv[...] + dv_x[...].astype(F32) + dv_z[...].astype(F32))
    gc[...] = back(text[...], dc[...] + dc_y[...].astype(F32) + dc_z[...].astype(F32))
    out[...] = loss[...] + loss_x[...] + loss_z[...]


def shards(film, text, matched, sharpness, offset):
    rows, width = film.shape
    R, C = lax.axis_size("row"), lax.axis_size("col")
    r, c = lax.axis_index("row"), lax.axis_index("col")
    Y, Z = R // 2, C // 4

    def swap(value, axis, bits):
        size = lax.axis_size(axis)
        return lax.ppermute(value, axis, [(i, i ^ bits) for i in range(size)])

    v16, c16 = pl.pallas_call(
        normalize_kernel,
        out_shape=[jax.ShapeDtypeStruct((rows, width), BF16)] * 2,
        in_specs=in_vmem(2),
        out_specs=in_vmem(2),
        compiler_params=params(),
    )(film, text)

    v_z = swap(v16, "col", 2)
    c_hi = [c16] + [swap(c16, "col", 4 * s) for s in range(1, Z)]
    v_x = swap(v16, "row", 1)
    c_own = [[b] + [swap(b, "row", 2 * t) for t in range(1, Y)] for b in c_hi]
    v_d = swap(v_z, "row", 1)
    c_own = [b for group in c_own for b in group]
    c_other = [swap(b, "col", 1) for b in c_own]
    v_blocks = [v16, v_z, v_x, v_d]
    c_blocks = c_own + c_other
    own = len(c_own)

    clip_ids = [r * C + c, r * C + (c ^ 2), (r ^ 1) * C + c, (r ^ 1) * C + (c ^ 2)]
    labels = jnp.concatenate(
        [lax.dynamic_slice_in_dim(matched, b * rows, rows, 0) for b in clip_ids]
    ).reshape(1, 4 * rows)
    bases = jnp.stack(
        [
            (((c ^ (4 * s)) ^ k) * R + (r ^ (2 * t))) * rows
            for k in range(2)
            for s in range(Z)
            for t in range(Y)
        ]
    ).astype(jnp.int32)
    scalars = jnp.concatenate([sharpness, offset])

    block = lambda dtype, n=1: jax.ShapeDtypeStruct((n * rows, width), dtype)
    outs = pl.pallas_call(
        lambda *refs: pair_kernel(4, 2 * own, own, *refs),
        out_shape=[block(F32)] + [block(BF16)] * 3 + [block(F32)] * own
        + [block(BF16, own), jax.ShapeDtypeStruct((1, 4 * rows), F32)],
        in_specs=[pl.BlockSpec(memory_space=pltpu.SMEM)] * 2 + in_vmem(1 + 4 + 2 * own),
        out_specs=in_vmem(4 + own + 2),
        scratch_shapes=[
            pltpu.VMEM((4 * rows, width), BF16),
            pltpu.VMEM((2 * own * rows, width), BF16),
            pltpu.VMEM((2 * own * rows, 4 * rows), BF16),
        ],
        compiler_params=params(),
    )(scalars, bases, labels, *v_blocks, *c_blocks)
    dv, dv_blocks, dc, away, loss = outs[0], outs[:4], list(outs[4 : 4 + own]), outs[-2], outs[-1]
    loss = [loss[:, i * rows : (i + 1) * rows] for i in range(4)]

    back = swap(away, "col", 1)
    dv_near = swap(dv_blocks[2], "row", 1)
    dv_far = swap(dv_blocks[3], "row", 1)
    loss_near = swap(loss[2], "row", 1)
    loss_far = swap(loss[3], "row", 1)
    dv_z = swap((dv_blocks[1].astype(F32) + dv_far.astype(F32)).astype(BF16), "col", 2)
    loss_z = swap(loss[1] + loss_far, "col", 2)

    dc = [b + back[i * rows : (i + 1) * rows].astype(F32) for i, b in enumerate(dc)]
    grid = [dc[s * Y : (s + 1) * Y] for s in range(Z)]
    total, far = [], []
    for s in range(Z):
        arrived = [swap(grid[s][t].astype(BF16), "row", 2 * t).astype(F32) for t in range(1, Y)]
        total.append((grid[s][0], arrived))
    near = sum(total[0][1])
    for s in range(1, Z):
        here = total[s][0] + sum(total[s][1])
        far.append(swap(here.astype(BF16), "col", 4 * s).astype(F32))
    far = sum(far)

    out, gv, gc = pl.pallas_call(
        finish_kernel,
        out_shape=[jax.ShapeDtypeStruct((1, rows), F32), block(F32), block(F32)],
        in_specs=[pl.BlockSpec(memory_space=pltpu.SMEM)] + in_vmem(11),
        out_specs=in_vmem(3),
        compiler_params=params(),
    )(scalars, film, text, dv, dv_near, dv_z, grid[0][0], near, far, loss[0], loss_near, loss_z)
    return out.reshape(rows), gv, gc


def solution(mesh):
    return jax.shard_map(
        shards,
        mesh=mesh,
        in_specs=(P(("row", "col"), None), P(("col", "row"), None), P(), P(), P()),
        out_specs=(P(("row", "col")), P(("row", "col"), None), P(("col", "row"), None)),
        check_vma=False,
    )
```

```python
import jax
import jax.numpy as jnp
from jax import lax
from jax.experimental import pallas as pl
from jax.experimental.pallas import tpu as pltpu
from jax.sharding import PartitionSpec as P

F32, BF16 = jnp.float32, jnp.bfloat16
MIB = 1024 * 1024
SPECS = {
    "s": pl.BlockSpec(memory_space=pltpu.SMEM),
    "v": pl.BlockSpec(memory_space=pltpu.VMEM),
    "h": pl.BlockSpec(memory_space=pl.ANY),
}


def vm(shape, dtype=BF16):
    return pltpu.VMEM(shape, dtype)


def call(name, kernel, out_shape, specs, *args, limit=4, flops=0, scratch=(), aliases={}):
    space = {"v": pltpu.VMEM, "h": pltpu.HBM}
    args = [
        pltpu.with_memory_space_constraint(a, space[s]) if s in space else a
        for a, s in zip(args, specs)
    ]
    return pl.pallas_call(
        kernel,
        name=name,
        out_shape=out_shape,
        in_specs=[SPECS[s] for s in specs],
        out_specs=[SPECS["v"]] * len(out_shape),
        scratch_shapes=list(scratch),
        input_output_aliases=aliases,
        compiler_params=pltpu.CompilerParams(vmem_limit_bytes=limit * MIB),
        cost_estimate=pl.CostEstimate(flops=flops, bytes_accessed=0, transcendentals=0),
    )(*args)


def unit_rows(rows):
    inverse = lax.rsqrt(jnp.sum(rows * rows, axis=1, keepdims=True) + 1e-06)
    return rows * inverse, inverse


def dot_nt(a, b):
    return lax.dot_general(a, b, (((1,), (1,)), ((), ())), preferred_element_type=F32)


def dot_tn(a, b):
    return lax.dot_general(a, b, (((0,), (0,)), ((), ())), preferred_element_type=F32)


def dot_nn(a, b):
    return jnp.dot(a, b, preferred_element_type=F32)


def log1p_sum(e):
    rows = e.shape[0]
    u = e
    for _ in range(3):
        rows //= 2
        a, b = u[:rows], u[rows:]
        u = a + b + a * b
    series = u * (1.0 - u * (0.5 - u * (1.0 / 3.0 - u * 0.25)))
    logs = jnp.where(u < 0.01, series, jnp.log(1.0 + u))
    return jnp.sum(logs, axis=0, keepdims=True)


def pairs(dots, scale, shift, base, labels, counted):
    logits = dots * scale + shift
    match = lax.broadcasted_iota(jnp.int32, logits.shape, 0) == labels - base
    e = jnp.exp(-jnp.abs(logits))
    whole = 1.0 + e
    over = pl.reciprocal(whole, approx=True)
    over = over * (2.0 - whole * over)
    sigmoid = jnp.where(logits >= 0.0, over, e * over)
    coef = (sigmoid - jnp.where(match, 1.0, 0.0)).astype(BF16)
    if not counted:
        return coef, None
    e, logits, match = e[:, :counted], logits[:, :counted], match[:, :counted]
    linear = jnp.maximum(jnp.where(match, -logits, logits), 0.0)
    return coef, jnp.sum(linear, axis=0, keepdims=True) + log1p_sum(e)


def shards(film, text, matched, sharpness, offset):
    rows, width = film.shape
    R, C = lax.axis_size("row"), lax.axis_size("col")
    Y, Z = R // 2, C // 4
    CHUNK = 256
    mat = (rows, width)
    limit = 6 + 2 * (Y * Z * 2 * rows) // 1024

    def swap(value, axis, bits):
        size = lax.axis_size(axis)
        return lax.ppermute(value, axis, [(i, i ^ bits) for i in range(size)])

    def cap_base(s, t, k):
        r, c = lax.axis_index("row"), lax.axis_index("col")
        return ((c ^ (4 * s + k)) * R + (r ^ (2 * t))) * rows

    def clip_index(x, z, k):
        r, c = lax.axis_index("row"), lax.axis_index("col")
        return (r ^ x) * C + (c ^ (2 * z + k))

    near = [(0, t) for t in range(Y)]
    up = [(s, 0) for s in range(1, Z)]
    diag = [(s, t) for s in range(1, Z) for t in range(1, Y)]
    caps_a = [(*p, 0) for p in near + up]
    caps_b = [(*p, 1) for p in near]
    caps_c = [(*p, 1) for p in up + diag]
    caps_d = [(*p, 0) for p in diag]
    clip_order = [(0, 0, 0), (1, 0, 0), (0, 1, 0), (0, 0, 1), (1, 0, 1), (0, 1, 1), (1, 1, 1), (1, 1, 0)]
    na, nb, nc, nd = (len(g) * rows for g in (caps_a, caps_b, caps_c, caps_d))
    n1, n3, n5 = rows, 3 * rows, 5 * rows

    PARTS = 4

    def normalize_kernel(film, text, matched, v16, c16, vhat, chat, vinv, cinv, labels, fbuf, tbuf, sems):
        step = rows // PARTS
        copies = []
        for j, (src, buf) in enumerate(((text, tbuf), (film, fbuf))):
            for i in range(PARTS):
                part = pl.ds(i * step, step)
                copies.append(pltpu.make_async_copy(src.at[part], buf.at[part], sems.at[j * PARTS + i]))
        for copy in copies:
            copy.start()
        labels[...] = jnp.concatenate(
            [matched[pl.ds(clip_index(*p), 1), :] for p in clip_order], axis=1
        )
        for copy in copies[:PARTS]:
            copy.wait()
        hat, inverse = unit_rows(tbuf[...])
        chat[...], cinv[...], c16[...] = hat, inverse, hat.astype(BF16)
        for copy in copies[PARTS:]:
            copy.wait()
        hat, inverse = unit_rows(fbuf[...])
        vhat[...], vinv[...], v16[...] = hat, inverse, hat.astype(BF16)

    v16, c16, vhat, chat, vinv, cinv, labels = pl.pallas_call(
        normalize_kernel,
        name="normalize",
        out_shape=[vm(mat), vm(mat), vm(mat, F32), vm(mat, F32), vm((rows, 1), F32), vm((rows, 1), F32),
                   vm((1, 8 * rows), jnp.int32)],
        in_specs=[SPECS["h"], SPECS["h"], SPECS["v"]],
        out_specs=[SPECS["v"]] * 7,
        scratch_shapes=[pltpu.VMEM(mat, F32)] * 2
        + [pltpu.SemaphoreType.DMA((2 * PARTS,))],
        compiler_params=pltpu.CompilerParams(vmem_limit_bytes=8 * MIB),
    )(*[
        pltpu.with_memory_space_constraint(a, pltpu.HBM)
        for a in (film, text, matched.reshape(-1, rows))
    ])

    def hand_on_kernel(block, *refs):
        pass

    def hand_on(name, block, *after, flops=0):
        return call(
            name, hand_on_kernel, [vm(block.shape, block.dtype)], "v" * (1 + len(after)),
            block, *after, aliases={0: 0}, flops=flops,
        )[0]

    LONG = 10**10

    def consts_kernel(scale, shift, out):
        out[0:1, :] = jnp.full((1, 128), scale[0], F32)
        out[1:2, :] = jnp.full((1, 128), shift[0], F32)

    (consts,) = call("consts", consts_kernel, [vm((2, 128), F32)], "ss", sharpness, offset)

    def copies_kernel(v16, c16, v_out, c_out, both):
        v_out[...] = v16[...]
        c_out[...] = c16[...]
        both[:rows, :] = c16[...]
        both[rows:, :] = v16[...]

    c_z = [hand_on("captions_z", swap(c16, "col", 4 * s), consts, flops=LONG) for s in range(1, Z)]
    v_z = hand_on("clips_z", swap(v16, "col", 2), flops=LONG)
    v16b, c16b, both = call("copies", copies_kernel, [vm(mat), vm(mat), vm((2 * rows, width))], "vv", v16, c16)
    c_y = [swap(c16b, "row", 2 * t) for t in range(1, Y)]
    v_x = swap(v16b, "row", 1)
    both_k = swap(both, "col", 1)
    c_d = [swap(b, "row", 2 * t) for b in c_z for t in range(1, Y)]
    v_d = swap(v_z, "row", 1)
    cy_k = [swap(b, "col", 1) for b in c_y]
    vx_k = swap(v_x, "col", 1)
    cz_k = [swap(b, "col", 1) for b in c_z]
    vz_k = swap(v_z, "col", 1)

    def stack(target, blocks):
        for i, b in enumerate(blocks):
            target[pl.ds(i * rows, rows), :] = b[...]

    def strip(consts, caps, captions, clips, labels, counted, put):
        total = jnp.zeros((1, counted), F32) if counted else None
        scale, shift = consts[0:1, 0:1], consts[1:2, 0:1]
        dots = dot_nt(captions, clips)
        for i, p in enumerate(caps):
            block = dots[i * rows : (i + 1) * rows]
            coef, add = pairs(block, scale, shift, cap_base(*p), labels, counted)
            put(i, coef)
            if counted:
                total += add
        return total

    def put_in(target, first=0, cols=None):
        def put(i, coef):
            where = pl.ds(first + i * rows, rows)
            target[where, :] = coef if cols is None else coef[:, :cols]
        return put

    def early_kernel(consts, labels, both, both_k, *refs):
        n = Y - 1 + Z - 1
        c_yz, v_xz, refs = refs[:n], refs[n : n + 2], refs[n + 2 :]
        cy_k, vx_k, refs = refs[: Y - 1], refs[Y - 1], refs[Y:]
        CA, VA, P1, Q1, loss = refs
        stack(CA, [both.at[:rows], *c_yz, both_k.at[:rows], *cy_k])
        stack(VA, [both.at[rows:], *v_xz, both_k.at[rows:], vx_k])
        total = strip(consts, caps_a, CA[:na, :], VA[...], labels[:, :n5], n3, put_in(P1))
        total += strip(consts, caps_b, CA[na:, :], VA[:n3, :], labels[:, :n3], n3, put_in(Q1))
        loss[...] = total

    CA, VA, P1, Q1, loss1 = call(
        "early_pairs", early_kernel,
        [vm((na + nb, width)), vm((n5, width)), vm((na, n5)), vm((nb, n3)), vm((1, n3), F32)],
        "vv" + "v" * (2 + len(c_y) + len(c_z) + 2 + len(c_y) + 1),
        consts, labels, both, both_k, *c_y, *c_z, v_x, v_z, *cy_k, vx_k,
        flops=2 * 21 * rows * rows * width, limit=limit,
    )

    v_d = hand_on("clips_d", v_d, loss1)
    c_d = [hand_on("captions_d", b, loss1) for b in c_d]
    vd_k = swap(v_d, "col", 1)
    cd_k = [swap(b, "col", 1) for b in c_d]

    def far_captions_kernel(consts, labels, VA, loss1, *refs):
        n = len(caps_d)
        caps, clips, refs = refs[:n], refs[n : n + 3], refs[n + 3 :]
        VB, b, loss, dcs, (CD, b2) = refs[0], refs[1], refs[2], refs[3:-2], refs[-2:]
        stack(CD, caps)
        stack(VB, clips)
        loss[...] = loss1[...] + strip(
            consts, caps_d, CD[...], VA[...], labels[:, :n5], n3, put_in(b)
        )
        strip(consts, caps_d, CD[...], VB[...], labels[:, n5:], 0, put_in(b2))
        for i in range(width // CHUNK):
            cols = pl.ds(i * CHUNK, CHUNK)
            part = dot_nn(b[...], VA[:, cols]) + dot_nn(b2[...], VB[:, cols])
            for j, ref in enumerate(dcs):
                ref[:, cols] = part[j * rows : (j + 1) * rows].astype(BF16)

    VB, b, loss2, *dc_d = call(
        "far_captions", far_captions_kernel,
        [vm((3 * n1, width)), vm((nd, n5)), vm((1, n3), F32)] + [vm(mat)] * len(caps_d),
        "vv" + "v" * (2 + len(caps_d) + 3),
        consts, labels, VA, loss1, *c_d, vz_k, vd_k, v_d,
        flops=2 * 16 * rows * rows * width, limit=limit,
        scratch=[pltpu.VMEM((nd, width), BF16), pltpu.VMEM((nd, 3 * n1), BF16)],
    )

    def far_clips_kernel(consts, labels, loss2, CA, vd, *refs):
        n = len(caps_c) + len(caps_d)
        caps, (CB, a, loss, dv) = refs[:n], refs[n:]
        stack(CB, caps)
        late = labels[:, 7 * n1 :]
        total = strip(consts, caps_a + caps_b, CA[...], vd[...], late, n1, put_in(a))
        total += strip(consts, caps_c + caps_d, CB[...], vd[...], late, n1, put_in(a, na + nb))
        loss[...] = total
        for i in range(width // CHUNK):
            cols = pl.ds(i * CHUNK, CHUNK)
            dv[:, cols] = (
                dot_tn(a[: na + nb, :], CA[:, cols]) + dot_tn(a[na + nb :, :], CB[:, cols])
            ).astype(BF16)

    CB, a, loss_d, dv_d = call(
        "far_clips", far_clips_kernel,
        [vm((nc + nd, width)), vm((na + nb + nc + nd, n1)), vm((1, n1), F32), vm(mat)],
        "vvv" + "v" * (2 + len(caps_c) + len(caps_d)),
        consts, labels, loss2, CA, v_d, *cz_k, *cd_k, *c_d,
        flops=2 * 16 * rows * rows * width, limit=limit,
    )

    def near(name, clip, first, count, dtype, *after):
        clips = slice(clip * rows, (clip + 1) * rows)
        caps = slice(first * rows, (first + count) * rows)

        def near_kernel(consts, labels, CA, VA, P1, Q1, CB, VB, a, b, loss2, *refs):
            loss, dv, *dcs, c, d = refs[len(after) :]
            loss[...] = loss2[:, clips] + strip(
                consts, caps_c, CB[:nc, :], VA[clips, :], labels[:, clips], n1, put_in(c)
            )
            strip(
                consts, caps_a[first : first + count], CA[caps, :], VB[: 2 * n1, :],
                labels[:, n5 : 7 * n1], 0, put_in(d),
            )
            for i in range(width // CHUNK):
                cols = pl.ds(i * CHUNK, CHUNK)
                part = (
                    dot_tn(P1[:, clips], CA[:na, cols])
                    + dot_tn(Q1[:, clips], CA[na:, cols])
                    + dot_tn(c[...], CB[:nc, cols])
                    + dot_tn(b[:, clips], CB[nc:, cols])
                )
                dv[:, cols] = part.astype(dv.dtype)
                part = (
                    dot_nn(P1[caps, :], VA[:, cols])
                    + dot_nn(d[...], VB[: 2 * n1, cols])
                    + dot_nn(a[caps, :], VB[2 * n1 :, cols])
                )
                for j, ref in enumerate(dcs):
                    ref[:, cols] = part[j * rows : (j + 1) * rows].astype(ref.dtype)

        return call(
            name, near_kernel,
            [vm((1, n1), F32)] + [vm(mat, dtype)] * (1 + count),
            "v" * (11 + len(after)),
            consts, labels, CA, VA, P1, Q1, CB, VB, a, b, loss2, *after,
            flops=2 * 20 * rows * rows * width, limit=limit,
            scratch=[pltpu.VMEM((nc, n1), BF16), pltpu.VMEM((count * rows, 2 * n1), BF16)],
        )

    far_c = [[swap(dc_d[s * (Y - 1) + t - 1], "row", 2 * t) for t in range(1, Y)] for s in range(Z - 1)]
    far_v = swap(dv_d, "row", 1)
    loss_z, dvz, *dcz = near("near_z", 2, Y, Z - 1, F32)

    def add_kernel(*refs):
        total = refs[0][...].astype(F32)
        for ref in refs[1:-1]:
            total += ref[...].astype(F32)
        refs[-1][...] = total.astype(BF16)

    def add(name, *terms):
        return call(name, add_kernel, [vm(mat)], "v" * len(terms), *terms)[0]

    sum_c = [add("add_captions", dcz[s], *far_c[s]) for s in range(Z - 1)]
    sum_v = add("add_clips", dvz, far_v)
    got_h = [
        hand_on("captions_back", swap(sum_c[s], "col", 4 * (s + 1)), flops=LONG) for s in range(Z - 1)
    ]
    got_z = hand_on("clips_back", swap(sum_v, "col", 2), flops=LONG)

    loss_x, dvx, *dcy = near("near_xy", 1, 1, Y - 1, BF16, sum_v, *sum_c)
    got_x = swap(dvx, "row", 1)
    got_y = [swap(dcy[t - 1], "row", 2 * t) for t in range(1, Y)]
    loss_0, dv0, dc0 = near("near_own", 0, 0, 1, F32, loss_x)

    def pack_kernel(x, d, out):
        out[0:1, :] = x[...]
        out[1:2, :] = d[...]

    (loss_x,) = call("pack_loss", pack_kernel, [vm((2, n1), F32)], "vv", loss_x, loss_d)

    def loss_kernel(loss_z, arrived, out):
        out[...] = loss_z[...] + arrived[1:2, :]

    far_loss = swap(loss_x, "row", 1)
    (sum_loss,) = call("add_loss", loss_kernel, [vm((1, n1), F32)], "vv", loss_z, far_loss)
    got_loss = swap(sum_loss, "col", 2)

    def finish(name, losses, *args):
        def finish_kernel(consts, hat_ref, inverse_ref, *refs):
            adds, (grad, *loss, buf, sem) = refs[: -3 - bool(losses)], refs[-3 - bool(losses) :]
            total = adds[losses][...]
            for ref in adds[losses + 1 :]:
                total += ref[...].astype(F32)
            total = total * consts[0:1, 0:1]
            hat = hat_ref[...]
            along = jnp.sum(hat * total, axis=1, keepdims=True)
            buf[...] = inverse_ref[...] * (total - hat * along)
            copy = pltpu.make_async_copy(buf, grad, sem)
            copy.start()
            if losses:
                loss_0, far_loss, got_loss = adds[:losses]
                loss[0][...] = loss_0[...] + far_loss[0:1, :] + got_loss[...]
            copy.wait()

        shapes = [jax.ShapeDtypeStruct(mat, F32)] + [jax.ShapeDtypeStruct((1, rows), F32)] * bool(losses)
        return pl.pallas_call(
            finish_kernel,
            name=name,
            out_shape=shapes,
            in_specs=[SPECS["v"]] * len(args),
            out_specs=[SPECS["h"]] + [SPECS["v"]] * bool(losses),
            scratch_shapes=[pltpu.VMEM(mat, F32), pltpu.SemaphoreType.DMA],
            compiler_params=pltpu.CompilerParams(vmem_limit_bytes=4 * MIB),
        )(*[pltpu.with_memory_space_constraint(x, pltpu.VMEM) for x in args])

    gv, clip_loss = finish(
        "finish_clips", 3, consts, vhat, vinv, loss_0, far_loss, got_loss, dv0, got_x, got_z
    )
    (gc,) = finish("finish_captions", 0, consts, chat, cinv, dc0, *got_y, *got_h)
    return clip_loss.reshape(rows), gv, gc


def solution(mesh):
    return jax.shard_map(
        shards,
        mesh=mesh,
        in_specs=(P(("row", "col"), None), P(("col", "row"), None), P(), P(), P()),
        out_specs=(P(("row", "col")), P(("row", "col"), None), P(("col", "row"), None)),
        check_vma=False,
    )
```

```python
import jax
import jax.numpy as jnp
from jax import lax
from jax.experimental import pallas as pl
from jax.experimental.pallas import tpu as pltpu
from jax.sharding import PartitionSpec as P

F32, BF16 = jnp.float32, jnp.bfloat16
MIB = 1024 * 1024
CHUNK = 256
PARTS = 4
LONG = 10**10
SPECS = {
    "s": pl.BlockSpec(memory_space=pltpu.SMEM),
    "v": pl.BlockSpec(memory_space=pltpu.VMEM),
    "h": pl.BlockSpec(memory_space=pl.ANY),
}


def vm(shape, dtype=BF16):
    return pltpu.VMEM(shape, dtype)


def call(name, kernel, out_shape, args, spec="v", out_spec="v", limit=4, flops=0, scratch=(), aliases={}):
    space = {"v": pltpu.VMEM, "h": pltpu.HBM}
    if spec in space:
        args = [pltpu.with_memory_space_constraint(a, space[spec]) for a in args]
    return pl.pallas_call(
        kernel,
        name=name,
        out_shape=out_shape,
        in_specs=[SPECS[spec]] * len(args),
        out_specs=[SPECS[out_spec]] * len(out_shape),
        scratch_shapes=list(scratch),
        input_output_aliases=aliases,
        compiler_params=pltpu.CompilerParams(vmem_limit_bytes=limit * MIB),
        cost_estimate=pl.CostEstimate(flops=flops, bytes_accessed=0, transcendentals=0),
    )(*args)


def hand_on(name, block, *after, flops=0):
    return call(
        name, lambda *refs: None, [vm(block.shape, block.dtype)], [block, *after],
        aliases={0: 0}, flops=flops,
    )[0]


def unit_rows(rows):
    inverse = lax.rsqrt(jnp.sum(rows * rows, axis=1, keepdims=True) + 1e-06)
    return rows * inverse, inverse


def dot_nt(a, b):
    return lax.dot_general(a, b, (((1,), (1,)), ((), ())), preferred_element_type=F32)


def dot_tn(a, b):
    return lax.dot_general(a, b, (((0,), (0,)), ((), ())), preferred_element_type=F32)


def dot_nn(a, b):
    return jnp.dot(a, b, preferred_element_type=F32)


def log1p_sum(e):
    rows = e.shape[0]
    u = e
    for _ in range(3):
        rows //= 2
        a, b = u[:rows], u[rows:]
        u = a + b + a * b
    series = u * (1.0 - u * (0.5 - u * (1.0 / 3.0 - u * 0.25)))
    logs = jnp.where(u < 0.01, series, jnp.log(1.0 + u))
    return jnp.sum(logs, axis=0, keepdims=True)


def pairs(dots, scale, shift, base, labels, counted):
    logits = dots * scale + shift
    match = lax.broadcasted_iota(jnp.int32, logits.shape, 0) == labels - base
    e = jnp.exp(-jnp.abs(logits))
    whole = 1.0 + e
    over = pl.reciprocal(whole, approx=True)
    over = over * (2.0 - whole * over)
    sigmoid = jnp.where(logits >= 0.0, over, e * over)
    coef = (sigmoid - jnp.where(match, 1.0, 0.0)).astype(BF16)
    if not counted:
        return coef, None
    e, logits, match = e[:, :counted], logits[:, :counted], match[:, :counted]
    linear = jnp.maximum(jnp.where(match, -logits, logits), 0.0)
    return coef, jnp.sum(linear, axis=0, keepdims=True) + log1p_sum(e)


def stack(target, blocks):
    at = 0
    for b in blocks:
        target[pl.ds(at, b.shape[0]), :] = b[...]
        at += b.shape[0]


def shards(film, text, matched, sharpness, offset):
    rows, width = film.shape
    half = rows // 2
    R, C = lax.axis_size("row"), lax.axis_size("col")
    Y, Z = R // 2, C // 4
    mat, hmat = (rows, width), (half, width)
    limit = 6 + 2 * (Y * Z * 2 * rows) // 1024

    def swap(value, axis, bits):
        size = lax.axis_size(axis)
        return lax.ppermute(value, axis, [(i, i ^ bits) for i in range(size)])

    def first_caption(s, t, k):
        r, c = lax.axis_index("row"), lax.axis_index("col")
        return ((c ^ (4 * s + k)) * R + (r ^ (2 * t))) * rows

    def clip_index(x, z, k):
        r, c = lax.axis_index("row"), lax.axis_index("col")
        return (r ^ x) * C + (c ^ (2 * z + k))

    near = [(0, t) for t in range(Y)]
    up = [(s, 0) for s in range(1, Z)]
    diag = [(s, t) for s in range(1, Z) for t in range(1, Y)]
    clip_order = [(x, z, k) for k in range(2) for z in range(2) for x in range(2)]
    nn, nh = len(near) * rows, (len(up) + len(diag)) * half
    n1, n3, n4 = rows, 3 * rows, 4 * rows

    def near_pieces(k):
        return [(*p, k, 0, rows) for p in near]

    def half_pieces(k, h):
        return [(*p, k, h * half, half) for p in up + diag]

    def strip(consts, pieces, captions, clips, labels, counted, put):
        scale, shift = consts[0:1, 0:1], consts[1:2, 0:1]
        dots = dot_nt(captions, clips)
        at, total = 0, 0.0
        for s, t, k, first, size in pieces:
            base = first_caption(s, t, k) + first
            coef, add = pairs(dots[at : at + size], scale, shift, base, labels, counted)
            put(at, coef)
            total = total + add if counted else None
            at += size
        return total

    def put_in(target, first=0):
        def put(at, coef):
            target[pl.ds(first + at, coef.shape[0]), :] = coef
        return put

    def normalize_kernel(film, text, matched, v16, c16, ca, vhat, chat, vinv, cinv, labels, fbuf, tbuf, mbuf, sems):
        step = rows // PARTS
        get_matched = pltpu.make_async_copy(matched, mbuf, sems.at[2 * PARTS])
        copies = []
        for j, (src, buf) in enumerate(((film, fbuf), (text, tbuf))):
            for i in range(PARTS):
                part = pl.ds(i * step, step)
                copies.append(pltpu.make_async_copy(src.at[part], buf.at[part], sems.at[j * PARTS + i]))
        for copy in copies:
            copy.start()
        get_matched.start()
        for copy in copies[:PARTS]:
            copy.wait()
        hat, inverse = unit_rows(fbuf[...])
        vhat[...], vinv[...], v16[...] = hat, inverse, hat.astype(BF16)
        for copy in copies[PARTS:]:
            copy.wait()
        hat, inverse = unit_rows(tbuf[...])
        chat[...], cinv[...], c16[...] = hat, inverse, hat.astype(BF16)
        ca[...] = hat[:half].astype(BF16)
        get_matched.wait()
        labels[...] = jnp.concatenate(
            [mbuf[pl.ds(clip_index(*p), 1), :] for p in clip_order], axis=1
        )

    matched = matched.reshape(-1, rows)
    v16, c16, ca, vhat, chat, vinv, cinv, labels = call(
        "normalize", normalize_kernel,
        [vm(mat), vm(mat), vm(hmat), vm(mat, F32), vm(mat, F32), vm((rows, 1), F32), vm((rows, 1), F32),
         vm((1, 8 * rows), jnp.int32)],
        [film, text, matched], spec="h", limit=8,
        scratch=[pltpu.VMEM(mat, F32)] * 2
        + [pltpu.VMEM(matched.shape, jnp.int32), pltpu.SemaphoreType.DMA((2 * PARTS + 1,))],
    )

    def consts_kernel(scale, shift, out):
        out[0:1, :] = jnp.full((1, 128), scale[0], F32)
        out[1:2, :] = jnp.full((1, 128), shift[0], F32)

    (consts,) = call("consts", consts_kernel, [vm((2, 128), F32)], [sharpness, offset], spec="s")

    def copies_kernel(v16, c16, v_out, c_out, cb, both):
        v_out[...] = v16[...]
        c_out[...] = c16[...]
        cb[...] = c16[half:, :]
        both[:rows, :] = c16[...]
        both[rows:, :] = v16[...]

    v_z = hand_on("clips_z", swap(v16, "col", 2), flops=LONG)
    c_za = [hand_on("captions_za", swap(ca, "col", 4 * s), flops=LONG) for s in range(1, Z)]
    v16b, c16b, cb, both = call(
        "copies", copies_kernel, [vm(mat), vm(mat), vm(hmat), vm((2 * rows, width))], [v16, c16]
    )
    c_y = [swap(c16b, "row", 2 * t) for t in range(1, Y)]
    v_x = swap(v16b, "row", 1)
    c_za = [hand_on("captions_zy", b, consts, *c_y) for b in c_za]
    v_z = hand_on("clips_zx", v_z, v_x)
    c_zb = [swap(cb, "col", 4 * s) for s in range(1, Z)]
    both_k = swap(both, "col", 1)
    v_d = swap(v_z, "row", 1)
    c_da = [hand_on("captions_da", swap(b, "row", 2 * t), flops=LONG) for b in c_za for t in range(1, Y)]
    c_db = [swap(b, "row", 2 * t) for b in c_zb for t in range(1, Y)]
    cy_k = [swap(b, "col", 1) for b in c_y]
    vx_k = swap(v_x, "col", 1)
    vz_k = swap(v_z, "col", 1)
    vd_k = swap(v_d, "col", 1)
    c_h = [c_za + c_da]
    ch_k = [[swap(b, "col", 1) for b in c_h[0]]]

    def stack_kernel(both, both_k, vx, vz, vd, vxk, vzk, vdk, VV):
        stack(VV, [both.at[rows:], vx, vz, vd, both_k.at[rows:], vxk, vzk, vdk])

    (VV,) = call("clips", stack_kernel, [vm((8 * n1, width))], [both, both_k, v_x, v_z, v_d, vx_k, vz_k, vd_k])

    def half_sums(h):
        def half_kernel(consts, labels, VV, *refs):
            n = len(c_h[h])
            caps, (loss, p, *sums, H, coef) = refs[:n], refs[n:]
            stack(H, caps)
            loss[...] = strip(consts, half_pieces(0, h), H[...], VV[...], labels[...], n4, put_in(coef))
            p[...] = coef[:, :n4]
            for i in range(width // CHUNK):
                cols = pl.ds(i * CHUNK, CHUNK)
                part = dot_nn(coef[...], VV[:, cols])
                for j, ref in enumerate(sums):
                    ref[:, cols] = part[j * half : (j + 1) * half].astype(ref.dtype)

        loss, p, *sums = call(
            "half_" + "ab"[h], half_kernel,
            [vm((1, n4), F32), vm((nh, n4))] + [vm(hmat, F32)] * len(up) + [vm(hmat)] * len(diag),
            [consts, labels, VV, *c_h[h]],
            flops=2 * 16 * rows * rows * width, limit=limit,
            scratch=[pltpu.VMEM((nh, width), BF16), pltpu.VMEM((nh, 8 * n1), BF16)],
        )
        return loss, p, sums[: len(up)], sums[len(up) :]

    loss_a, p_a, dcz_a, dcd_a = half_sums(0)

    def diagonal_kernel(consts, labels, both, both_k, vd, *refs):
        n = len(near) - 1
        m = len(c_h[0])
        cy, cyk, c_a, c_ak = refs[:n], refs[n : 2 * n], refs[2 * n : 2 * n + m], refs[2 * n + m : 2 * n + 2 * m]
        S1, g, loss = refs[2 * n + 2 * m :]
        stack(S1, [both.at[:rows], *cy, *c_a, both_k.at[:rows], *cyk, *c_ak])
        m = nn + nh
        late = labels[:, n3:n4]
        strip(consts, near_pieces(0) + half_pieces(0, 0), S1[:m, :], vd[...], late, 0, put_in(g))
        loss[...] = strip(
            consts, near_pieces(1) + half_pieces(1, 0), S1[m:, :], vd[...], late, n1, put_in(g, m)
        )

    S1, g1, loss_d1 = call(
        "diagonal_clips", diagonal_kernel,
        [vm((2 * (nn + nh), width)), vm((2 * (nn + nh), n1)), vm((1, n1), F32)],
        [consts, labels, both, both_k, v_d, *c_y, *cy_k, *c_h[0], *ch_k[0]],
        flops=2 * 6 * rows * rows * width, limit=limit,
    )

    c_h.append([hand_on("captions_b", b, loss_a, flops=LONG // 3) for b in c_zb + c_db])
    ch_k.append([swap(b, "col", 1) for b in c_h[1]])
    loss_b, p_b, dcz_b, dcd_b = half_sums(1)

    def far_clips_kernel(consts, labels, vd, S1, g1, p_b, *refs):
        m = len(c_h[1])
        caps, (S2, loss, dv, g2) = refs[: 2 * m], refs[2 * m :]
        stack(S2, caps)
        g2[:nh, :] = p_b[:, n3:]
        loss[...] = strip(
            consts, half_pieces(1, 1), S2[nh:, :], vd[...], labels[:, n3:n4], n1, put_in(g2, nh)
        )
        for i in range(width // CHUNK):
            cols = pl.ds(i * CHUNK, CHUNK)
            dv[:, cols] = (dot_tn(g1[...], S1[:, cols]) + dot_tn(g2[...], S2[:, cols])).astype(BF16)

    S2, loss_d2, dv_d = call(
        "far_clips", far_clips_kernel,
        [vm((2 * nh, width)), vm((1, n1), F32), vm(mat)],
        [consts, labels, v_d, S1, g1, p_b, *c_h[1], *ch_k[1]],
        flops=2 * 9 * rows * rows * width, limit=limit,
        scratch=[pltpu.VMEM((2 * nh, n1), BF16)],
    )

    far_v = swap(dv_d, "row", 1)

    def add_kernel(*refs):
        total = refs[0][...].astype(F32)
        for ref in refs[1:-1]:
            total += ref[...].astype(F32)
        refs[-1][...] = total.astype(BF16)

    def add(name, *terms):
        return call(name, add_kernel, [vm(terms[0].shape)], terms)[0]

    def captions_back(h, dcz, dcd):
        far = [
            [
                hand_on("far_" + "ab"[h], swap(dcd[s * (Y - 1) + t - 1], "row", 2 * t), dv_d, flops=LONG)
                for t in range(1, Y)
            ]
            for s in range(Z - 1)
        ]
        sums = [add("add_" + "ab"[h], dcz[s], *far[s]) for s in range(Z - 1)]
        return sums, [swap(sums[s], "col", 4 * (s + 1)) for s in range(Z - 1)]

    sums_a, got_a = captions_back(0, dcz_a, dcd_a)
    sums_b, got_b = captions_back(1, dcz_b, dcd_b)

    def near_captions_kernel(consts, labels, VV, S1, dv_d, *refs):
        loss, p, *sums, coef = refs[Z - 1 :]
        loss[...] = strip(consts, near_pieces(0), S1[:nn, :], VV[...], labels[...], n4, put_in(coef))
        p[...] = coef[:, :n3]
        for i in range(width // CHUNK):
            cols = pl.ds(i * CHUNK, CHUNK)
            part = dot_nn(coef[...], VV[:, cols])
            for j, ref in enumerate(sums):
                ref[:, cols] = part[j * rows : (j + 1) * rows].astype(ref.dtype)

    loss_n, p_n, dc0, *dcy = call(
        "near_captions", near_captions_kernel,
        [vm((1, n4), F32), vm((nn, n3)), vm(mat, F32)] + [vm(mat)] * (Y - 1),
        [consts, labels, VV, S1, dv_d, *sums_a],
        flops=2 * 32 * rows * rows * width, limit=limit,
        scratch=[pltpu.VMEM((nn, 8 * n1), BF16)],
    )

    def z_clips_kernel(consts, labels, VV, S1, S2, p_n, p_a, p_b, *refs):
        loss, G1, G2, dv = refs[Z - 1 :]
        m = nn + nh
        G1[:nn, :] = p_n[...]
        G1[nn:m, :] = p_a[:, :n3]
        G2[:nh, :] = p_b[:, :n3]
        own = VV[:n3, :]
        loss[...] = strip(
            consts, near_pieces(1) + half_pieces(1, 0), S1[m:, :], own, labels[:, :n3], n3, put_in(G1, m)
        ) + strip(consts, half_pieces(1, 1), S2[nh:, :], own, labels[:, :n3], n3, put_in(G2, nh))
        for i in range(width // CHUNK):
            cols = pl.ds(i * CHUNK, CHUNK)
            dv[:, cols] = dot_tn(G1[:, 2 * n1 :], S1[:, cols]) + dot_tn(G2[:, 2 * n1 :], S2[:, cols])

    loss_k, G1, G2, dvz = call(
        "z_clips", z_clips_kernel,
        [vm((1, n3), F32), vm((2 * (nn + nh), n3)), vm((2 * nh, n3)), vm(mat, F32)],
        [consts, labels, VV, S1, S2, p_n, p_a, p_b, *sums_b],
        flops=2 * 20 * rows * rows * width, limit=limit,
    )

    sum_v = add("add_clips", dvz, far_v)
    got_z = hand_on("clips_back", swap(sum_v, "col", 2), flops=LONG)
    got_h = [[hand_on("captions_back", b, sum_v, flops=LONG) for b in got] for got in (got_a, got_b)]
    got_y = [swap(dcy[t - 1], "row", 2 * t) for t in range(1, Y)]

    def losses_kernel(l_a, l_b, l_n, l_k, l_d1, l_d2, loss_0, loss_x, loss_z):
        total = l_a[...] + l_b[...] + l_n[...]
        own = total[:, :n3] + l_k[...]
        loss_0[...] = own[:, :n1]
        loss_x[0:1, :] = own[:, n1 : 2 * n1]
        loss_x[1:2, :] = total[:, n3:] + l_d1[...] + l_d2[...]
        loss_z[...] = own[:, 2 * n1 :]

    def add_loss_kernel(loss_z, arrived, out):
        out[...] = loss_z[...] + arrived[1:2, :]

    loss_0, loss_x, loss_z = call(
        "losses", losses_kernel, [vm((1, n1), F32), vm((2, n1), F32), vm((1, n1), F32)],
        [loss_a, loss_b, loss_n, loss_k, loss_d1, loss_d2],
    )
    far_loss = swap(loss_x, "row", 1)
    (sum_loss,) = call("add_loss", add_loss_kernel, [vm((1, n1), F32)], [loss_z, far_loss])
    got_loss = swap(sum_loss, "col", 2)

    def near_clips_kernel(S1, S2, G1, G2, sum_v, sum_loss, dv0, dvx):
        for i in range(width // CHUNK):
            cols = pl.ds(i * CHUNK, CHUNK)
            part = dot_tn(G1[:, : 2 * n1], S1[:, cols]) + dot_tn(G2[:, : 2 * n1], S2[:, cols])
            dv0[:, cols] = part[:n1]
            dvx[:, cols] = part[n1:].astype(BF16)

    dv0, dvx = call(
        "near_clips", near_clips_kernel, [vm(mat, F32), vm(mat)],
        [S1, S2, G1, G2, sum_v, sum_loss],
        flops=2 * 16 * rows * rows * width, limit=limit,
    )
    got_x = swap(dvx, "row", 1)

    def finish(name, losses, consts, hat, inverse, own, whole, halves):
        tail = 2 + 2 * bool(losses)

        def finish_kernel(consts, hat_ref, inverse_ref, *refs):
            adds, (grad, *loss, buf, sems) = refs[: -1 - tail], refs[-1 - tail :]
            copies = []
            if losses:
                out, lbuf = loss
                loss_0, far_loss, got_loss = adds[:3]
                lbuf[...] = loss_0[...] + far_loss[0:1, :] + got_loss[...]
                copies.append(pltpu.make_async_copy(lbuf, out, sems.at[2]))
                copies[-1].start()
            adds = adds[len(losses) :]
            for i in range(2):
                part = pl.ds(i * half, half)
                total = adds[0][part, :]
                for ref in adds[1 : 1 + len(whole)]:
                    total += ref[part, :].astype(F32)
                for ref in adds[1 + len(whole) :][i * len(halves[0]) : (i + 1) * len(halves[0])]:
                    total += ref[...].astype(F32)
                total = total * consts[0:1, 0:1]
                hat = hat_ref[part, :]
                along = jnp.sum(hat * total, axis=1, keepdims=True)
                buf[part, :] = inverse_ref[part, :] * (total - hat * along)
                copies.append(pltpu.make_async_copy(buf.at[part], grad.at[part], sems.at[i]))
                copies[-1].start()
            for copy in copies:
                copy.wait()

        return call(
            name, finish_kernel,
            [jax.ShapeDtypeStruct(mat, F32)] + [jax.ShapeDtypeStruct((1, rows), F32)] * bool(losses),
            [consts, hat, inverse, *losses, own, *whole, *halves[0], *halves[1]], out_spec="h",
            scratch=[pltpu.VMEM((1, rows), F32)] * bool(losses)
            + [pltpu.VMEM(mat, F32), pltpu.SemaphoreType.DMA((3,))],
        )

    (gc,) = finish("finish_captions", [], consts, chat, cinv, dc0, got_y, got_h)
    gv, clip_loss = finish(
        "finish_clips", [loss_0, far_loss, got_loss], consts, vhat, vinv, dv0, [got_x, got_z], ([], [])
    )
    return clip_loss.reshape(rows), gv, gc


def solution(mesh):
    return jax.shard_map(
        shards,
        mesh=mesh,
        in_specs=(P(("row", "col"), None), P(("col", "row"), None), P(), P(), P()),
        out_specs=(P(("row", "col")), P(("row", "col"), None), P(("col", "row"), None)),
        check_vma=False,
    )
```

```python
import jax
import jax.numpy as jnp
from jax import lax
from jax.experimental import pallas as pl
from jax.experimental.pallas import tpu as pltpu
from jax.sharding import PartitionSpec as P

F32, BF16 = jnp.float32, jnp.bfloat16
MIB = 1024 * 1024
CHUNK = 256
PARTS = 4
LONG = 10**10
SPECS = {
    "s": pl.BlockSpec(memory_space=pltpu.SMEM),
    "v": pl.BlockSpec(memory_space=pltpu.VMEM),
    "h": pl.BlockSpec(memory_space=pl.ANY),
}


def vm(shape, dtype=BF16):
    return pltpu.VMEM(shape, dtype)


def call(name, kernel, out_shape, args, spec="v", out_spec="v", limit=4, flops=0, scratch=(), aliases={}):
    space = {"v": pltpu.VMEM, "h": pltpu.HBM}
    if spec in space:
        args = [pltpu.with_memory_space_constraint(a, space[spec]) for a in args]
    return pl.pallas_call(
        kernel,
        name=name,
        out_shape=out_shape,
        in_specs=[SPECS[spec]] * len(args),
        out_specs=[SPECS[out_spec]] * len(out_shape),
        scratch_shapes=list(scratch),
        input_output_aliases=aliases,
        compiler_params=pltpu.CompilerParams(vmem_limit_bytes=limit * MIB),
        cost_estimate=pl.CostEstimate(flops=flops, bytes_accessed=0, transcendentals=0),
    )(*args)


def hand_on(name, block, *after, flops=0):
    return call(
        name, lambda *refs: None, [vm(block.shape, block.dtype)], [block, *after],
        aliases={0: 0}, flops=flops,
    )[0]


def unit_rows(rows):
    inverse = lax.rsqrt(jnp.sum(rows * rows, axis=1, keepdims=True) + 1e-06)
    return rows * inverse, inverse


def dot_nt(a, b):
    return lax.dot_general(a, b, (((1,), (1,)), ((), ())), preferred_element_type=F32)


def dot_tn(a, b):
    return lax.dot_general(a, b, (((0,), (0,)), ((), ())), preferred_element_type=F32)


def dot_nn(a, b):
    return jnp.dot(a, b, preferred_element_type=F32)


def log1p_sum(e):
    rows = e.shape[0]
    u = e
    for _ in range(3):
        rows //= 2
        a, b = u[:rows], u[rows:]
        u = a + b + a * b
    series = u * (1.0 - u * (0.5 - u * (1.0 / 3.0 - u * 0.25)))
    logs = jnp.where(u < 0.01, series, jnp.log(1.0 + u))
    return jnp.sum(logs, axis=0, keepdims=True)


def pairs(dots, scale, shift, base, labels, counted):
    logits = dots * scale + shift
    match = lax.broadcasted_iota(jnp.int32, logits.shape, 0) == labels - base
    e = jnp.exp(-jnp.abs(logits))
    whole = 1.0 + e
    over = pl.reciprocal(whole, approx=True)
    over = over * (2.0 - whole * over)
    sigmoid = jnp.where(logits >= 0.0, over, e * over)
    coef = (sigmoid - jnp.where(match, 1.0, 0.0)).astype(BF16)
    if not counted:
        return coef, None
    e, logits, match = e[:, :counted], logits[:, :counted], match[:, :counted]
    linear = jnp.maximum(jnp.where(match, -logits, logits), 0.0)
    return coef, jnp.sum(linear, axis=0, keepdims=True) + log1p_sum(e)


def stack(target, blocks):
    at = 0
    for b in blocks:
        target[pl.ds(at, b.shape[0]), :] = b[...]
        at += b.shape[0]


def shards(film, text, matched, sharpness, offset):
    rows, width = film.shape
    half = rows // 2
    R, C = lax.axis_size("row"), lax.axis_size("col")
    Y, Z = R // 2, C // 4
    mat, hmat = (rows, width), (half, width)
    limit = 6 + 2 * (Y * Z * 2 * rows) // 1024

    def swap(value, axis, bits):
        size = lax.axis_size(axis)
        return lax.ppermute(value, axis, [(i, i ^ bits) for i in range(size)])

    def first_caption(s, t, k):
        r, c = lax.axis_index("row"), lax.axis_index("col")
        return ((c ^ (4 * s + k)) * R + (r ^ (2 * t))) * rows

    def clip_index(x, z, k):
        r, c = lax.axis_index("row"), lax.axis_index("col")
        return (r ^ x) * C + (c ^ (2 * z + k))

    near = [(0, t) for t in range(Y)]
    up = [(s, 0) for s in range(1, Z)]
    diag = [(s, t) for s in range(1, Z) for t in range(1, Y)]
    clip_order = [(x, z, k) for k in range(2) for z in range(2) for x in range(2)]
    nn, nh = len(near) * rows, (len(up) + len(diag)) * half
    n1, n3, n4 = rows, 3 * rows, 4 * rows

    def near_pieces(k):
        return [(*p, k, 0, rows) for p in near]

    def half_pieces(k, h):
        return [(*p, k, h * half, half) for p in up + diag]

    def strip(consts, pieces, captions, clips, labels, counted, put):
        scale, shift = consts[0:1, 0:1], consts[1:2, 0:1]
        dots = dot_nt(captions, clips)
        at, total = 0, 0.0
        for s, t, k, first, size in pieces:
            base = first_caption(s, t, k) + first
            coef, add = pairs(dots[at : at + size], scale, shift, base, labels, counted)
            put(at, coef)
            total = total + add if counted else None
            at += size
        return total

    def put_in(target, first=0):
        def put(at, coef):
            target[pl.ds(first + at, coef.shape[0]), :] = coef
        return put

    def normalize_kernel(film, text, matched, v16, c16, va, vb, ca, cb, vhat, chat, vinv, cinv, labels, fbuf, tbuf, mbuf, sems):
        step = rows // PARTS
        get_matched = pltpu.make_async_copy(matched, mbuf, sems.at[2 * PARTS])
        copies = []
        for j, (src, buf) in enumerate(((film, fbuf), (text, tbuf))):
            for i in range(PARTS):
                part = pl.ds(i * step, step)
                copies.append(pltpu.make_async_copy(src.at[part], buf.at[part], sems.at[j * PARTS + i]))
        for copy in copies:
            copy.start()
        get_matched.start()
        for copy in copies[:PARTS]:
            copy.wait()
        hat, inverse = unit_rows(fbuf[...])
        vhat[...], vinv[...], v16[...] = hat, inverse, hat.astype(BF16)
        va[...] = hat[:half].astype(BF16)
        vb[...] = hat[half:].astype(BF16)
        for copy in copies[PARTS:]:
            copy.wait()
        hat, inverse = unit_rows(tbuf[...])
        chat[...], cinv[...], c16[...] = hat, inverse, hat.astype(BF16)
        ca[...] = hat[:half].astype(BF16)
        cb[...] = hat[half:].astype(BF16)
        get_matched.wait()
        labels[...] = jnp.concatenate(
            [mbuf[pl.ds(clip_index(*p), 1), :] for p in clip_order], axis=1
        )

    matched = matched.reshape(-1, rows)
    v16, c16, va, vb, ca, cb, vhat, chat, vinv, cinv, labels = call(
        "normalize", normalize_kernel,
        [vm(mat), vm(mat)] + [vm(hmat)] * 4 + [vm(mat, F32), vm(mat, F32), vm((rows, 1), F32), vm((rows, 1), F32),
         vm((1, 8 * rows), jnp.int32)],
        [film, text, matched], spec="h", limit=8,
        scratch=[pltpu.VMEM(mat, F32)] * 2
        + [pltpu.VMEM(matched.shape, jnp.int32), pltpu.SemaphoreType.DMA((2 * PARTS + 1,))],
    )

    def consts_kernel(scale, shift, out):
        out[0:1, :] = jnp.full((1, 128), scale[0], F32)
        out[1:2, :] = jnp.full((1, 128), shift[0], F32)

    (consts,) = call("consts", consts_kernel, [vm((2, 128), F32)], [sharpness, offset], spec="s")

    def join(name, *blocks):
        def join_kernel(*refs):
            stack(refs[-1], refs[:-1])

        return call(name, join_kernel, [vm((sum(b.shape[0] for b in blocks), width))], blocks)[0]

    v_z = [hand_on("clips_z", swap(b, "col", 2), flops=LONG) for b in (va, vb)]
    c_za = [hand_on("captions_za", swap(ca, "col", 4 * s), consts, flops=LONG) for s in range(1, Z)]
    cb = hand_on("captions_hb", cb, v_z[0])
    c_zb = [hand_on("captions_zb", swap(cb, "col", 4 * s), flops=LONG) for s in range(1, Z)]
    c_y = [swap(c16, "row", 2 * t) for t in range(1, Y)]
    v_x = swap(v16, "row", 1)
    v_d = [swap(b, "row", 1) for b in v_z]
    c_da = [hand_on("captions_da", swap(b, "row", 2 * t), flops=LONG) for b in c_za for t in range(1, Y)]
    c_db = [swap(b, "row", 2 * t) for b in c_zb for t in range(1, Y)]
    N = join("near_blocks", c16, *c_y, v16, v_x, *v_z)
    N_k = swap(N, "col", 1)
    v_d = join("diagonal_block", *v_d)
    vd_k = swap(v_d, "col", 1)
    H = [join("half_a_blocks", *c_za, *c_da)]
    H_k = [swap(H[0], "col", 1)]

    def clips_kernel(N, N_k, vd, vdk, VV):
        stack(VV, [N.at[nn:], vd, N_k.at[nn:], vdk])

    (VV,) = call("clips", clips_kernel, [vm((8 * n1, width))], [N, N_k, v_d, vd_k])

    def half_sums(h):
        def half_kernel(consts, labels, VV, H, loss, p, *refs):
            sums, coef = refs[:-1], refs[-1]
            loss[...] = strip(consts, half_pieces(0, h), H[...], VV[...], labels[...], n4, put_in(coef))
            p[...] = coef[:, :n4]
            for i in range(width // CHUNK):
                cols = pl.ds(i * CHUNK, CHUNK)
                part = dot_nn(coef[...], VV[:, cols])
                for j, ref in enumerate(sums):
                    ref[:, cols] = part[j * half : (j + 1) * half].astype(ref.dtype)

        loss, p, *sums = call(
            "half_" + "ab"[h], half_kernel,
            [vm((1, n4), F32), vm((nh, n4))] + [vm(hmat, F32)] * len(up) + [vm(hmat)] * len(diag),
            [consts, labels, VV, H[h]],
            flops=2 * 16 * rows * rows * width, limit=limit,
            scratch=[pltpu.VMEM((nh, 8 * n1), BF16)],
        )
        return loss, p, sums[: len(up)], sums[len(up) :]

    loss_a, p_a, dcz_a, dcd_a = half_sums(0)

    def diagonal_kernel(consts, labels, N, N_k, vd, H, H_k, after, S1, g, loss):
        stack(S1, [N.at[:nn], H, N_k.at[:nn], H_k])
        m = nn + nh
        late = labels[:, n3:n4]
        strip(consts, near_pieces(0) + half_pieces(0, 0), S1[:m, :], vd[...], late, 0, put_in(g))
        loss[...] = strip(
            consts, near_pieces(1) + half_pieces(1, 0), S1[m:, :], vd[...], late, n1, put_in(g, m)
        )

    S1, g1, loss_d1 = call(
        "diagonal_clips", diagonal_kernel,
        [vm((2 * (nn + nh), width)), vm((2 * (nn + nh), n1)), vm((1, n1), F32)],
        [consts, labels, N, N_k, v_d, H[0], H_k[0], loss_a],
        flops=2 * 6 * rows * rows * width, limit=limit,
    )

    c_db = [hand_on("captions_db", b, loss_d1, flops=LONG) for b in c_db]
    H.append(join("half_b_blocks", *c_zb, *c_db))
    H_k.append(swap(H[1], "col", 1))
    loss_b, p_b, dcz_b, dcd_b = half_sums(1)

    def far_clips_kernel(consts, labels, vd, S1, g1, p_b, H, H_k, S2, loss, dv, g2):
        stack(S2, [H, H_k])
        g2[:nh, :] = p_b[:, n3:]
        loss[...] = strip(
            consts, half_pieces(1, 1), S2[nh:, :], vd[...], labels[:, n3:n4], n1, put_in(g2, nh)
        )
        for i in range(width // CHUNK):
            cols = pl.ds(i * CHUNK, CHUNK)
            dv[:, cols] = (dot_tn(g1[...], S1[:, cols]) + dot_tn(g2[...], S2[:, cols])).astype(BF16)

    S2, loss_d2, dv_d = call(
        "far_clips", far_clips_kernel,
        [vm((2 * nh, width)), vm((1, n1), F32), vm(mat)],
        [consts, labels, v_d, S1, g1, p_b, H[1], H_k[1]],
        flops=2 * 9 * rows * rows * width, limit=limit,
        scratch=[pltpu.VMEM((2 * nh, n1), BF16)],
    )

    far_v = swap(dv_d, "row", 1)

    def add_kernel(*refs):
        total = refs[0][...].astype(F32)
        for ref in refs[1:-1]:
            total += ref[...].astype(F32)
        refs[-1][...] = total.astype(BF16)

    def add(name, *terms):
        return call(name, add_kernel, [vm(terms[0].shape)], terms)[0]

    def captions_back(h, dcz, dcd, after):
        far = [
            [
                hand_on("far_" + "ab"[h], swap(dcd[s * (Y - 1) + t - 1], "row", 2 * t), after, flops=LONG)
                for t in range(1, Y)
            ]
            for s in range(Z - 1)
        ]
        far = [[hand_on("far_" + "ab"[h], b, dv_d) for b in group] for group in far]
        sums = [add("add_" + "ab"[h], dcz[s], *far[s]) for s in range(Z - 1)]
        return sums, [swap(sums[s], "col", 4 * (s + 1)) for s in range(Z - 1)]

    sums_a, got_a = captions_back(0, dcz_a, dcd_a, loss_b)
    sums_b, got_b = captions_back(1, dcz_b, dcd_b, sums_a[0])

    def near_captions_kernel(consts, labels, VV, S1, dv_d, *refs):
        loss, p, *sums, coef = refs[2 * (Z - 1) :]
        loss[...] = strip(consts, near_pieces(0), S1[:nn, :], VV[...], labels[...], n4, put_in(coef))
        p[...] = coef[:, :n3]
        for i in range(width // CHUNK):
            cols = pl.ds(i * CHUNK, CHUNK)
            part = dot_nn(coef[...], VV[:, cols])
            for j, ref in enumerate(sums):
                ref[:, cols] = part[j * rows : (j + 1) * rows].astype(ref.dtype)

    loss_n, p_n, dc0, *dcy = call(
        "near_captions", near_captions_kernel,
        [vm((1, n4), F32), vm((nn, n3)), vm(mat, F32)] + [vm(mat)] * (Y - 1),
        [consts, labels, VV, S1, dv_d, *sums_a, *sums_b],
        flops=2 * 32 * rows * rows * width, limit=limit,
        scratch=[pltpu.VMEM((nn, 8 * n1), BF16)],
    )

    def z_clips_kernel(consts, labels, VV, S1, S2, p_n, p_a, p_b, *refs):
        loss, G1, G2, dv = refs
        m = nn + nh
        G1[:nn, :] = p_n[...]
        G1[nn:m, :] = p_a[:, :n3]
        G2[:nh, :] = p_b[:, :n3]
        own = VV[:n3, :]
        loss[...] = strip(
            consts, near_pieces(1) + half_pieces(1, 0), S1[m:, :], own, labels[:, :n3], n3, put_in(G1, m)
        ) + strip(consts, half_pieces(1, 1), S2[nh:, :], own, labels[:, :n3], n3, put_in(G2, nh))
        for i in range(width // CHUNK):
            cols = pl.ds(i * CHUNK, CHUNK)
            dv[:, cols] = dot_tn(G1[:, 2 * n1 :], S1[:, cols]) + dot_tn(G2[:, 2 * n1 :], S2[:, cols])

    loss_k, G1, G2, dvz = call(
        "z_clips", z_clips_kernel,
        [vm((1, n3), F32), vm((2 * (nn + nh), n3)), vm((2 * nh, n3)), vm(mat, F32)],
        [consts, labels, VV, S1, S2, p_n, p_a, p_b],
        flops=2 * 20 * rows * rows * width, limit=limit,
    )

    sum_v = add("add_clips", dvz, far_v)
    got_z = hand_on("clips_back", swap(sum_v, "col", 2), flops=3 * LONG)
    got_h = [[hand_on("captions_back", b, sum_v, flops=3 * LONG) for b in got] for got in (got_a, got_b)]
    got_y = [hand_on("captions_y", swap(dcy[t - 1], "row", 2 * t), sum_v, flops=LONG) for t in range(1, Y)]

    def losses_kernel(l_a, l_b, l_n, l_k, l_d1, l_d2, got, sum_v, loss_0, loss_x, loss_z):
        total = l_a[...] + l_b[...] + l_n[...]
        own = total[:, :n3] + l_k[...]
        loss_0[...] = own[:, :n1]
        loss_x[0:1, :] = own[:, n1 : 2 * n1]
        loss_x[1:2, :] = total[:, n3:] + l_d1[...] + l_d2[...]
        loss_z[...] = own[:, 2 * n1 :]

    def add_loss_kernel(loss_z, arrived, out):
        out[...] = loss_z[...] + arrived[1:2, :]

    loss_0, loss_x, loss_z = call(
        "losses", losses_kernel, [vm((1, n1), F32), vm((2, n1), F32), vm((1, n1), F32)],
        [loss_a, loss_b, loss_n, loss_k, loss_d1, loss_d2, got_a[0], sum_v],
    )
    far_loss = swap(loss_x, "row", 1)
    (sum_loss,) = call("add_loss", add_loss_kernel, [vm((1, n1), F32)], [loss_z, far_loss])
    got_loss = swap(sum_loss, "col", 2)

    def near_clips_kernel(S1, S2, G1, G2, dv0, dvx):
        for i in range(width // CHUNK):
            cols = pl.ds(i * CHUNK, CHUNK)
            part = dot_tn(G1[:, : 2 * n1], S1[:, cols]) + dot_tn(G2[:, : 2 * n1], S2[:, cols])
            dv0[:, cols] = part[:n1]
            dvx[:, cols] = part[n1:].astype(BF16)

    dv0, dvx = call(
        "near_clips", near_clips_kernel, [vm(mat, F32), vm(mat)],
        [S1, S2, G1, G2],
        flops=2 * 16 * rows * rows * width, limit=limit,
    )
    got_x = hand_on("clips_x", swap(dvx, "row", 1), sum_v, flops=LONG)

    def finish(name, losses, consts, hat, inverse, own, whole, halves, *after):
        tail = 2 + 2 * bool(losses)

        def finish_kernel(consts, hat_ref, inverse_ref, *refs):
            adds, (grad, *loss, buf, sems) = refs[: -1 - tail - len(after)], refs[-1 - tail :]
            copies = []
            if losses:
                out, lbuf = loss
                loss_0, far_loss, got_loss = adds[:3]
                lbuf[...] = loss_0[...] + far_loss[0:1, :] + got_loss[...]
                copies.append(pltpu.make_async_copy(lbuf, out, sems.at[2]))
                copies[-1].start()
            adds = adds[len(losses) :]
            for i in range(2):
                part = pl.ds(i * half, half)
                total = adds[0][part, :]
                for ref in adds[1 : 1 + len(whole)]:
                    total += ref[part, :].astype(F32)
                for ref in adds[1 + len(whole) :][i * len(halves[0]) : (i + 1) * len(halves[0])]:
                    total += ref[...].astype(F32)
                total = total * consts[0:1, 0:1]
                hat = hat_ref[part, :]
                along = jnp.sum(hat * total, axis=1, keepdims=True)
                buf[part, :] = inverse_ref[part, :] * (total - hat * along)
                copies.append(pltpu.make_async_copy(buf.at[part], grad.at[part], sems.at[i]))
                copies[-1].start()
            for copy in copies:
                copy.wait()

        return call(
            name, finish_kernel,
            [jax.ShapeDtypeStruct(mat, F32)] + [jax.ShapeDtypeStruct((1, rows), F32)] * bool(losses),
            [consts, hat, inverse, *losses, own, *whole, *halves[0], *halves[1], *after], out_spec="h",
            scratch=[pltpu.VMEM((1, rows), F32)] * bool(losses)
            + [pltpu.VMEM(mat, F32), pltpu.SemaphoreType.DMA((3,))],
        )

    (gc,) = finish("finish_captions", [], consts, chat, cinv, dc0, got_y, got_h, sum_loss)
    gv, clip_loss = finish(
        "finish_clips", [loss_0, far_loss, got_loss], consts, vhat, vinv, dv0, [got_x, got_z], ([], [])
    )
    return clip_loss.reshape(rows), gv, gc


def solution(mesh):
    return jax.shard_map(
        shards,
        mesh=mesh,
        in_specs=(P(("row", "col"), None), P(("col", "row"), None), P(), P(), P()),
        out_specs=(P(("row", "col")), P(("row", "col"), None), P(("col", "row"), None)),
        check_vma=False,
    )
```

```python
import jax
import jax.numpy as jnp
from jax import lax
from jax.experimental import pallas as pl
from jax.experimental.pallas import tpu as pltpu
from jax.sharding import PartitionSpec as P

F32, BF16 = jnp.float32, jnp.bfloat16
MIB = 1024 * 1024
CHUNK = 256
PARTS = 4
LONG = 10**10
SPECS = {
    "s": pl.BlockSpec(memory_space=pltpu.SMEM),
    "v": pl.BlockSpec(memory_space=pltpu.VMEM),
    "h": pl.BlockSpec(memory_space=pl.ANY),
}


def vm(shape, dtype=BF16):
    return pltpu.VMEM(shape, dtype)


def call(name, kernel, out_shape, args, spec="v", out_spec="v", limit=4, flops=0, scratch=(), aliases={}):
    space = {"v": pltpu.VMEM, "h": pltpu.HBM}
    if spec in space:
        args = [pltpu.with_memory_space_constraint(a, space[spec]) for a in args]
    return pl.pallas_call(
        kernel,
        name=name,
        out_shape=out_shape,
        in_specs=[SPECS[spec]] * len(args),
        out_specs=[SPECS[out_spec]] * len(out_shape),
        scratch_shapes=list(scratch),
        input_output_aliases=aliases,
        compiler_params=pltpu.CompilerParams(vmem_limit_bytes=limit * MIB),
        cost_estimate=pl.CostEstimate(flops=flops, bytes_accessed=0, transcendentals=0),
    )(*args)


def hand_on(name, block, *after, flops=0):
    return call(
        name, lambda *refs: None, [vm(block.shape, block.dtype)], [block, *after],
        aliases={0: 0}, flops=flops,
    )[0]


def unit_rows(rows):
    inverse = lax.rsqrt(jnp.sum(rows * rows, axis=1, keepdims=True) + 1e-06)
    return rows * inverse, inverse


def dot_nt(a, b):
    return lax.dot_general(a, b, (((1,), (1,)), ((), ())), preferred_element_type=F32)


def dot_tn(a, b):
    return lax.dot_general(a, b, (((0,), (0,)), ((), ())), preferred_element_type=F32)


def dot_nn(a, b):
    return jnp.dot(a, b, preferred_element_type=F32)


def log1p_sum(e):
    rows = e.shape[0]
    u = e
    for _ in range(3):
        rows //= 2
        a, b = u[:rows], u[rows:]
        u = a + b + a * b
    series = u * (1.0 - u * (0.5 - u * (1.0 / 3.0 - u * 0.25)))
    logs = jnp.where(u < 0.01, series, jnp.log(1.0 + u))
    return jnp.sum(logs, axis=0, keepdims=True)


def pairs(dots, scale, shift, base, labels, counted):
    logits = dots * scale + shift
    match = lax.broadcasted_iota(jnp.int32, logits.shape, 0) == labels - base
    e = jnp.exp(-jnp.abs(logits))
    whole = 1.0 + e
    over = pl.reciprocal(whole, approx=True)
    over = over * (2.0 - whole * over)
    sigmoid = jnp.where(logits >= 0.0, over, e * over)
    coef = (sigmoid - jnp.where(match, 1.0, 0.0)).astype(BF16)
    if not counted:
        return coef, None
    e, logits, match = e[:, :counted], logits[:, :counted], match[:, :counted]
    linear = jnp.maximum(jnp.where(match, -logits, logits), 0.0)
    return coef, jnp.sum(linear, axis=0, keepdims=True) + log1p_sum(e)


def stack(target, blocks):
    at = 0
    for b in blocks:
        target[pl.ds(at, b.shape[0]), :] = b[...]
        at += b.shape[0]


def shards(film, text, matched, sharpness, offset):
    rows, width = film.shape
    half = rows // 2
    R, C = lax.axis_size("row"), lax.axis_size("col")
    Y, Z = R // 2, C // 4
    mat, hmat = (rows, width), (half, width)
    limit = 6 + 2 * (Y * Z * 2 * rows) // 1024

    def swap(value, axis, bits):
        size = lax.axis_size(axis)
        return lax.ppermute(value, axis, [(i, i ^ bits) for i in range(size)])

    def first_caption(s, t, k):
        r, c = lax.axis_index("row"), lax.axis_index("col")
        return ((c ^ (4 * s + k)) * R + (r ^ (2 * t))) * rows

    def clip_index(x, z, k):
        r, c = lax.axis_index("row"), lax.axis_index("col")
        return (r ^ x) * C + (c ^ (2 * z + k))

    near = [(0, t) for t in range(Y)]
    up = [(s, 0) for s in range(1, Z)]
    diag = [(s, t) for s in range(1, Z) for t in range(1, Y)]
    clip_order = [(x, z, k) for k in range(2) for z in range(2) for x in range(2)]
    nn, na, nd = len(near) * rows, len(near + up) * rows, len(diag) * rows
    n1, n3, n4, n7 = rows, 3 * rows, 4 * rows, 7 * rows

    def strip(consts, blocks, k, captions, clips, labels, counted, put):
        scale, shift = consts[0:1, 0:1], consts[1:2, 0:1]
        dots = dot_nt(captions, clips)
        total = 0.0
        for i, (s, t) in enumerate(blocks):
            block = dots[i * rows : (i + 1) * rows]
            coef, add = pairs(block, scale, shift, first_caption(s, t, k), labels, counted)
            put(i * rows, coef)
            total = total + add if counted else None
        return total

    def put_in(target, first=0, left=0):
        def put(at, coef):
            target[pl.ds(first + at, coef.shape[0]), pl.ds(left, coef.shape[1])] = coef
        return put

    def normalize_kernel(film, text, matched, v16, c16, va, vb, vhat, chat, vinv, cinv, labels, fbuf, tbuf, mbuf, sems):
        step = rows // PARTS
        get_matched = pltpu.make_async_copy(matched, mbuf, sems.at[2 * PARTS])
        copies = []
        for j, (src, buf) in enumerate(((film, fbuf), (text, tbuf))):
            for i in range(PARTS):
                part = pl.ds(i * step, step)
                copies.append(pltpu.make_async_copy(src.at[part], buf.at[part], sems.at[j * PARTS + i]))
        for copy in copies:
            copy.start()
        get_matched.start()
        for copy in copies[:PARTS]:
            copy.wait()
        hat, inverse = unit_rows(fbuf[...])
        vhat[...], vinv[...], v16[...] = hat, inverse, hat.astype(BF16)
        va[...] = hat[:half].astype(BF16)
        vb[...] = hat[half:].astype(BF16)
        for copy in copies[PARTS:]:
            copy.wait()
        hat, inverse = unit_rows(tbuf[...])
        chat[...], cinv[...], c16[...] = hat, inverse, hat.astype(BF16)
        get_matched.wait()
        labels[...] = jnp.concatenate(
            [mbuf[pl.ds(clip_index(*p), 1), :] for p in clip_order], axis=1
        )

    matched = matched.reshape(-1, rows)
    v16, c16, va, vb, vhat, chat, vinv, cinv, labels = call(
        "normalize", normalize_kernel,
        [vm(mat), vm(mat)] + [vm(hmat)] * 2 + [vm(mat, F32), vm(mat, F32), vm((rows, 1), F32), vm((rows, 1), F32),
         vm((1, 8 * rows), jnp.int32)],
        [film, text, matched], spec="h", limit=8,
        scratch=[pltpu.VMEM(mat, F32)] * 2
        + [pltpu.VMEM(matched.shape, jnp.int32), pltpu.SemaphoreType.DMA((2 * PARTS + 1,))],
    )

    def consts_kernel(scale, shift, out):
        out[0:1, :] = jnp.full((1, 128), scale[0], F32)
        out[1:2, :] = jnp.full((1, 128), shift[0], F32)

    (consts,) = call("consts", consts_kernel, [vm((2, 128), F32)], [sharpness, offset], spec="s")

    def join(name, *blocks):
        def join_kernel(*refs):
            stack(refs[-1], refs[:-1])

        return call(name, join_kernel, [vm((sum(b.shape[0] for b in blocks), width))], blocks)[0]

    v_z = [hand_on("clips_z", swap(b, "col", 2), flops=LONG) for b in (va, vb)]
    c_z = [hand_on("captions_z", swap(c16, "col", 4 * s), consts, flops=1 * LONG) for s in range(1, Z)]
    c_y = [swap(c16, "row", 2 * t) for t in range(1, Y)]
    v_x = swap(v16, "row", 1)
    v_d = [hand_on("clips_d", swap(b, "row", 1), flops=2 * LONG // 4) for b in v_z]
    c_d = [swap(b, "row", 2 * t) for b in c_z for t in range(1, Y)]
    N = join("near_blocks", c16, *c_y, v16, v_x, *v_z)
    N_k = hand_on("near_other", swap(N, "col", 1), flops=4 * LONG // 4)
    cz_k = [swap(b, "col", 1) for b in c_z]
    v_d = join("diagonal_clips", *v_d)
    vd_k = swap(v_d, "col", 1)

    def early_kernel(consts, labels, N, N_k, *refs):
        n = len(up)
        cz, czk, (S1, p, q, loss) = refs[:n], refs[n : 2 * n], refs[2 * n :]
        stack(S1, [N.at[:nn], *cz, N_k.at[:nn], *czk])
        own = N[nn:, :]
        loss[...] = strip(
            consts, near + up, 0, S1[:na, :], own, labels[:, :n3], n3, put_in(p)
        ) + strip(consts, near + up, 1, S1[na:, :], own, labels[:, :n3], n3, put_in(q))
        strip(
            consts, near + up, 0, S1[:na, :], N_k[nn:, :], labels[:, n4:n7], 0, put_in(p, left=n3)
        )

    S1, p, q, loss_a = call(
        "early_pairs", early_kernel,
        [vm((2 * na, width)), vm((na, 2 * n3)), vm((na, n3)), vm((1, n3), F32)],
        [consts, labels, N, N_k, *c_z, *cz_k],
        flops=2 * 27 * rows * rows * width, limit=limit,
    )

    def middle_kernel(consts, labels, N, N_k, vd, vdk, S1, p, q, VV, G1, loss, dc0, *refs):
        dcy, dcz, coef = refs[: Y - 1], refs[Y - 1 : -1], refs[-1]
        stack(VV, [N.at[nn:], vd, N_k.at[nn:], vdk])
        coef[:, :n3] = p[:, :n3]
        coef[:, n4:n7] = p[:, n3:]
        G1[na:, :n3] = q[...]
        late = labels[:, n3:n4]
        loss[...] = strip(
            consts, near + up, 0, S1[:na, :], vd[...], late, n1, put_in(coef, left=n3)
        ) + strip(consts, near + up, 1, S1[na:, :], vd[...], late, n1, put_in(G1, na, n3))
        strip(consts, near + up, 0, S1[:na, :], vdk[...], labels[:, n7:], 0, put_in(coef, left=n7))
        G1[:na, :] = coef[:, :n4]
        for i in range(width // CHUNK):
            cols = pl.ds(i * CHUNK, CHUNK)
            part = dot_nn(coef[...], VV[:, cols])
            for j, ref in enumerate((dc0, *dcy)):
                ref[:, cols] = part[j * rows : (j + 1) * rows].astype(ref.dtype)
            for j, ref in enumerate(dcz):
                ref[:, cols] = part[nn + j * half : nn + (j + 1) * half]

    VV, G1, loss_m, dc0, *dcs = call(
        "middle_sums", middle_kernel,
        [vm((8 * n1, width)), vm((2 * na, n4)), vm((1, n1), F32), vm(mat, F32)]
        + [vm(mat)] * (Y - 1) + [vm(hmat, F32)] * (2 * (Z - 1)),
        [consts, labels, N, N_k, v_d, vd_k, S1, p, q],
        flops=2 * 33 * rows * rows * width, limit=limit,
        scratch=[pltpu.VMEM((na, 8 * n1), BF16)],
    )
    dcy, dcz = dcs[: Y - 1], dcs[Y - 1 :]
    c_d = [hand_on("captions_d", b, dc0, flops=3 * LONG) for b in c_d]
    D_k = [swap(b, "col", 1) for b in c_d]

    def far_captions_kernel(consts, labels, VV, *refs):
        n = len(diag)
        caps, (loss, p, *sums, D, coef) = refs[:n], refs[n:]
        stack(D, caps)
        loss[...] = strip(consts, diag, 0, D[...], VV[...], labels[...], n4, put_in(coef))
        p[...] = coef[:, :n4]
        for i in range(width // CHUNK):
            cols = pl.ds(i * CHUNK, CHUNK)
            part = dot_nn(coef[...], VV[:, cols])
            for j, ref in enumerate(sums):
                ref[:, cols] = part[j * half : (j + 1) * half].astype(BF16)

    loss_c, p_d, *dcd = call(
        "far_captions", far_captions_kernel,
        [vm((1, n4), F32), vm((nd, n4))] + [vm(hmat)] * (2 * len(diag)),
        [consts, labels, VV, *c_d],
        flops=2 * 16 * rows * rows * width, limit=limit,
        scratch=[pltpu.VMEM((nd, width), BF16), pltpu.VMEM((nd, 8 * n1), BF16)],
    )

    def far_clips_kernel(consts, labels, VV, S1, G1, p_d, *refs):
        n = len(diag)
        caps, (S2, G2, loss, dv) = refs[: 2 * n], refs[2 * n :]
        stack(S2, caps)
        G2[:nd, :] = p_d[...]
        loss[...] = strip(consts, diag, 1, S2[nd:, :], VV[:n4, :], labels[:, :n4], n4, put_in(G2, nd))
        for i in range(width // CHUNK):
            cols = pl.ds(i * CHUNK, CHUNK)
            dv[:, cols] = (dot_tn(G1[:, n3:], S1[:, cols]) + dot_tn(G2[:, n3:], S2[:, cols])).astype(BF16)

    S2, G2, loss_d, dv_d = call(
        "far_clips", far_clips_kernel,
        [vm((2 * nd, width)), vm((2 * nd, n4)), vm((1, n4), F32), vm(mat)],
        [consts, labels, VV, S1, G1, p_d, *c_d, *D_k],
        flops=2 * 12 * rows * rows * width, limit=limit,
    )
    far_v = swap(dv_d, "row", 1)

    def near_clips_kernel(S1, S2, G1, G2, dv0, dvx, dvz):
        for i in range(width // CHUNK):
            cols = pl.ds(i * CHUNK, CHUNK)
            part = dot_tn(G1[:, :n3], S1[:, cols]) + dot_tn(G2[:, :n3], S2[:, cols])
            for j, ref in enumerate((dv0, dvx, dvz)):
                ref[:, cols] = part[j * rows : (j + 1) * rows].astype(ref.dtype)

    dv0, dvx, dvz = call(
        "near_clips", near_clips_kernel, [vm(mat, F32), vm(mat), vm(mat, F32)], [S1, S2, G1, G2],
        flops=2 * 24 * rows * rows * width, limit=limit,
    )

    def add_kernel(*refs):
        total = refs[0][...].astype(F32)
        for ref in refs[1:-1]:
            total += ref[...].astype(F32)
        refs[-1][...] = total.astype(BF16)

    def add(name, *terms):
        return call(name, add_kernel, [vm(terms[0].shape)], terms)[0]

    def captions_back(h, *after):
        sums = []
        for s in range(Z - 1):
            far = [
                hand_on("far_" + "ab"[h], swap(dcd[2 * (s * (Y - 1) + t - 1) + h], "row", 2 * t), *after, flops=LONG)
                for t in range(1, Y)
            ]
            sums.append(add("add_" + "ab"[h], dcz[2 * s + h], *far))
        return sums, [swap(sums[s], "col", 4 * (s + 1)) for s in range(Z - 1)]

    sums_a, got_a = captions_back(0, dv_d)
    sums_b, got_b = captions_back(1, sums_a[0])
    sum_v = add("add_clips", dvz, far_v)
    got_z = hand_on("clips_back", swap(sum_v, "col", 2), flops=3 * LONG)
    got_h = [[hand_on("captions_back", b, sum_v, flops=3 * LONG) for b in got] for got in (got_a, got_b)]
    got_y = [hand_on("captions_y", swap(dcy[t - 1], "row", 2 * t), sum_v, flops=LONG) for t in range(1, Y)]
    got_x = hand_on("clips_x", swap(dvx, "row", 1), sum_v, flops=LONG)

    def losses_kernel(l_a, l_m, l_c, l_d, *refs):
        loss_0, loss_x, loss_z = refs[-3:]
        total = l_c[...] + l_d[...]
        own = total[:, :n3] + l_a[...]
        loss_0[...] = own[:, :n1]
        loss_x[0:1, :] = own[:, n1 : 2 * n1]
        loss_x[1:2, :] = total[:, n3:] + l_m[...]
        loss_z[...] = own[:, 2 * n1 :]

    def add_loss_kernel(loss_z, arrived, out):
        out[...] = loss_z[...] + arrived[1:2, :]

    loss_0, loss_x, loss_z = call(
        "losses", losses_kernel, [vm((1, n1), F32), vm((2, n1), F32), vm((1, n1), F32)],
        [loss_a, loss_m, loss_c, loss_d, got_a[0], sum_v],
    )
    far_loss = swap(loss_x, "row", 1)
    (sum_loss,) = call("add_loss", add_loss_kernel, [vm((1, n1), F32)], [loss_z, far_loss])
    got_loss = swap(sum_loss, "col", 2)

    def finish(name, losses, consts, hat, inverse, own, whole, halves, *after):
        tail = 2 + 2 * bool(losses)

        def finish_kernel(consts, hat_ref, inverse_ref, *refs):
            adds, (grad, *loss, buf, sems) = refs[: -1 - tail - len(after)], refs[-1 - tail :]
            copies = []
            if losses:
                out, lbuf = loss
                loss_0, far_loss, got_loss = adds[:3]
                lbuf[...] = loss_0[...] + far_loss[0:1, :] + got_loss[...]
                copies.append(pltpu.make_async_copy(lbuf, out, sems.at[2]))
                copies[-1].start()
            adds = adds[len(losses) :]
            for i in range(2):
                part = pl.ds(i * half, half)
                total = adds[0][part, :]
                for ref in adds[1 : 1 + len(whole)]:
                    total += ref[part, :].astype(F32)
                for ref in adds[1 + len(whole) :][i * len(halves[0]) : (i + 1) * len(halves[0])]:
                    total += ref[...].astype(F32)
                total = total * consts[0:1, 0:1]
                hat = hat_ref[part, :]
                along = jnp.sum(hat * total, axis=1, keepdims=True)
                buf[part, :] = inverse_ref[part, :] * (total - hat * along)
                copies.append(pltpu.make_async_copy(buf.at[part], grad.at[part], sems.at[i]))
                copies[-1].start()
            for copy in copies:
                copy.wait()

        return call(
            name, finish_kernel,
            [jax.ShapeDtypeStruct(mat, F32)] + [jax.ShapeDtypeStruct((1, rows), F32)] * bool(losses),
            [consts, hat, inverse, *losses, own, *whole, *halves[0], *halves[1], *after], out_spec="h",
            scratch=[pltpu.VMEM((1, rows), F32)] * bool(losses)
            + [pltpu.VMEM(mat, F32), pltpu.SemaphoreType.DMA((3,))],
        )

    (gc,) = finish("finish_captions", [], consts, chat, cinv, dc0, got_y, got_h, sum_loss)
    gv, clip_loss = finish(
        "finish_clips", [loss_0, far_loss, got_loss], consts, vhat, vinv, dv0, [got_x, got_z], ([], [])
    )
    return clip_loss.reshape(rows), gv, gc


def solution(mesh):
    return jax.shard_map(
        shards,
        mesh=mesh,
        in_specs=(P(("row", "col"), None), P(("col", "row"), None), P(), P(), P()),
        out_specs=(P(("row", "col")), P(("row", "col"), None), P(("col", "row"), None)),
        check_vma=False,
    )
```

```python
import jax
import jax.numpy as jnp
from jax import lax
from jax.experimental import pallas as pl
from jax.experimental.pallas import tpu as pltpu
from jax.sharding import PartitionSpec as P

F32, BF16 = jnp.float32, jnp.bfloat16
MIB = 1024 * 1024
CHUNK = 256
PARTS = 4
LONG = 10**10
SPECS = {
    "s": pl.BlockSpec(memory_space=pltpu.SMEM),
    "v": pl.BlockSpec(memory_space=pltpu.VMEM),
    "h": pl.BlockSpec(memory_space=pl.ANY),
}


def vm(shape, dtype=BF16):
    return pltpu.VMEM(shape, dtype)


def call(name, kernel, out_shape, args, spec="v", out_spec="v", limit=4, flops=0, scratch=(), aliases={}):
    space = {"v": pltpu.VMEM, "h": pltpu.HBM}
    if spec in space:
        args = [pltpu.with_memory_space_constraint(a, space[spec]) for a in args]
    return pl.pallas_call(
        kernel,
        name=name,
        out_shape=out_shape,
        in_specs=[SPECS[spec]] * len(args),
        out_specs=[SPECS[out_spec]] * len(out_shape),
        scratch_shapes=list(scratch),
        input_output_aliases=aliases,
        compiler_params=pltpu.CompilerParams(vmem_limit_bytes=limit * MIB),
        cost_estimate=pl.CostEstimate(flops=flops, bytes_accessed=0, transcendentals=0),
    )(*args)


def hand_on(name, block, *after, flops=0):
    return call(
        name, lambda *refs: None, [vm(block.shape, block.dtype)], [block, *after],
        aliases={0: 0}, flops=flops,
    )[0]


def unit_rows(rows):
    inverse = lax.rsqrt(jnp.sum(rows * rows, axis=1, keepdims=True) + 1e-06)
    return rows * inverse, inverse


def dot_nt(a, b):
    return lax.dot_general(a, b, (((1,), (1,)), ((), ())), preferred_element_type=F32)


def dot_tn(a, b):
    return lax.dot_general(a, b, (((0,), (0,)), ((), ())), preferred_element_type=F32)


def dot_nn(a, b):
    return jnp.dot(a, b, preferred_element_type=F32)


def log1p_sum(e):
    rows = e.shape[0]
    u = e
    for _ in range(3):
        rows //= 2
        a, b = u[:rows], u[rows:]
        u = a + b + a * b
    series = u * (1.0 - u * (0.5 - u * (1.0 / 3.0 - u * 0.25)))
    logs = jnp.where(u < 0.01, series, jnp.log(1.0 + u))
    return jnp.sum(logs, axis=0, keepdims=True)


def pairs(dots, scale, shift, base, labels, counted):
    logits = dots * scale + shift
    match = lax.broadcasted_iota(jnp.int32, logits.shape, 0) == labels - base
    e = jnp.exp(-jnp.abs(logits))
    whole = 1.0 + e
    over = pl.reciprocal(whole, approx=True)
    over = over * (2.0 - whole * over)
    sigmoid = jnp.where(logits >= 0.0, over, e * over)
    coef = (sigmoid - jnp.where(match, 1.0, 0.0)).astype(BF16)
    if not counted:
        return coef, None
    e, logits, match = e[:, :counted], logits[:, :counted], match[:, :counted]
    linear = jnp.maximum(jnp.where(match, -logits, logits), 0.0)
    return coef, jnp.sum(linear, axis=0, keepdims=True) + log1p_sum(e)


def stack(target, blocks):
    at = 0
    for b in blocks:
        target[pl.ds(at, b.shape[0]), :] = b[...]
        at += b.shape[0]


def shards(film, text, matched, sharpness, offset):
    rows, width = film.shape
    half = rows // 2
    R, C = lax.axis_size("row"), lax.axis_size("col")
    Y, Z = R // 2, C // 4
    mat, hmat = (rows, width), (half, width)
    limit = 6 + 2 * (Y * Z * 2 * rows) // 1024

    def swap(value, axis, bits):
        size = lax.axis_size(axis)
        return lax.ppermute(value, axis, [(i, i ^ bits) for i in range(size)])

    def first_caption(s, t, k):
        r, c = lax.axis_index("row"), lax.axis_index("col")
        return ((c ^ (4 * s + k)) * R + (r ^ (2 * t))) * rows

    def clip_index(x, z, k):
        r, c = lax.axis_index("row"), lax.axis_index("col")
        return (r ^ x) * C + (c ^ (2 * z + k))

    near = [(0, t) for t in range(Y)]
    up = [(s, 0) for s in range(1, Z)]
    diag = [(s, t) for s in range(1, Z) for t in range(1, Y)]
    clip_order = [(x, z, k) for k in range(2) for z in range(2) for x in range(2)]
    nn, na, nd = len(near) * rows, len(near + up) * rows, len(diag) * rows
    n1, n3, n4, n7 = rows, 3 * rows, 4 * rows, 7 * rows

    def strip(consts, blocks, k, captions, clips, labels, counted, put):
        scale, shift = consts[0:1, 0:1], consts[1:2, 0:1]
        dots = dot_nt(captions, clips)
        total = 0.0
        for i, (s, t) in enumerate(blocks):
            block = dots[i * rows : (i + 1) * rows]
            coef, add = pairs(block, scale, shift, first_caption(s, t, k), labels, counted)
            put(i * rows, coef)
            total = total + add if counted else None
        return total

    def put_in(target, first=0, left=0):
        def put(at, coef):
            target[pl.ds(first + at, coef.shape[0]), pl.ds(left, coef.shape[1])] = coef
        return put

    def normalize_kernel(film, text, matched, v16, c16, va, vb, vhat, chat, vinv, cinv, labels, fbuf, tbuf, mbuf, sems):
        step = rows // PARTS
        get_matched = pltpu.make_async_copy(matched, mbuf, sems.at[2 * PARTS])
        copies = []
        for j, (src, buf) in enumerate(((film, fbuf), (text, tbuf))):
            for i in range(PARTS):
                part = pl.ds(i * step, step)
                copies.append(pltpu.make_async_copy(src.at[part], buf.at[part], sems.at[j * PARTS + i]))
        for copy in copies:
            copy.start()
        get_matched.start()
        for copy in copies[:PARTS]:
            copy.wait()
        hat, inverse = unit_rows(fbuf[...])
        vhat[...], vinv[...], v16[...] = hat, inverse, hat.astype(BF16)
        va[...] = hat[:half].astype(BF16)
        vb[...] = hat[half:].astype(BF16)
        for copy in copies[PARTS:]:
            copy.wait()
        hat, inverse = unit_rows(tbuf[...])
        chat[...], cinv[...], c16[...] = hat, inverse, hat.astype(BF16)
        get_matched.wait()
        labels[...] = jnp.concatenate(
            [mbuf[pl.ds(clip_index(*p), 1), :] for p in clip_order], axis=1
        )

    matched = matched.reshape(-1, rows)
    v16, c16, va, vb, vhat, chat, vinv, cinv, labels = call(
        "normalize", normalize_kernel,
        [vm(mat), vm(mat)] + [vm(hmat)] * 2 + [vm(mat, F32), vm(mat, F32), vm((rows, 1), F32), vm((rows, 1), F32),
         vm((1, 8 * rows), jnp.int32)],
        [film, text, matched], spec="h", limit=8,
        scratch=[pltpu.VMEM(mat, F32)] * 2
        + [pltpu.VMEM(matched.shape, jnp.int32), pltpu.SemaphoreType.DMA((2 * PARTS + 1,))],
    )

    def consts_kernel(scale, shift, out):
        out[0:1, :] = jnp.full((1, 128), scale[0], F32)
        out[1:2, :] = jnp.full((1, 128), shift[0], F32)

    (consts,) = call("consts", consts_kernel, [vm((2, 128), F32)], [sharpness, offset], spec="s")

    def join(name, *blocks):
        def join_kernel(*refs):
            stack(refs[-1], refs[:-1])

        return call(name, join_kernel, [vm((sum(b.shape[0] for b in blocks), width))], blocks)[0]

    v_z = [hand_on("clips_z", swap(b, "col", 2), flops=n * LONG // 4) for b, n in ((va, 4), (vb, 24))]
    c_z = [hand_on("captions_z", swap(c16, "col", 4 * s), consts, flops=4 * LONG // 4) for s in range(1, Z)]
    c_y = [swap(c16, "row", 2 * t) for t in range(1, Y)]
    v_x = swap(v16, "row", 1)
    v_d = [hand_on("clips_d", swap(b, "row", 1), flops=2 * LONG // 4) for b in v_z]
    c_d = [swap(b, "row", 2 * t) for b in c_z for t in range(1, Y)]
    N = join("near_blocks", c16, *c_y, v16, v_x, *v_z)
    N_k = hand_on("near_other", swap(N, "col", 1), flops=4 * LONG // 4)
    cz_k = [swap(b, "col", 1) for b in c_z]
    v_d = join("diagonal_clips", *v_d)
    vd_k = swap(v_d, "col", 1)

    def early_kernel(consts, labels, N, N_k, *refs):
        n = len(up)
        cz, czk, (S1, p, q, loss) = refs[:n], refs[n : 2 * n], refs[2 * n :]
        stack(S1, [N.at[:nn], *cz, N_k.at[:nn], *czk])
        own = N[nn:, :]
        loss[...] = strip(
            consts, near + up, 0, S1[:na, :], own, labels[:, :n3], n3, put_in(p)
        ) + strip(consts, near + up, 1, S1[na:, :], own, labels[:, :n3], n3, put_in(q))
        strip(
            consts, near + up, 0, S1[:na, :], N_k[nn:, :], labels[:, n4:n7], 0, put_in(p, left=n3)
        )

    S1, p, q, loss_a = call(
        "early_pairs", early_kernel,
        [vm((2 * na, width)), vm((na, 2 * n3)), vm((na, n3)), vm((1, n3), F32)],
        [consts, labels, N, N_k, *c_z, *cz_k],
        flops=2 * 27 * rows * rows * width, limit=limit,
    )

    def middle_kernel(consts, labels, N, N_k, vd, vdk, S1, p, q, VV, G1, loss, dc0, *refs):
        dcy, dcz, coef = refs[: Y - 1], refs[Y - 1 : -1], refs[-1]
        stack(VV, [N.at[nn:], vd, N_k.at[nn:], vdk])
        coef[:, :n3] = p[:, :n3]
        coef[:, n4:n7] = p[:, n3:]
        G1[na:, :n3] = q[...]
        late = labels[:, n3:n4]
        loss[...] = strip(
            consts, near + up, 0, S1[:na, :], vd[...], late, n1, put_in(coef, left=n3)
        ) + strip(consts, near + up, 1, S1[na:, :], vd[...], late, n1, put_in(G1, na, n3))
        strip(consts, near + up, 0, S1[:na, :], vdk[...], labels[:, n7:], 0, put_in(coef, left=n7))
        G1[:na, :] = coef[:, :n4]
        for i in range(width // CHUNK):
            cols = pl.ds(i * CHUNK, CHUNK)
            part = dot_nn(coef[...], VV[:, cols])
            for j, ref in enumerate((dc0, *dcy)):
                ref[:, cols] = part[j * rows : (j + 1) * rows].astype(ref.dtype)
            for j, ref in enumerate(dcz):
                ref[:, cols] = part[nn + j * half : nn + (j + 1) * half]

    VV, G1, loss_m, dc0, *dcs = call(
        "middle_sums", middle_kernel,
        [vm((8 * n1, width)), vm((2 * na, n4)), vm((1, n1), F32), vm(mat, F32)]
        + [vm(mat)] * (Y - 1) + [vm(hmat, F32)] * (2 * (Z - 1)),
        [consts, labels, N, N_k, v_d, vd_k, S1, p, q],
        flops=2 * 33 * rows * rows * width, limit=limit,
        scratch=[pltpu.VMEM((na, 8 * n1), BF16)],
    )
    dcy, dcz = dcs[: Y - 1], dcs[Y - 1 :]
    c_d = [hand_on("captions_d", b, dc0, flops=3 * LONG) for b in c_d]
    D_k = [swap(b, "col", 1) for b in c_d]

    def far_captions_kernel(consts, labels, VV, *refs):
        n = len(diag)
        caps, (loss, p, *sums, D, coef) = refs[:n], refs[n:]
        stack(D, caps)
        loss[...] = strip(consts, diag, 0, D[...], VV[...], labels[...], n4, put_in(coef))
        p[...] = coef[:, :n4]
        for i in range(width // CHUNK):
            cols = pl.ds(i * CHUNK, CHUNK)
            part = dot_nn(coef[...], VV[:, cols])
            for j, ref in enumerate(sums):
                ref[:, cols] = part[j * half : (j + 1) * half].astype(BF16)

    loss_c, p_d, *dcd = call(
        "far_captions", far_captions_kernel,
        [vm((1, n4), F32), vm((nd, n4))] + [vm(hmat)] * (2 * len(diag)),
        [consts, labels, VV, *c_d],
        flops=2 * 16 * rows * rows * width, limit=limit,
        scratch=[pltpu.VMEM((nd, width), BF16), pltpu.VMEM((nd, 8 * n1), BF16)],
    )

    def far_clips_kernel(consts, labels, VV, S1, G1, p_d, *refs):
        n = len(diag)
        caps, (S2, G2, loss, dv) = refs[: 2 * n], refs[2 * n :]
        stack(S2, caps)
        G2[:nd, :] = p_d[...]
        loss[...] = strip(consts, diag, 1, S2[nd:, :], VV[:n4, :], labels[:, :n4], n4, put_in(G2, nd))
        for i in range(width // CHUNK):
            cols = pl.ds(i * CHUNK, CHUNK)
            dv[:, cols] = (dot_tn(G1[:, n3:], S1[:, cols]) + dot_tn(G2[:, n3:], S2[:, cols])).astype(BF16)

    S2, G2, loss_d, dv_d = call(
        "far_clips", far_clips_kernel,
        [vm((2 * nd, width)), vm((2 * nd, n4)), vm((1, n4), F32), vm(mat)],
        [consts, labels, VV, S1, G1, p_d, *c_d, *D_k],
        flops=2 * 12 * rows * rows * width, limit=limit,
    )
    far_v = swap(dv_d, "row", 1)

    def add_kernel(*refs):
        total = refs[0][...].astype(F32)
        for ref in refs[1:-1]:
            total += ref[...].astype(F32)
        refs[-1][...] = total.astype(BF16)

    def add(name, *terms):
        return call(name, add_kernel, [vm(terms[0].shape)], terms)[0]

    def captions_back(h, *after):
        sums = []
        for s in range(Z - 1):
            far = [
                hand_on("far_" + "ab"[h], swap(dcd[2 * (s * (Y - 1) + t - 1) + h], "row", 2 * t), *after, flops=(4, 0)[h] * LONG // 4)
                for t in range(1, Y)
            ]
            sums.append(add("add_" + "ab"[h], dcz[2 * s + h], *far))
        return sums, [swap(sums[s], "col", 4 * (s + 1)) for s in range(Z - 1)]

    sums_a, got_a = captions_back(0, dv_d)
    dcd = [hand_on("far_b", b, dv_d) if i % 2 else b for i, b in enumerate(dcd)]
    def near_clips_kernel(S1, S2, G1, G2, after, dv0, dvx, dvz):
        for i in range(width // CHUNK):
            cols = pl.ds(i * CHUNK, CHUNK)
            part = dot_tn(G1[:, :n3], S1[:, cols]) + dot_tn(G2[:, :n3], S2[:, cols])
            for j, ref in enumerate((dv0, dvx, dvz)):
                ref[:, cols] = part[j * rows : (j + 1) * rows].astype(ref.dtype)

    dv0, dvx, dvz = call(
        "near_clips", near_clips_kernel, [vm(mat, F32), vm(mat), vm(mat, F32)], [S1, S2, G1, G2, sums_a[0]],
        flops=2 * 24 * rows * rows * width, limit=limit,
    )

    sums_b, got_b = captions_back(1, dvz)
    sum_v = add("add_clips", dvz, far_v)
    got_z = hand_on("clips_back", swap(sum_v, "col", 2), flops=3 * LONG)
    got_h = [[hand_on("captions_back", b, sum_v, flops=3 * LONG) for b in got] for got in (got_a, got_b)]
    dcy = [hand_on("near_y", b, *sums_b) for b in dcy]
    got_y = [hand_on("captions_y", swap(dcy[t - 1], "row", 2 * t), sum_v, flops=LONG) for t in range(1, Y)]
    got_x = hand_on("clips_x", swap(dvx, "row", 1), sum_v, flops=4 * LONG)

    def losses_kernel(l_a, l_m, l_c, l_d, after, *refs):
        loss_0, loss_x, loss_z = refs[-3:]
        total = l_c[...] + l_d[...]
        own = total[:, :n3] + l_a[...]
        loss_0[...] = own[:, :n1]
        loss_x[0:1, :] = own[:, n1 : 2 * n1]
        loss_x[1:2, :] = total[:, n3:] + l_m[...]
        loss_z[...] = own[:, 2 * n1 :]

    def add_loss_kernel(loss_z, arrived, got, sum_v, out):
        out[...] = loss_z[...] + arrived[1:2, :]

    loss_0, loss_x, loss_z = call(
        "losses", losses_kernel, [vm((1, n1), F32), vm((2, n1), F32), vm((1, n1), F32)],
        [loss_a, loss_m, loss_c, loss_d, sums_a[0]],
    )
    far_loss = hand_on("losses_x", swap(loss_x, "row", 1), *sums_b)
    (sum_loss,) = call("add_loss", add_loss_kernel, [vm((1, n1), F32)], [loss_z, far_loss, got_a[0], sum_v])
    got_loss = swap(sum_loss, "col", 2)

    def finish(name, losses, consts, hat, inverse, own, whole, halves, *after):
        tail = 2 + 2 * bool(losses)

        def finish_kernel(consts, hat_ref, inverse_ref, *refs):
            adds, (grad, *loss, buf, sems) = refs[: -1 - tail - len(after)], refs[-1 - tail :]
            copies = []
            if losses:
                out, lbuf = loss
                loss_0, far_loss, got_loss = adds[:3]
                lbuf[...] = loss_0[...] + far_loss[0:1, :] + got_loss[...]
                copies.append(pltpu.make_async_copy(lbuf, out, sems.at[2]))
                copies[-1].start()
            adds = adds[len(losses) :]
            for i in range(2):
                part = pl.ds(i * half, half)
                total = adds[0][part, :]
                for ref in adds[1 : 1 + len(whole)]:
                    total += ref[part, :].astype(F32)
                for ref in adds[1 + len(whole) :][i * len(halves[0]) : (i + 1) * len(halves[0])]:
                    total += ref[...].astype(F32)
                total = total * consts[0:1, 0:1]
                hat = hat_ref[part, :]
                along = jnp.sum(hat * total, axis=1, keepdims=True)
                buf[part, :] = inverse_ref[part, :] * (total - hat * along)
                copies.append(pltpu.make_async_copy(buf.at[part], grad.at[part], sems.at[i]))
                copies[-1].start()
            for copy in copies:
                copy.wait()

        return call(
            name, finish_kernel,
            [jax.ShapeDtypeStruct(mat, F32)] + [jax.ShapeDtypeStruct((1, rows), F32)] * bool(losses),
            [consts, hat, inverse, *losses, own, *whole, *halves[0], *halves[1], *after], out_spec="h",
            scratch=[pltpu.VMEM((1, rows), F32)] * bool(losses)
            + [pltpu.VMEM(mat, F32), pltpu.SemaphoreType.DMA((3,))],
        )

    (gc,) = finish("finish_captions", [], consts, chat, cinv, dc0, got_y, got_h, sum_loss)
    gv, clip_loss = finish(
        "finish_clips", [loss_0, far_loss, got_loss], consts, vhat, vinv, dv0, [got_x, got_z], ([], [])
    )
    return clip_loss.reshape(rows), gv, gc


def solution(mesh):
    return jax.shard_map(
        shards,
        mesh=mesh,
        in_specs=(P(("row", "col"), None), P(("col", "row"), None), P(), P(), P()),
        out_specs=(P(("row", "col")), P(("row", "col"), None), P(("col", "row"), None)),
        check_vma=False,
    )
```

```python
import jax
import jax.numpy as jnp
from jax import lax
from jax.experimental import pallas as pl
from jax.experimental.pallas import tpu as pltpu
from jax.sharding import PartitionSpec as P

F32, BF16 = jnp.float32, jnp.bfloat16
MIB = 1024 * 1024
CHUNK = 256
PARTS = 4
LONG = 10**10
SPECS = {
    "s": pl.BlockSpec(memory_space=pltpu.SMEM),
    "v": pl.BlockSpec(memory_space=pltpu.VMEM),
    "h": pl.BlockSpec(memory_space=pl.ANY),
}


def vm(shape, dtype=BF16):
    return pltpu.VMEM(shape, dtype)


def call(name, kernel, out_shape, args, spec="v", out_spec="v", limit=4, flops=0, scratch=(), aliases={}):
    space = {"v": pltpu.VMEM, "h": pltpu.HBM}
    if spec in space:
        args = [pltpu.with_memory_space_constraint(a, space[spec]) for a in args]
    return pl.pallas_call(
        kernel,
        name=name,
        out_shape=out_shape,
        in_specs=[SPECS[spec]] * len(args),
        out_specs=[SPECS[out_spec]] * len(out_shape),
        scratch_shapes=list(scratch),
        input_output_aliases=aliases,
        compiler_params=pltpu.CompilerParams(vmem_limit_bytes=limit * MIB),
        cost_estimate=pl.CostEstimate(flops=flops, bytes_accessed=0, transcendentals=0),
    )(*args)


def hand_on(name, block, *after, flops=0):
    return call(
        name, lambda *refs: None, [vm(block.shape, block.dtype)], [block, *after],
        aliases={0: 0}, flops=flops,
    )[0]


def unit_rows(rows):
    inverse = lax.rsqrt(jnp.sum(rows * rows, axis=1, keepdims=True) + 1e-06)
    return rows * inverse, inverse


def dot_nt(a, b):
    return lax.dot_general(a, b, (((1,), (1,)), ((), ())), preferred_element_type=F32)


def dot_tn(a, b):
    return lax.dot_general(a, b, (((0,), (0,)), ((), ())), preferred_element_type=F32)


def dot_nn(a, b):
    return jnp.dot(a, b, preferred_element_type=F32)


def log1p_sum(e):
    rows = e.shape[0]
    u = e
    for _ in range(3):
        rows //= 2
        a, b = u[:rows], u[rows:]
        u = a + b + a * b
    series = u * (1.0 - u * (0.5 - u * (1.0 / 3.0 - u * 0.25)))
    logs = jnp.where(u < 0.01, series, jnp.log(1.0 + u))
    return jnp.sum(logs, axis=0, keepdims=True)


def pairs(dots, scale, shift, base, labels, counted):
    logits = dots * scale + shift
    match = lax.broadcasted_iota(jnp.int32, logits.shape, 0) == labels - base
    e = jnp.exp(-jnp.abs(logits))
    whole = 1.0 + e
    over = pl.reciprocal(whole, approx=True)
    over = over * (2.0 - whole * over)
    sigmoid = jnp.where(logits >= 0.0, over, e * over)
    coef = (sigmoid - jnp.where(match, 1.0, 0.0)).astype(BF16)
    if not counted:
        return coef, None
    e, logits, match = e[:, :counted], logits[:, :counted], match[:, :counted]
    linear = jnp.maximum(jnp.where(match, -logits, logits), 0.0)
    return coef, jnp.sum(linear, axis=0, keepdims=True) + log1p_sum(e)


def stack(target, blocks):
    at = 0
    for b in blocks:
        target[pl.ds(at, b.shape[0]), :] = b[...]
        at += b.shape[0]


def shards(film, text, matched, sharpness, offset):
    rows, width = film.shape
    half = rows // 2
    R, C = lax.axis_size("row"), lax.axis_size("col")
    Y, Z = R // 2, C // 4
    mat, hmat = (rows, width), (half, width)
    limit = 6 + 2 * (Y * Z * 2 * rows) // 1024

    def swap(value, axis, bits):
        size = lax.axis_size(axis)
        return lax.ppermute(value, axis, [(i, i ^ bits) for i in range(size)])

    def first_caption(s, t, k):
        r, c = lax.axis_index("row"), lax.axis_index("col")
        return ((c ^ (4 * s + k)) * R + (r ^ (2 * t))) * rows

    def clip_index(x, z, k):
        r, c = lax.axis_index("row"), lax.axis_index("col")
        return (r ^ x) * C + (c ^ (2 * z + k))

    near = [(0, t) for t in range(Y)]
    up = [(s, 0) for s in range(1, Z)]
    diag = [(s, t) for s in range(1, Z) for t in range(1, Y)]
    clip_order = [(x, z, k) for k in range(2) for z in range(2) for x in range(2)]
    nn, na, nd = len(near) * rows, len(near + up) * rows, len(diag) * rows
    n1, n3, n4, n7 = rows, 3 * rows, 4 * rows, 7 * rows

    def strip(consts, blocks, k, captions, clips, labels, counted, put):
        scale, shift = consts[0:1, 0:1], consts[1:2, 0:1]
        dots = dot_nt(captions, clips)
        total = 0.0
        for i, (s, t) in enumerate(blocks):
            block = dots[i * rows : (i + 1) * rows]
            coef, add = pairs(block, scale, shift, first_caption(s, t, k), labels, counted)
            put(i * rows, coef)
            total = total + add if counted else None
        return total

    def put_in(target, first=0, left=0):
        def put(at, coef):
            target[pl.ds(first + at, coef.shape[0]), pl.ds(left, coef.shape[1])] = coef
        return put

    def normalize_kernel(film, text, matched, v16, c16, va, vb, vhat, chat, vinv, cinv, labels, fbuf, tbuf, mbuf, sems):
        step = rows // PARTS
        get_matched = pltpu.make_async_copy(matched, mbuf, sems.at[2 * PARTS])
        copies = []
        for j, (src, buf) in enumerate(((film, fbuf), (text, tbuf))):
            for i in range(PARTS):
                part = pl.ds(i * step, step)
                copies.append(pltpu.make_async_copy(src.at[part], buf.at[part], sems.at[j * PARTS + i]))
        for copy in copies:
            copy.start()
        get_matched.start()
        for copy in copies[:PARTS]:
            copy.wait()
        hat, inverse = unit_rows(fbuf[...])
        vhat[...], vinv[...], v16[...] = hat, inverse, hat.astype(BF16)
        va[...] = hat[:half].astype(BF16)
        vb[...] = hat[half:].astype(BF16)
        for copy in copies[PARTS:]:
            copy.wait()
        hat, inverse = unit_rows(tbuf[...])
        chat[...], cinv[...], c16[...] = hat, inverse, hat.astype(BF16)
        get_matched.wait()
        labels[...] = jnp.concatenate(
            [mbuf[pl.ds(clip_index(*p), 1), :] for p in clip_order], axis=1
        )

    matched = matched.reshape(-1, rows)
    v16, c16, va, vb, vhat, chat, vinv, cinv, labels = call(
        "normalize", normalize_kernel,
        [vm(mat), vm(mat)] + [vm(hmat)] * 2 + [vm(mat, F32), vm(mat, F32), vm((rows, 1), F32), vm((rows, 1), F32),
         vm((1, 8 * rows), jnp.int32)],
        [film, text, matched], spec="h", limit=8,
        scratch=[pltpu.VMEM(mat, F32)] * 2
        + [pltpu.VMEM(matched.shape, jnp.int32), pltpu.SemaphoreType.DMA((2 * PARTS + 1,))],
    )

    def consts_kernel(scale, shift, out):
        out[0:1, :] = jnp.full((1, 128), scale[0], F32)
        out[1:2, :] = jnp.full((1, 128), shift[0], F32)

    (consts,) = call("consts", consts_kernel, [vm((2, 128), F32)], [sharpness, offset], spec="s")

    def join(name, *blocks):
        def join_kernel(*refs):
            stack(refs[-1], refs[:-1])

        return call(name, join_kernel, [vm((sum(b.shape[0] for b in blocks), width))], blocks)[0]

    v_z = [hand_on("clips_z", swap(b, "col", 2), flops=n * LONG // 4) for b, n in ((va, 4), (vb, 24))]
    c_z = [hand_on("captions_z", swap(c16, "col", 4 * s), consts, flops=4 * LONG // 4) for s in range(1, Z)]
    c_y = [swap(c16, "row", 2 * t) for t in range(1, Y)]
    v_x = swap(v16, "row", 1)
    v_d = [hand_on("clips_d", swap(b, "row", 1), flops=2 * LONG // 4) for b in v_z]
    c_d = [swap(b, "row", 2 * t) for b in c_z for t in range(1, Y)]
    N = join("near_blocks", c16, *c_y, v16, v_x, *v_z)
    N_k = hand_on("near_other", swap(N, "col", 1), flops=4 * LONG // 4)
    cz_k = [swap(b, "col", 1) for b in c_z]
    v_d = join("diagonal_clips", *v_d)
    vd_k = swap(v_d, "col", 1)

    def early_kernel(consts, labels, N, N_k, *refs):
        n = len(up)
        cz, czk, (S1, p, q, loss) = refs[:n], refs[n : 2 * n], refs[2 * n :]
        stack(S1, [N.at[:nn], *cz, N_k.at[:nn], *czk])
        own = N[nn:, :]
        loss[...] = strip(
            consts, near + up, 0, S1[:na, :], own, labels[:, :n3], n3, put_in(p)
        ) + strip(consts, near + up, 1, S1[na:, :], own, labels[:, :n3], n3, put_in(q))
        strip(
            consts, near + up, 0, S1[:na, :], N_k[nn:, :], labels[:, n4:n7], 0, put_in(p, left=n3)
        )

    S1, p, q, loss_a = call(
        "early_pairs", early_kernel,
        [vm((2 * na, width)), vm((na, 2 * n3)), vm((na, n3)), vm((1, n3), F32)],
        [consts, labels, N, N_k, *c_z, *cz_k],
        flops=2 * 27 * rows * rows * width, limit=limit,
    )

    def middle_kernel(consts, labels, N, N_k, vd, vdk, S1, p, q, VV, G1, loss, dc0, *refs):
        dcy, dcz, coef = refs[: Y - 1], refs[Y - 1 : -1], refs[-1]
        stack(VV, [N.at[nn:], vd, N_k.at[nn:], vdk])
        coef[:, :n3] = p[:, :n3]
        coef[:, n4:n7] = p[:, n3:]
        G1[na:, :n3] = q[...]
        late = labels[:, n3:n4]
        loss[...] = strip(
            consts, near + up, 0, S1[:na, :], vd[...], late, n1, put_in(coef, left=n3)
        ) + strip(consts, near + up, 1, S1[na:, :], vd[...], late, n1, put_in(G1, na, n3))
        strip(consts, near + up, 0, S1[:na, :], vdk[...], labels[:, n7:], 0, put_in(coef, left=n7))
        G1[:na, :] = coef[:, :n4]
        for i in range(width // CHUNK):
            cols = pl.ds(i * CHUNK, CHUNK)
            part = dot_nn(coef[...], VV[:, cols])
            for j, ref in enumerate((dc0, *dcy)):
                ref[:, cols] = part[j * rows : (j + 1) * rows].astype(ref.dtype)
            for j, ref in enumerate(dcz):
                ref[:, cols] = part[nn + j * half : nn + (j + 1) * half]

    VV, G1, loss_m, dc0, *dcs = call(
        "middle_sums", middle_kernel,
        [vm((8 * n1, width)), vm((2 * na, n4)), vm((1, n1), F32), vm(mat, F32)]
        + [vm(mat)] * (Y - 1) + [vm(hmat, F32)] * (2 * (Z - 1)),
        [consts, labels, N, N_k, v_d, vd_k, S1, p, q],
        flops=2 * 33 * rows * rows * width, limit=limit,
        scratch=[pltpu.VMEM((na, 8 * n1), BF16)],
    )
    dcy, dcz = dcs[: Y - 1], dcs[Y - 1 :]
    c_d = [hand_on("captions_d", b, dc0, flops=3 * LONG) for b in c_d]
    D_k = [swap(b, "col", 1) for b in c_d]

    def far_captions_kernel(consts, labels, VV, *refs):
        n = len(diag)
        caps, (loss, p, *sums, D, coef) = refs[:n], refs[n:]
        stack(D, caps)
        loss[...] = strip(consts, diag, 0, D[...], VV[...], labels[...], n4, put_in(coef))
        p[...] = coef[:, :n4]
        for i in range(width // CHUNK):
            cols = pl.ds(i * CHUNK, CHUNK)
            part = dot_nn(coef[...], VV[:, cols])
            for j, ref in enumerate(sums):
                ref[:, cols] = part[j * half : (j + 1) * half].astype(BF16)

    loss_c, p_d, *dcd = call(
        "far_captions", far_captions_kernel,
        [vm((1, n4), F32), vm((nd, n4))] + [vm(hmat)] * (2 * len(diag)),
        [consts, labels, VV, *c_d],
        flops=2 * 16 * rows * rows * width, limit=limit,
        scratch=[pltpu.VMEM((nd, width), BF16), pltpu.VMEM((nd, 8 * n1), BF16)],
    )

    def far_clips_kernel(consts, labels, VV, S1, G1, p_d, *refs):
        n = len(diag)
        caps, (S2, G2, loss, dv) = refs[: 2 * n], refs[2 * n :]
        stack(S2, caps)
        G2[:nd, :] = p_d[...]
        loss[...] = strip(consts, diag, 1, S2[nd:, :], VV[:n4, :], labels[:, :n4], n4, put_in(G2, nd))
        for i in range(width // CHUNK):
            cols = pl.ds(i * CHUNK, CHUNK)
            dv[:, cols] = (dot_tn(G1[:, n3:], S1[:, cols]) + dot_tn(G2[:, n3:], S2[:, cols])).astype(BF16)

    S2, G2, loss_d, dv_d = call(
        "far_clips", far_clips_kernel,
        [vm((2 * nd, width)), vm((2 * nd, n4)), vm((1, n4), F32), vm(mat)],
        [consts, labels, VV, S1, G1, p_d, *c_d, *D_k],
        flops=2 * 12 * rows * rows * width, limit=limit,
    )
    far_v = swap(dv_d, "row", 1)

    def add_kernel(*refs):
        total = refs[0][...].astype(F32)
        for ref in refs[1:-1]:
            total += ref[...].astype(F32)
        refs[-1][...] = total.astype(BF16)

    def add(name, *terms):
        return call(name, add_kernel, [vm(terms[0].shape)], terms)[0]

    def captions_back(h, *after):
        sums = []
        for s in range(Z - 1):
            far = [
                hand_on("far_" + "ab"[h], swap(dcd[2 * (s * (Y - 1) + t - 1) + h], "row", 2 * t), *after, flops=(4, 0)[h] * LONG // 4)
                for t in range(1, Y)
            ]
            sums.append(add("add_" + "ab"[h], dcz[2 * s + h], *far))
        return sums, [swap(sums[s], "col", 4 * (s + 1)) for s in range(Z - 1)]

    sums_a, got_a = captions_back(0, dv_d)
    dcd = [hand_on("far_b", b, dv_d) if i % 2 else b for i, b in enumerate(dcd)]
    def near_clips_kernel(S1, S2, G1, G2, after, dv0, dvx, dvz):
        for i in range(width // CHUNK):
            cols = pl.ds(i * CHUNK, CHUNK)
            part = dot_tn(G1[:, :n3], S1[:, cols]) + dot_tn(G2[:, :n3], S2[:, cols])
            for j, ref in enumerate((dv0, dvx, dvz)):
                ref[:, cols] = part[j * rows : (j + 1) * rows].astype(ref.dtype)

    dv0, dvx, dvz = call(
        "near_clips", near_clips_kernel, [vm(mat, F32), vm(mat), vm(mat, F32)], [S1, S2, G1, G2, sums_a[0]],
        flops=2 * 24 * rows * rows * width, limit=limit,
    )

    sums_b, got_b = captions_back(1, dvz)
    sum_v = add("add_clips", dvz, far_v)
    got_z = hand_on("clips_back", swap(sum_v, "col", 2), flops=3 * LONG)
    got_h = [[hand_on("captions_back", b, sum_v, flops=3 * LONG) for b in got] for got in (got_a, got_b)]
    dcy = [hand_on("near_y", b, *sums_b) for b in dcy]
    dvx = hand_on("near_x", dvx, *sums_b)
    got_y = [hand_on("captions_y", swap(dcy[t - 1], "row", 2 * t), sum_v, flops=LONG) for t in range(1, Y)]
    got_x = hand_on("clips_x", swap(dvx, "row", 1), sum_v, flops=4 * LONG)

    def losses_kernel(l_a, l_m, l_c, l_d, after, *refs):
        loss_0, loss_x, loss_z = refs[-3:]
        total = l_c[...] + l_d[...]
        own = total[:, :n3] + l_a[...]
        loss_0[...] = own[:, :n1]
        loss_x[0:1, :] = own[:, n1 : 2 * n1]
        loss_x[1:2, :] = total[:, n3:] + l_m[...]
        loss_z[...] = own[:, 2 * n1 :]

    def add_loss_kernel(loss_z, arrived, got, sum_v, out):
        out[...] = loss_z[...] + arrived[1:2, :]

    loss_0, loss_x, loss_z = call(
        "losses", losses_kernel, [vm((1, n1), F32), vm((2, n1), F32), vm((1, n1), F32)],
        [loss_a, loss_m, loss_c, loss_d, sums_a[0]],
    )
    far_loss = hand_on("losses_x", swap(loss_x, "row", 1), *sums_b)
    (sum_loss,) = call("add_loss", add_loss_kernel, [vm((1, n1), F32)], [loss_z, far_loss, got_a[0], sum_v])
    got_loss = swap(sum_loss, "col", 2)

    def finish(name, losses, consts, hat, inverse, own, whole, halves, *after):
        tail = 2 + 2 * bool(losses)

        def finish_kernel(consts, hat_ref, inverse_ref, *refs):
            adds, (grad, *loss, buf, sems) = refs[: -1 - tail - len(after)], refs[-1 - tail :]
            copies = []
            if losses:
                out, lbuf = loss
                loss_0, far_loss, got_loss = adds[:3]
                lbuf[...] = loss_0[...] + far_loss[0:1, :] + got_loss[...]
                copies.append(pltpu.make_async_copy(lbuf, out, sems.at[2]))
                copies[-1].start()
            adds = adds[len(losses) :]
            for i in range(2):
                part = pl.ds(i * half, half)
                total = adds[0][part, :]
                for ref in adds[1 : 1 + len(whole)]:
                    total += ref[part, :].astype(F32)
                for ref in adds[1 + len(whole) :][i * len(halves[0]) : (i + 1) * len(halves[0])]:
                    total += ref[...].astype(F32)
                total = total * consts[0:1, 0:1]
                hat = hat_ref[part, :]
                along = jnp.sum(hat * total, axis=1, keepdims=True)
                buf[part, :] = inverse_ref[part, :] * (total - hat * along)
                copies.append(pltpu.make_async_copy(buf.at[part], grad.at[part], sems.at[i]))
                copies[-1].start()
            for copy in copies:
                copy.wait()

        return call(
            name, finish_kernel,
            [jax.ShapeDtypeStruct(mat, F32)] + [jax.ShapeDtypeStruct((1, rows), F32)] * bool(losses),
            [consts, hat, inverse, *losses, own, *whole, *halves[0], *halves[1], *after], out_spec="h",
            scratch=[pltpu.VMEM((1, rows), F32)] * bool(losses)
            + [pltpu.VMEM(mat, F32), pltpu.SemaphoreType.DMA((3,))],
        )

    (gc,) = finish("finish_captions", [], consts, chat, cinv, dc0, got_y, got_h, sum_loss)
    gv, clip_loss = finish(
        "finish_clips", [loss_0, far_loss, got_loss], consts, vhat, vinv, dv0, [got_x, got_z], ([], [])
    )
    return clip_loss.reshape(rows), gv, gc


def solution(mesh):
    return jax.shard_map(
        shards,
        mesh=mesh,
        in_specs=(P(("row", "col"), None), P(("col", "row"), None), P(), P(), P()),
        out_specs=(P(("row", "col")), P(("row", "col"), None), P(("col", "row"), None)),
        check_vma=False,
    )
```

```python
import jax
import jax.numpy as jnp
from jax import lax
from jax.experimental import pallas as pl
from jax.experimental.pallas import tpu as pltpu
from jax.sharding import PartitionSpec as P

F32, BF16 = jnp.float32, jnp.bfloat16
MIB = 1024 * 1024
CHUNK = 256
PARTS = 4
LONG = 10**10
SPECS = {
    "s": pl.BlockSpec(memory_space=pltpu.SMEM),
    "v": pl.BlockSpec(memory_space=pltpu.VMEM),
    "h": pl.BlockSpec(memory_space=pl.ANY),
}


def vm(shape, dtype=BF16):
    return pltpu.VMEM(shape, dtype)


def call(name, kernel, out_shape, args, spec="v", out_spec="v", limit=4, flops=0, scratch=(), aliases={}):
    space = {"v": pltpu.VMEM, "h": pltpu.HBM}
    if spec in space:
        args = [pltpu.with_memory_space_constraint(a, space[spec]) for a in args]
    return pl.pallas_call(
        kernel,
        name=name,
        out_shape=out_shape,
        in_specs=[SPECS[spec]] * len(args),
        out_specs=[SPECS[out_spec]] * len(out_shape),
        scratch_shapes=list(scratch),
        input_output_aliases=aliases,
        compiler_params=pltpu.CompilerParams(vmem_limit_bytes=limit * MIB),
        cost_estimate=pl.CostEstimate(flops=flops, bytes_accessed=0, transcendentals=0),
    )(*args)


def hand_on(name, block, *after, flops=0):
    return call(
        name, lambda *refs: None, [vm(block.shape, block.dtype)], [block, *after],
        aliases={0: 0}, flops=flops,
    )[0]


def unit_rows(rows):
    inverse = lax.rsqrt(jnp.sum(rows * rows, axis=1, keepdims=True) + 1e-06)
    return rows * inverse, inverse


def dot_nt(a, b):
    return lax.dot_general(a, b, (((1,), (1,)), ((), ())), preferred_element_type=F32)


def dot_tn(a, b):
    return lax.dot_general(a, b, (((0,), (0,)), ((), ())), preferred_element_type=F32)


def dot_nn(a, b):
    return jnp.dot(a, b, preferred_element_type=F32)


def log1p_sum(e):
    rows = e.shape[0]
    u = e
    for _ in range(3):
        rows //= 2
        a, b = u[:rows], u[rows:]
        u = a + b + a * b
    series = u * (1.0 - u * (0.5 - u * (1.0 / 3.0 - u * 0.25)))
    logs = jnp.where(u < 0.01, series, jnp.log(1.0 + u))
    return jnp.sum(logs, axis=0, keepdims=True)


def pairs(dots, scale, shift, base, labels, counted):
    logits = dots * scale + shift
    match = lax.broadcasted_iota(jnp.int32, logits.shape, 0) == labels - base
    e = jnp.exp(-jnp.abs(logits))
    whole = 1.0 + e
    over = pl.reciprocal(whole, approx=True)
    over = over * (2.0 - whole * over)
    sigmoid = jnp.where(logits >= 0.0, over, e * over)
    coef = (sigmoid - jnp.where(match, 1.0, 0.0)).astype(BF16)
    if not counted:
        return coef, None
    e, logits, match = e[:, :counted], logits[:, :counted], match[:, :counted]
    linear = jnp.maximum(jnp.where(match, -logits, logits), 0.0)
    return coef, jnp.sum(linear, axis=0, keepdims=True) + log1p_sum(e)


def stack(target, blocks):
    at = 0
    for b in blocks:
        target[pl.ds(at, b.shape[0]), :] = b[...]
        at += b.shape[0]


def shards(film, text, matched, sharpness, offset):
    rows, width = film.shape
    half = rows // 2
    R, C = lax.axis_size("row"), lax.axis_size("col")
    Y, Z = R // 2, C // 4
    mat, hmat = (rows, width), (half, width)
    limit = 6 + 2 * (Y * Z * 2 * rows) // 1024

    def swap(value, axis, bits):
        size = lax.axis_size(axis)
        return lax.ppermute(value, axis, [(i, i ^ bits) for i in range(size)])

    def first_caption(s, t, k):
        r, c = lax.axis_index("row"), lax.axis_index("col")
        return ((c ^ (4 * s + k)) * R + (r ^ (2 * t))) * rows

    def clip_index(x, z, k):
        r, c = lax.axis_index("row"), lax.axis_index("col")
        return (r ^ x) * C + (c ^ (2 * z + k))

    near = [(0, t) for t in range(Y)]
    up = [(s, 0) for s in range(1, Z)]
    diag = [(s, t) for s in range(1, Z) for t in range(1, Y)]
    clip_order = [(x, z, k) for k in range(2) for z in range(2) for x in range(2)]
    nn, na, nd = len(near) * rows, len(near + up) * rows, len(diag) * rows
    n1, n3, n4, n7 = rows, 3 * rows, 4 * rows, 7 * rows

    def strip(consts, blocks, k, captions, clips, labels, counted, put):
        scale, shift = consts[0:1, 0:1], consts[1:2, 0:1]
        dots = dot_nt(captions, clips)
        total = 0.0
        for i, (s, t) in enumerate(blocks):
            block = dots[i * rows : (i + 1) * rows]
            coef, add = pairs(block, scale, shift, first_caption(s, t, k), labels, counted)
            put(i * rows, coef)
            total = total + add if counted else None
        return total

    def put_in(target, first=0, left=0):
        def put(at, coef):
            target[pl.ds(first + at, coef.shape[0]), pl.ds(left, coef.shape[1])] = coef
        return put

    def normalize_kernel(film, text, matched, v16, c16, va, vb, vhat, chat, vinv, cinv, labels, fbuf, tbuf, mbuf, sems):
        step = rows // PARTS
        get_matched = pltpu.make_async_copy(matched, mbuf, sems.at[2 * PARTS])
        copies = []
        for j, (src, buf) in enumerate(((film, fbuf), (text, tbuf))):
            for i in range(PARTS):
                part = pl.ds(i * step, step)
                copies.append(pltpu.make_async_copy(src.at[part], buf.at[part], sems.at[j * PARTS + i]))
        for copy in copies:
            copy.start()
        get_matched.start()
        for copy in copies[:PARTS]:
            copy.wait()
        hat, inverse = unit_rows(fbuf[...])
        vhat[...], vinv[...], v16[...] = hat, inverse, hat.astype(BF16)
        va[...] = hat[:half].astype(BF16)
        vb[...] = hat[half:].astype(BF16)
        for copy in copies[PARTS:]:
            copy.wait()
        hat, inverse = unit_rows(tbuf[...])
        chat[...], cinv[...], c16[...] = hat, inverse, hat.astype(BF16)
        get_matched.wait()
        labels[...] = jnp.concatenate(
            [mbuf[pl.ds(clip_index(*p), 1), :] for p in clip_order], axis=1
        )

    matched = matched.reshape(-1, rows)
    v16, c16, va, vb, vhat, chat, vinv, cinv, labels = call(
        "normalize", normalize_kernel,
        [vm(mat), vm(mat)] + [vm(hmat)] * 2 + [vm(mat, F32), vm(mat, F32), vm((rows, 1), F32), vm((rows, 1), F32),
         vm((1, 8 * rows), jnp.int32)],
        [film, text, matched], spec="h", limit=8,
        scratch=[pltpu.VMEM(mat, F32)] * 2
        + [pltpu.VMEM(matched.shape, jnp.int32), pltpu.SemaphoreType.DMA((2 * PARTS + 1,))],
    )

    def consts_kernel(scale, shift, out):
        out[0:1, :] = jnp.full((1, 128), scale[0], F32)
        out[1:2, :] = jnp.full((1, 128), shift[0], F32)

    (consts,) = call("consts", consts_kernel, [vm((2, 128), F32)], [sharpness, offset], spec="s")

    def join(name, *blocks):
        def join_kernel(*refs):
            stack(refs[-1], refs[:-1])

        return call(name, join_kernel, [vm((sum(b.shape[0] for b in blocks), width))], blocks)[0]

    v_z = [hand_on("clips_z", swap(b, "col", 2), flops=n * LONG // 4) for b, n in ((va, 4), (vb, 24))]
    c_z = [hand_on("captions_z", swap(c16, "col", 4 * s), consts, flops=4 * LONG // 4) for s in range(1, Z)]
    c_y = [swap(c16, "row", 2 * t) for t in range(1, Y)]
    v_x = swap(v16, "row", 1)
    v_d = [hand_on("clips_d", swap(b, "row", 1), flops=2 * LONG // 4) for b in v_z]
    c_d = [swap(b, "row", 2 * t) for b in c_z for t in range(1, Y)]
    N = join("near_blocks", c16, *c_y, v16, v_x, *v_z)
    N_k = hand_on("near_other", swap(N, "col", 1), flops=4 * LONG // 4)
    cz_k = [swap(b, "col", 1) for b in c_z]
    v_d = join("diagonal_clips", *v_d)
    vd_k = swap(v_d, "col", 1)

    def early_kernel(consts, labels, N, N_k, *refs):
        n = len(up)
        cz, czk, (S1, p, q, loss) = refs[:n], refs[n : 2 * n], refs[2 * n :]
        stack(S1, [N.at[:nn], *cz, N_k.at[:nn], *czk])
        own = N[nn:, :]
        loss[...] = strip(
            consts, near + up, 0, S1[:na, :], own, labels[:, :n3], n3, put_in(p)
        ) + strip(consts, near + up, 1, S1[na:, :], own, labels[:, :n3], n3, put_in(q))
        strip(
            consts, near + up, 0, S1[:na, :], N_k[nn:, :], labels[:, n4:n7], 0, put_in(p, left=n3)
        )

    S1, p, q, loss_a = call(
        "early_pairs", early_kernel,
        [vm((2 * na, width)), vm((na, 2 * n3)), vm((na, n3)), vm((1, n3), F32)],
        [consts, labels, N, N_k, *c_z, *cz_k],
        flops=2 * 27 * rows * rows * width, limit=limit,
    )

    def middle_kernel(consts, labels, N, N_k, vd, vdk, S1, p, q, VV, G1, coef, loss):
        stack(VV, [N.at[nn:], vd, N_k.at[nn:], vdk])
        coef[:, :n3] = p[:, :n3]
        coef[:, n4:n7] = p[:, n3:]
        G1[na:, :n3] = q[...]
        late = labels[:, n3:n4]
        loss[...] = strip(
            consts, near + up, 0, S1[:na, :], vd[...], late, n1, put_in(coef, left=n3)
        ) + strip(consts, near + up, 1, S1[na:, :], vd[...], late, n1, put_in(G1, na, n3))
        strip(consts, near + up, 0, S1[:na, :], vdk[...], labels[:, n7:], 0, put_in(coef, left=n7))
        G1[:na, :] = coef[:, :n4]

    VV, G1, coef_a, loss_m = call(
        "middle_pairs", middle_kernel,
        [vm((8 * n1, width)), vm((2 * na, n4)), vm((na, 8 * n1)), vm((1, n1), F32)],
        [consts, labels, N, N_k, v_d, vd_k, S1, p, q],
        flops=2 * 9 * rows * rows * width, limit=limit,
    )
    c_d = [hand_on("captions_d", b, loss_m, flops=3 * LONG) for b in c_d]
    D_k = [swap(b, "col", 1) for b in c_d]

    def far_captions_kernel(consts, labels, VV, *refs):
        n = len(diag)
        caps, (loss, p, *sums, D, coef) = refs[:n], refs[n:]
        stack(D, caps)
        loss[...] = strip(consts, diag, 0, D[...], VV[...], labels[...], n4, put_in(coef))
        p[...] = coef[:, :n4]
        for i in range(width // CHUNK):
            cols = pl.ds(i * CHUNK, CHUNK)
            part = dot_nn(coef[...], VV[:, cols])
            for j, ref in enumerate(sums):
                ref[:, cols] = part[j * half : (j + 1) * half].astype(BF16)

    loss_c, p_d, *dcd = call(
        "far_captions", far_captions_kernel,
        [vm((1, n4), F32), vm((nd, n4))] + [vm(hmat)] * (2 * len(diag)),
        [consts, labels, VV, *c_d],
        flops=2 * 16 * rows * rows * width, limit=limit,
        scratch=[pltpu.VMEM((nd, width), BF16), pltpu.VMEM((nd, 8 * n1), BF16)],
    )

    def far_clips_kernel(consts, labels, VV, S1, G1, p_d, *refs):
        n = len(diag)
        caps, (S2, G2, loss, dv) = refs[: 2 * n], refs[2 * n :]
        stack(S2, caps)
        G2[:nd, :] = p_d[...]
        loss[...] = strip(consts, diag, 1, S2[nd:, :], VV[:n4, :], labels[:, :n4], n4, put_in(G2, nd))
        for i in range(width // CHUNK):
            cols = pl.ds(i * CHUNK, CHUNK)
            dv[:, cols] = (dot_tn(G1[:, n3:], S1[:, cols]) + dot_tn(G2[:, n3:], S2[:, cols])).astype(BF16)

    S2, G2, loss_d, dv_d = call(
        "far_clips", far_clips_kernel,
        [vm((2 * nd, width)), vm((2 * nd, n4)), vm((1, n4), F32), vm(mat)],
        [consts, labels, VV, S1, G1, p_d, *c_d, *D_k],
        flops=2 * 12 * rows * rows * width, limit=limit,
    )
    far_v = swap(dv_d, "row", 1)

    def near_captions_kernel(coef, VV, after, dc0, *refs):
        dcy, dcz = refs[: Y - 1], refs[Y - 1 :]
        for i in range(width // CHUNK):
            cols = pl.ds(i * CHUNK, CHUNK)
            part = dot_nn(coef[...], VV[:, cols])
            for j, ref in enumerate((dc0, *dcy)):
                ref[:, cols] = part[j * rows : (j + 1) * rows].astype(ref.dtype)
            for j, ref in enumerate(dcz):
                ref[:, cols] = part[nn + j * half : nn + (j + 1) * half]

    dc0, *dcs = call(
        "near_captions", near_captions_kernel,
        [vm(mat, F32)] + [vm(mat)] * (Y - 1) + [vm(hmat, F32)] * (2 * (Z - 1)),
        [coef_a, VV, dv_d],
        flops=2 * 24 * rows * rows * width, limit=limit,
    )
    dcy, dcz = dcs[: Y - 1], dcs[Y - 1 :]

    def add_kernel(*refs):
        total = refs[0][...].astype(F32)
        for ref in refs[1:-1]:
            total += ref[...].astype(F32)
        refs[-1][...] = total.astype(BF16)

    def add(name, *terms):
        return call(name, add_kernel, [vm(terms[0].shape)], terms)[0]

    def captions_back(h, *after):
        sums = []
        for s in range(Z - 1):
            far = [
                hand_on("far_" + "ab"[h], swap(dcd[2 * (s * (Y - 1) + t - 1) + h], "row", 2 * t), *after, flops=(4, 0)[h] * LONG // 4)
                for t in range(1, Y)
            ]
            sums.append(add("add_" + "ab"[h], dcz[2 * s + h], *far))
        return sums, [swap(sums[s], "col", 4 * (s + 1)) for s in range(Z - 1)]

    sums_a, got_a = captions_back(0, dc0)
    dcd = [hand_on("far_b", b, dv_d) if i % 2 else b for i, b in enumerate(dcd)]
    def near_clips_kernel(S1, S2, G1, G2, after, dv0, dvx, dvz):
        for i in range(width // CHUNK):
            cols = pl.ds(i * CHUNK, CHUNK)
            part = dot_tn(G1[:, :n3], S1[:, cols]) + dot_tn(G2[:, :n3], S2[:, cols])
            for j, ref in enumerate((dv0, dvx, dvz)):
                ref[:, cols] = part[j * rows : (j + 1) * rows].astype(ref.dtype)

    dv0, dvx, dvz = call(
        "near_clips", near_clips_kernel, [vm(mat, F32), vm(mat), vm(mat, F32)], [S1, S2, G1, G2, sums_a[0]],
        flops=2 * 24 * rows * rows * width, limit=limit,
    )

    sums_b, got_b = captions_back(1, dvz)
    sum_v = add("add_clips", dvz, far_v)
    got_z = hand_on("clips_back", swap(sum_v, "col", 2), flops=3 * LONG)
    got_h = [[hand_on("captions_back", b, sum_v, flops=3 * LONG) for b in got] for got in (got_a, got_b)]
    dcy = [hand_on("near_y", b, *sums_b) for b in dcy]
    dvx = hand_on("near_x", dvx, sum_v)
    got_y = [hand_on("captions_y", swap(dcy[t - 1], "row", 2 * t), sum_v, flops=LONG) for t in range(1, Y)]
    got_x = hand_on("clips_x", swap(dvx, "row", 1), sum_v, flops=4 * LONG)

    def losses_kernel(l_a, l_m, l_c, l_d, after, *refs):
        loss_0, loss_x, loss_z = refs[-3:]
        total = l_c[...] + l_d[...]
        own = total[:, :n3] + l_a[...]
        loss_0[...] = own[:, :n1]
        loss_x[0:1, :] = own[:, n1 : 2 * n1]
        loss_x[1:2, :] = total[:, n3:] + l_m[...]
        loss_z[...] = own[:, 2 * n1 :]

    def add_loss_kernel(loss_z, arrived, got, sum_v, out):
        out[...] = loss_z[...] + arrived[1:2, :]

    loss_0, loss_x, loss_z = call(
        "losses", losses_kernel, [vm((1, n1), F32), vm((2, n1), F32), vm((1, n1), F32)],
        [loss_a, loss_m, loss_c, loss_d, sums_a[0]],
    )
    far_loss = hand_on("losses_x", swap(loss_x, "row", 1), *sums_b)
    (sum_loss,) = call("add_loss", add_loss_kernel, [vm((1, n1), F32)], [loss_z, far_loss, got_b[0], sum_v])
    got_loss = swap(sum_loss, "col", 2)

    def finish(name, losses, consts, hat, inverse, own, whole, halves, *after):
        tail = 2 + 2 * bool(losses)

        def finish_kernel(consts, hat_ref, inverse_ref, *refs):
            adds, (grad, *loss, buf, sems) = refs[: -1 - tail - len(after)], refs[-1 - tail :]
            copies = []
            if losses:
                out, lbuf = loss
                loss_0, far_loss, got_loss = adds[:3]
                lbuf[...] = loss_0[...] + far_loss[0:1, :] + got_loss[...]
                copies.append(pltpu.make_async_copy(lbuf, out, sems.at[2]))
                copies[-1].start()
            adds = adds[len(losses) :]
            for i in range(2):
                part = pl.ds(i * half, half)
                total = adds[0][part, :]
                for ref in adds[1 : 1 + len(whole)]:
                    total += ref[part, :].astype(F32)
                for ref in adds[1 + len(whole) :][i * len(halves[0]) : (i + 1) * len(halves[0])]:
                    total += ref[...].astype(F32)
                total = total * consts[0:1, 0:1]
                hat = hat_ref[part, :]
                along = jnp.sum(hat * total, axis=1, keepdims=True)
                buf[part, :] = inverse_ref[part, :] * (total - hat * along)
                copies.append(pltpu.make_async_copy(buf.at[part], grad.at[part], sems.at[i]))
                copies[-1].start()
            for copy in copies:
                copy.wait()

        return call(
            name, finish_kernel,
            [jax.ShapeDtypeStruct(mat, F32)] + [jax.ShapeDtypeStruct((1, rows), F32)] * bool(losses),
            [consts, hat, inverse, *losses, own, *whole, *halves[0], *halves[1], *after], out_spec="h",
            scratch=[pltpu.VMEM((1, rows), F32)] * bool(losses)
            + [pltpu.VMEM(mat, F32), pltpu.SemaphoreType.DMA((3,))],
        )

    (gc,) = finish("finish_captions", [], consts, chat, cinv, dc0, got_y, got_h, sum_loss)
    gv, clip_loss = finish(
        "finish_clips", [loss_0, far_loss, got_loss], consts, vhat, vinv, dv0, [got_x, got_z], ([], [])
    )
    return clip_loss.reshape(rows), gv, gc


def solution(mesh):
    return jax.shard_map(
        shards,
        mesh=mesh,
        in_specs=(P(("row", "col"), None), P(("col", "row"), None), P(), P(), P()),
        out_specs=(P(("row", "col")), P(("row", "col"), None), P(("col", "row"), None)),
        check_vma=False,
    )
```

```python
import jax
import jax.numpy as jnp
from jax import lax
from jax.experimental import pallas as pl
from jax.experimental.pallas import tpu as pltpu
from jax.sharding import PartitionSpec as P

F32, BF16 = jnp.float32, jnp.bfloat16
MIB = 1024 * 1024
CHUNK = 256
PARTS = 4
LONG = 10**10
SPECS = {
    "s": pl.BlockSpec(memory_space=pltpu.SMEM),
    "v": pl.BlockSpec(memory_space=pltpu.VMEM),
    "h": pl.BlockSpec(memory_space=pl.ANY),
}


def vm(shape, dtype=BF16):
    return pltpu.VMEM(shape, dtype)


def call(name, kernel, out_shape, args, spec="v", out_spec="v", limit=4, flops=0, scratch=(), aliases={}):
    space = {"v": pltpu.VMEM, "h": pltpu.HBM}
    if spec in space:
        args = [pltpu.with_memory_space_constraint(a, space[spec]) for a in args]
    return pl.pallas_call(
        kernel,
        name=name,
        out_shape=out_shape,
        in_specs=[SPECS[spec]] * len(args),
        out_specs=[SPECS[s] for s in (out_spec if len(out_spec) > 1 else out_spec * len(out_shape))],
        scratch_shapes=list(scratch),
        input_output_aliases=aliases,
        compiler_params=pltpu.CompilerParams(vmem_limit_bytes=limit * MIB),
        cost_estimate=pl.CostEstimate(flops=flops, bytes_accessed=0, transcendentals=0),
    )(*args)


def hand_on(name, block, *after, flops=0):
    return call(
        name, lambda *refs: None, [vm(block.shape, block.dtype)], [block, *after],
        aliases={0: 0}, flops=flops,
    )[0]


def unit_rows(rows):
    inverse = lax.rsqrt(jnp.sum(rows * rows, axis=1, keepdims=True) + 1e-06)
    return rows * inverse, inverse


def dot_nt(a, b):
    return lax.dot_general(a, b, (((1,), (1,)), ((), ())), preferred_element_type=F32)


def dot_tn(a, b):
    return lax.dot_general(a, b, (((0,), (0,)), ((), ())), preferred_element_type=F32)


def dot_nn(a, b):
    return jnp.dot(a, b, preferred_element_type=F32)


def log1p_sum(e):
    rows = e.shape[0]
    u = e
    for _ in range(3):
        rows //= 2
        a, b = u[:rows], u[rows:]
        u = a + b + a * b
    series = u * (1.0 - u * (0.5 - u * (1.0 / 3.0 - u * 0.25)))
    logs = jnp.where(u < 0.01, series, jnp.log(1.0 + u))
    return jnp.sum(logs, axis=0, keepdims=True)


def pairs(dots, scale, shift, base, labels, counted):
    logits = dots * scale + shift
    match = lax.broadcasted_iota(jnp.int32, logits.shape, 0) == labels - base
    e = jnp.exp(-jnp.abs(logits))
    whole = 1.0 + e
    over = pl.reciprocal(whole, approx=True)
    over = over * (2.0 - whole * over)
    sigmoid = jnp.where(logits >= 0.0, over, e * over)
    coef = (sigmoid - jnp.where(match, 1.0, 0.0)).astype(BF16)
    if not counted:
        return coef, None
    e, logits, match = e[:, :counted], logits[:, :counted], match[:, :counted]
    linear = jnp.maximum(jnp.where(match, -logits, logits), 0.0)
    return coef, jnp.sum(linear, axis=0, keepdims=True) + log1p_sum(e)


def stack(target, blocks):
    at = 0
    for b in blocks:
        target[pl.ds(at, b.shape[0]), :] = b[...]
        at += b.shape[0]


def shards(film, text, matched, sharpness, offset):
    rows, width = film.shape
    half = rows // 2
    R, C = lax.axis_size("row"), lax.axis_size("col")
    Y, Z = R // 2, C // 4
    mat, hmat = (rows, width), (half, width)
    limit = 6 + 2 * (Y * Z * 2 * rows) // 1024

    def swap(value, axis, bits):
        size = lax.axis_size(axis)
        return lax.ppermute(value, axis, [(i, i ^ bits) for i in range(size)])

    def first_caption(s, t, k):
        r, c = lax.axis_index("row"), lax.axis_index("col")
        return ((c ^ (4 * s + k)) * R + (r ^ (2 * t))) * rows

    def clip_index(x, z, k):
        r, c = lax.axis_index("row"), lax.axis_index("col")
        return (r ^ x) * C + (c ^ (2 * z + k))

    near = [(0, t) for t in range(Y)]
    up = [(s, 0) for s in range(1, Z)]
    diag = [(s, t) for s in range(1, Z) for t in range(1, Y)]
    clip_order = [(x, z, k) for k in range(2) for z in range(2) for x in range(2)]
    nn, na, nd = len(near) * rows, len(near + up) * rows, len(diag) * rows
    n1, n3, n4, n7 = rows, 3 * rows, 4 * rows, 7 * rows

    def strip(consts, blocks, k, captions, clips, labels, counted, put):
        scale, shift = consts[0:1, 0:1], consts[1:2, 0:1]
        dots = dot_nt(captions, clips)
        total = 0.0
        for i, (s, t) in enumerate(blocks):
            block = dots[i * rows : (i + 1) * rows]
            coef, add = pairs(block, scale, shift, first_caption(s, t, k), labels, counted)
            put(i * rows, coef)
            total = total + add if counted else None
        return total

    def put_in(target, first=0, left=0):
        def put(at, coef):
            target[pl.ds(first + at, coef.shape[0]), pl.ds(left, coef.shape[1])] = coef
        return put

    def normalize_kernel(film, text, matched, v16, c16, va, vb, vhat, chat, vinv, cinv, labels, fbuf, tbuf, mbuf, sems):
        step = rows // PARTS
        get_matched = pltpu.make_async_copy(matched, mbuf, sems.at[2 * PARTS])
        copies = []
        for j, (src, buf) in enumerate(((film, fbuf), (text, tbuf))):
            for i in range(PARTS):
                part = pl.ds(i * step, step)
                copies.append(pltpu.make_async_copy(src.at[part], buf.at[part], sems.at[j * PARTS + i]))
        for copy in copies:
            copy.start()
        get_matched.start()
        for copy in copies[:PARTS]:
            copy.wait()
        hat, inverse = unit_rows(fbuf[...])
        vhat[...], vinv[...], v16[...] = hat, inverse, hat.astype(BF16)
        va[...] = hat[:half].astype(BF16)
        vb[...] = hat[half:].astype(BF16)
        for copy in copies[PARTS:]:
            copy.wait()
        hat, inverse = unit_rows(tbuf[...])
        chat[...], cinv[...], c16[...] = hat, inverse, hat.astype(BF16)
        get_matched.wait()
        labels[...] = jnp.concatenate(
            [mbuf[pl.ds(clip_index(*p), 1), :] for p in clip_order], axis=1
        )

    matched = matched.reshape(-1, rows)
    v16, c16, va, vb, vhat, chat, vinv, cinv, labels = call(
        "normalize", normalize_kernel,
        [vm(mat), vm(mat)] + [vm(hmat)] * 2 + [vm(mat, F32), vm(mat, F32), vm((rows, 1), F32), vm((rows, 1), F32),
         vm((1, 8 * rows), jnp.int32)],
        [film, text, matched], spec="h", limit=8,
        scratch=[pltpu.VMEM(mat, F32)] * 2
        + [pltpu.VMEM(matched.shape, jnp.int32), pltpu.SemaphoreType.DMA((2 * PARTS + 1,))],
    )

    def consts_kernel(scale, shift, out):
        out[0:1, :] = jnp.full((1, 128), scale[0], F32)
        out[1:2, :] = jnp.full((1, 128), shift[0], F32)

    (consts,) = call("consts", consts_kernel, [vm((2, 128), F32)], [sharpness, offset], spec="s")

    def join(name, *blocks):
        def join_kernel(*refs):
            stack(refs[-1], refs[:-1])

        return call(name, join_kernel, [vm((sum(b.shape[0] for b in blocks), width))], blocks)[0]

    v_z = [hand_on("clips_z", swap(b, "col", 2), flops=n * LONG // 4) for b, n in ((va, 4), (vb, 24))]
    c_z = [hand_on("captions_z", swap(c16, "col", 4 * s), consts, flops=4 * LONG // 4) for s in range(1, Z)]
    c_y = [swap(c16, "row", 2 * t) for t in range(1, Y)]
    v_x = swap(v16, "row", 1)
    v_d = [hand_on("clips_d", swap(b, "row", 1), flops=2 * LONG // 4) for b in v_z]
    c_d = [swap(b, "row", 2 * t) for b in c_z for t in range(1, Y)]
    N = join("near_blocks", c16, *c_y, v16, v_x, *v_z)
    N_k = hand_on("near_other", swap(N, "col", 1), flops=4 * LONG // 4)
    cz_k = [swap(b, "col", 1) for b in c_z]
    v_d = join("diagonal_clips", *v_d)
    vd_k = swap(v_d, "col", 1)

    def early_kernel(consts, labels, N, N_k, *refs):
        n = len(up)
        cz, czk, (S1, p, q, loss) = refs[:n], refs[n : 2 * n], refs[2 * n :]
        stack(S1, [N.at[:nn], *cz, N_k.at[:nn], *czk])
        own = N[nn:, :]
        loss[...] = strip(
            consts, near + up, 0, S1[:na, :], own, labels[:, :n3], n3, put_in(p)
        ) + strip(consts, near + up, 1, S1[na:, :], own, labels[:, :n3], n3, put_in(q))
        strip(
            consts, near + up, 0, S1[:na, :], N_k[nn:, :], labels[:, n4:n7], 0, put_in(p, left=n3)
        )

    S1, p, q, loss_a = call(
        "early_pairs", early_kernel,
        [vm((2 * na, width)), vm((na, 2 * n3)), vm((na, n3)), vm((1, n3), F32)],
        [consts, labels, N, N_k, *c_z, *cz_k],
        flops=2 * 27 * rows * rows * width, limit=limit,
    )

    def middle_kernel(consts, labels, N, N_k, vd, vdk, S1, p, q, VV, G1, coef, loss):
        stack(VV, [N.at[nn:], vd, N_k.at[nn:], vdk])
        coef[:, :n3] = p[:, :n3]
        coef[:, n4:n7] = p[:, n3:]
        G1[na:, :n3] = q[...]
        late = labels[:, n3:n4]
        loss[...] = strip(
            consts, near + up, 0, S1[:na, :], vd[...], late, n1, put_in(coef, left=n3)
        ) + strip(consts, near + up, 1, S1[na:, :], vd[...], late, n1, put_in(G1, na, n3))
        strip(consts, near + up, 0, S1[:na, :], vdk[...], labels[:, n7:], 0, put_in(coef, left=n7))
        G1[:na, :] = coef[:, :n4]

    VV, G1, coef_a, loss_m = call(
        "middle_pairs", middle_kernel,
        [vm((8 * n1, width)), vm((2 * na, n4)), vm((na, 8 * n1)), vm((1, n1), F32)],
        [consts, labels, N, N_k, v_d, vd_k, S1, p, q],
        flops=2 * 9 * rows * rows * width, limit=limit,
    )
    c_d = [hand_on("captions_d", b, loss_m, flops=3 * LONG) for b in c_d]
    D_k = [swap(b, "col", 1) for b in c_d]

    def far_captions_kernel(consts, labels, VV, *refs):
        n = len(diag)
        caps, (loss, p, *sums, D, coef) = refs[:n], refs[n:]
        stack(D, caps)
        loss[...] = strip(consts, diag, 0, D[...], VV[...], labels[...], n4, put_in(coef))
        p[...] = coef[:, :n4]
        for i in range(width // CHUNK):
            cols = pl.ds(i * CHUNK, CHUNK)
            part = dot_nn(coef[...], VV[:, cols])
            for j, ref in enumerate(sums):
                ref[:, cols] = part[j * half : (j + 1) * half].astype(BF16)

    loss_c, p_d, *dcd = call(
        "far_captions", far_captions_kernel,
        [vm((1, n4), F32), vm((nd, n4))] + [vm(hmat)] * (2 * len(diag)),
        [consts, labels, VV, *c_d],
        flops=2 * 16 * rows * rows * width, limit=limit,
        scratch=[pltpu.VMEM((nd, width), BF16), pltpu.VMEM((nd, 8 * n1), BF16)],
    )

    def far_clips_kernel(consts, labels, VV, S1, G1, p_d, *refs):
        n = len(diag)
        caps, (S2, G2, loss, dv) = refs[: 2 * n], refs[2 * n :]
        stack(S2, caps)
        G2[:nd, :] = p_d[...]
        loss[...] = strip(consts, diag, 1, S2[nd:, :], VV[:n4, :], labels[:, :n4], n4, put_in(G2, nd))
        for i in range(width // CHUNK):
            cols = pl.ds(i * CHUNK, CHUNK)
            dv[:, cols] = (dot_tn(G1[:, n3:], S1[:, cols]) + dot_tn(G2[:, n3:], S2[:, cols])).astype(BF16)

    S2, G2, loss_d, dv_d = call(
        "far_clips", far_clips_kernel,
        [vm((2 * nd, width)), vm((2 * nd, n4)), vm((1, n4), F32), vm(mat)],
        [consts, labels, VV, S1, G1, p_d, *c_d, *D_k],
        flops=2 * 12 * rows * rows * width, limit=limit,
    )
    far_v = swap(dv_d, "row", 1)

    def near_captions_kernel(coef, VV, after, dc0, *refs):
        dcy, dcz = refs[: Y - 1], refs[Y - 1 :]
        for i in range(width // CHUNK):
            cols = pl.ds(i * CHUNK, CHUNK)
            part = dot_nn(coef[...], VV[:, cols])
            for j, ref in enumerate((dc0, *dcy)):
                ref[:, cols] = part[j * rows : (j + 1) * rows].astype(ref.dtype)
            for j, ref in enumerate(dcz):
                ref[:, cols] = part[nn + j * half : nn + (j + 1) * half]

    dc0, *dcs = call(
        "near_captions", near_captions_kernel,
        [vm(mat, F32)] + [vm(mat)] * (Y - 1) + [vm(hmat, F32)] * (2 * (Z - 1)),
        [coef_a, VV, dv_d],
        flops=2 * 24 * rows * rows * width, limit=limit,
    )
    dcy, dcz = dcs[: Y - 1], dcs[Y - 1 :]

    def add_kernel(*refs):
        total = refs[0][...].astype(F32)
        for ref in refs[1:-1]:
            total += ref[...].astype(F32)
        refs[-1][...] = total.astype(BF16)

    def add(name, *terms):
        return call(name, add_kernel, [vm(terms[0].shape)], terms)[0]

    def captions_back(h, *after):
        sums = []
        for s in range(Z - 1):
            far = [
                hand_on("far_" + "ab"[h], swap(dcd[2 * (s * (Y - 1) + t - 1) + h], "row", 2 * t), *after, flops=(4, 0)[h] * LONG // 4)
                for t in range(1, Y)
            ]
            sums.append(add("add_" + "ab"[h], dcz[2 * s + h], *far))
        return sums, [swap(sums[s], "col", 4 * (s + 1)) for s in range(Z - 1)]

    sums_a, got_a = captions_back(0, dc0)
    dcd = [hand_on("far_b", b, dv_d) if i % 2 else b for i, b in enumerate(dcd)]
    def near_clips_kernel(S1, S2, G1, G2, after, dv0, dvx, dvz):
        for i in range(width // CHUNK):
            cols = pl.ds(i * CHUNK, CHUNK)
            part = dot_tn(G1[:, :n3], S1[:, cols]) + dot_tn(G2[:, :n3], S2[:, cols])
            for j, ref in enumerate((dv0, dvx, dvz)):
                ref[:, cols] = part[j * rows : (j + 1) * rows].astype(ref.dtype)

    dv0, dvx, dvz = call(
        "near_clips", near_clips_kernel, [vm(mat, F32), vm(mat), vm(mat, F32)], [S1, S2, G1, G2, sums_a[0]],
        flops=2 * 24 * rows * rows * width, limit=limit,
    )

    sums_b, got_b = captions_back(1, dvz)
    sum_v = add("add_clips", dvz, far_v)
    got_z = swap(sum_v, "col", 2)
    got_h = [[hand_on("captions_back", b, sum_v, flops=3 * LONG) for b in got] for got in (got_a, got_b)]
    dcy = [hand_on("near_y", b, sum_v) for b in dcy]
    dvx = hand_on("near_x", dvx, sum_v)
    got_y = [hand_on("captions_y", swap(dcy[t - 1], "row", 2 * t), sum_v, flops=LONG) for t in range(1, Y)]
    got_x = hand_on("clips_x", swap(dvx, "row", 1), sum_v, flops=4 * LONG)

    def losses_kernel(l_a, l_m, l_c, l_d, after, *refs):
        loss_0, loss_x, loss_z = refs[-3:]
        total = l_c[...] + l_d[...]
        own = total[:, :n3] + l_a[...]
        loss_0[...] = own[:, :n1]
        loss_x[0:1, :] = own[:, n1 : 2 * n1]
        loss_x[1:2, :] = total[:, n3:] + l_m[...]
        loss_z[...] = own[:, 2 * n1 :]

    def add_loss_kernel(loss_z, arrived, got, sum_v, out):
        out[...] = loss_z[...] + arrived[1:2, :]

    loss_0, loss_x, loss_z = call(
        "losses", losses_kernel, [vm((1, n1), F32), vm((2, n1), F32), vm((1, n1), F32)],
        [loss_a, loss_m, loss_c, loss_d, sums_a[0]],
    )
    far_loss = hand_on("losses_x", swap(loss_x, "row", 1), *sums_b)
    (sum_loss,) = call("add_loss", add_loss_kernel, [vm((1, n1), F32)], [loss_z, far_loss, got_b[0], sum_v])
    got_loss = swap(sum_loss, "col", 2)

    def finish(name, losses, consts, hat, inverse, own, whole, halves, *after):
        tail = 3 + bool(losses)

        def finish_kernel(consts, hat_ref, inverse_ref, *refs):
            adds, (grad, *loss, buf, sems) = refs[: -1 - tail - len(after)], refs[-1 - tail :]
            copies = []
            if not losses:
                loss[0][...] = jnp.zeros((8, 128), F32)
            if losses:
                out, lbuf = loss
                loss_0, far_loss, got_loss = adds[:3]
                lbuf[...] = loss_0[...] + far_loss[0:1, :] + got_loss[...]
                copies.append(pltpu.make_async_copy(lbuf, out, sems.at[2]))
                copies[-1].start()
            adds = adds[len(losses) :]
            for i in range(2):
                part = pl.ds(i * half, half)
                total = adds[0][part, :]
                for ref in adds[1 : 1 + len(whole)]:
                    total += ref[part, :].astype(F32)
                for ref in adds[1 + len(whole) :][i * len(halves[0]) : (i + 1) * len(halves[0])]:
                    total += ref[...].astype(F32)
                total = total * consts[0:1, 0:1]
                hat = hat_ref[part, :]
                along = jnp.sum(hat * total, axis=1, keepdims=True)
                buf[part, :] = inverse_ref[part, :] * (total - hat * along)
                copies.append(pltpu.make_async_copy(buf.at[part], grad.at[part], sems.at[i]))
                copies[-1].start()
            for copy in copies:
                copy.wait()

        return call(
            name, finish_kernel,
            [jax.ShapeDtypeStruct(mat, F32)]
            + ([jax.ShapeDtypeStruct((1, rows), F32)] if losses else [vm((8, 128), F32)]),
            [consts, hat, inverse, *losses, own, *whole, *halves[0], *halves[1], *after], out_spec="hh" if losses else "hv",
            scratch=[pltpu.VMEM((1, rows), F32)] * bool(losses)
            + [pltpu.VMEM(mat, F32), pltpu.SemaphoreType.DMA((3,))],
        )

    gc, done = finish("finish_captions", [], consts, chat, cinv, dc0, got_y, got_h, sum_loss)
    got_z = hand_on("clips_back", got_z, done, flops=3 * LONG)
    gv, clip_loss = finish(
        "finish_clips", [loss_0, far_loss, got_loss], consts, vhat, vinv, dv0, [got_x, got_z], ([], [])
    )
    return clip_loss.reshape(rows), gv, gc


def solution(mesh):
    return jax.shard_map(
        shards,
        mesh=mesh,
        in_specs=(P(("row", "col"), None), P(("col", "row"), None), P(), P(), P()),
        out_specs=(P(("row", "col")), P(("row", "col"), None), P(("col", "row"), None)),
        check_vma=False,
    )
```

```python
import jax
import jax.numpy as jnp
from jax import lax
from jax.experimental import pallas as pl
from jax.experimental.pallas import tpu as pltpu
from jax.sharding import PartitionSpec as P

F32, BF16 = jnp.float32, jnp.bfloat16
MIB = 1024 * 1024
CHUNK = 256
PARTS = 4
LONG = 10**10
SPECS = {
    "s": pl.BlockSpec(memory_space=pltpu.SMEM),
    "v": pl.BlockSpec(memory_space=pltpu.VMEM),
    "h": pl.BlockSpec(memory_space=pl.ANY),
}


def vm(shape, dtype=BF16):
    return pltpu.VMEM(shape, dtype)


def call(name, kernel, out_shape, args, spec="v", out_spec="v", limit=4, flops=0, scratch=(), aliases={}):
    space = {"v": pltpu.VMEM, "h": pltpu.HBM}
    if spec in space:
        args = [pltpu.with_memory_space_constraint(a, space[spec]) for a in args]
    return pl.pallas_call(
        kernel,
        name=name,
        out_shape=out_shape,
        in_specs=[SPECS[spec]] * len(args),
        out_specs=[SPECS[s] for s in (out_spec if len(out_spec) > 1 else out_spec * len(out_shape))],
        scratch_shapes=list(scratch),
        input_output_aliases=aliases,
        compiler_params=pltpu.CompilerParams(vmem_limit_bytes=limit * MIB),
        cost_estimate=pl.CostEstimate(flops=flops, bytes_accessed=0, transcendentals=0),
    )(*args)


def hand_on(name, block, *after, flops=0):
    return call(
        name, lambda *refs: None, [vm(block.shape, block.dtype)], [block, *after],
        aliases={0: 0}, flops=flops,
    )[0]


def unit_rows(rows):
    inverse = lax.rsqrt(jnp.sum(rows * rows, axis=1, keepdims=True) + 1e-06)
    return rows * inverse, inverse


def dot_nt(a, b):
    return lax.dot_general(a, b, (((1,), (1,)), ((), ())), preferred_element_type=F32)


def dot_tn(a, b):
    return lax.dot_general(a, b, (((0,), (0,)), ((), ())), preferred_element_type=F32)


def dot_nn(a, b):
    return jnp.dot(a, b, preferred_element_type=F32)


def log1p_sum(e):
    rows = e.shape[0]
    u = e
    for _ in range(3):
        rows //= 2
        a, b = u[:rows], u[rows:]
        u = a + b + a * b
    series = u * (1.0 - u * (0.5 - u * (1.0 / 3.0 - u * 0.25)))
    logs = jnp.where(u < 0.01, series, jnp.log(1.0 + u))
    return jnp.sum(logs, axis=0, keepdims=True)


def pairs(dots, scale, shift, base, labels, counted):
    logits = dots * scale + shift
    match = lax.broadcasted_iota(jnp.int32, logits.shape, 0) == labels - base
    e = jnp.exp(-jnp.abs(logits))
    whole = 1.0 + e
    over = pl.reciprocal(whole, approx=True)
    over = over * (2.0 - whole * over)
    sigmoid = jnp.where(logits >= 0.0, over, e * over)
    coef = (sigmoid - jnp.where(match, 1.0, 0.0)).astype(BF16)
    if not counted:
        return coef, None
    e, logits, match = e[:, :counted], logits[:, :counted], match[:, :counted]
    linear = jnp.maximum(jnp.where(match, -logits, logits), 0.0)
    return coef, jnp.sum(linear, axis=0, keepdims=True) + log1p_sum(e)


def stack(target, blocks):
    at = 0
    for b in blocks:
        target[pl.ds(at, b.shape[0]), :] = b[...]
        at += b.shape[0]


def shards(film, text, matched, sharpness, offset):
    rows, width = film.shape
    half = rows // 2
    R, C = lax.axis_size("row"), lax.axis_size("col")
    Y, Z = R // 2, C // 4
    mat, hmat = (rows, width), (half, width)
    limit = 6 + 2 * (Y * Z * 2 * rows) // 1024

    def swap(value, axis, bits):
        size = lax.axis_size(axis)
        return lax.ppermute(value, axis, [(i, i ^ bits) for i in range(size)])

    def first_caption(s, t, k):
        r, c = lax.axis_index("row"), lax.axis_index("col")
        return ((c ^ (4 * s + k)) * R + (r ^ (2 * t))) * rows

    def clip_index(x, z, k):
        r, c = lax.axis_index("row"), lax.axis_index("col")
        return (r ^ x) * C + (c ^ (2 * z + k))

    near = [(0, t) for t in range(Y)]
    up = [(s, 0) for s in range(1, Z)]
    diag = [(s, t) for s in range(1, Z) for t in range(1, Y)]
    clip_order = [(x, z, k) for k in range(2) for z in range(2) for x in range(2)]
    nn, na, nd = len(near) * rows, len(near + up) * rows, len(diag) * rows
    n1, n3, n4, n7 = rows, 3 * rows, 4 * rows, 7 * rows

    def strip(consts, blocks, k, captions, clips, labels, counted, put):
        scale, shift = consts[0:1, 0:1], consts[1:2, 0:1]
        dots = dot_nt(captions, clips)
        total = 0.0
        for i, (s, t) in enumerate(blocks):
            block = dots[i * rows : (i + 1) * rows]
            coef, add = pairs(block, scale, shift, first_caption(s, t, k), labels, counted)
            put(i * rows, coef)
            total = total + add if counted else None
        return total

    def put_in(target, first=0, left=0):
        def put(at, coef):
            target[pl.ds(first + at, coef.shape[0]), pl.ds(left, coef.shape[1])] = coef
        return put

    def normalize_kernel(film, text, matched, v16, c16, va, vb, vhat, chat, vinv, cinv, labels, fbuf, tbuf, mbuf, sems):
        step = rows // PARTS
        get_matched = pltpu.make_async_copy(matched, mbuf, sems.at[2 * PARTS])
        copies = []
        for j, (src, buf) in enumerate(((film, fbuf), (text, tbuf))):
            for i in range(PARTS):
                part = pl.ds(i * step, step)
                copies.append(pltpu.make_async_copy(src.at[part], buf.at[part], sems.at[j * PARTS + i]))
        for copy in copies:
            copy.start()
        get_matched.start()
        for copy in copies[:PARTS]:
            copy.wait()
        hat, inverse = unit_rows(fbuf[...])
        vhat[...], vinv[...], v16[...] = hat, inverse, hat.astype(BF16)
        va[...] = hat[:half].astype(BF16)
        vb[...] = hat[half:].astype(BF16)
        for copy in copies[PARTS:]:
            copy.wait()
        hat, inverse = unit_rows(tbuf[...])
        chat[...], cinv[...], c16[...] = hat, inverse, hat.astype(BF16)
        get_matched.wait()
        labels[...] = jnp.concatenate(
            [mbuf[pl.ds(clip_index(*p), 1), :] for p in clip_order], axis=1
        )

    matched = matched.reshape(-1, rows)
    v16, c16, va, vb, vhat, chat, vinv, cinv, labels = call(
        "normalize", normalize_kernel,
        [vm(mat), vm(mat)] + [vm(hmat)] * 2 + [vm(mat, F32), vm(mat, F32), vm((rows, 1), F32), vm((rows, 1), F32),
         vm((1, 8 * rows), jnp.int32)],
        [film, text, matched], spec="h", limit=8,
        scratch=[pltpu.VMEM(mat, F32)] * 2
        + [pltpu.VMEM(matched.shape, jnp.int32), pltpu.SemaphoreType.DMA((2 * PARTS + 1,))],
    )

    def consts_kernel(scale, shift, out):
        out[0:1, :] = jnp.full((1, 128), scale[0], F32)
        out[1:2, :] = jnp.full((1, 128), shift[0], F32)

    (consts,) = call("consts", consts_kernel, [vm((2, 128), F32)], [sharpness, offset], spec="s")

    def join(name, *blocks):
        def join_kernel(*refs):
            stack(refs[-1], refs[:-1])

        return call(name, join_kernel, [vm((sum(b.shape[0] for b in blocks), width))], blocks)[0]

    v_z = [hand_on("clips_z", swap(b, "col", 2), flops=n * LONG // 4) for b, n in ((va, 4), (vb, 24))]
    c_z = [hand_on("captions_z", swap(c16, "col", 4 * s), consts, flops=4 * LONG // 4) for s in range(1, Z)]
    c_y = [swap(c16, "row", 2 * t) for t in range(1, Y)]
    v_x = swap(v16, "row", 1)
    v_d = [hand_on("clips_d", swap(b, "row", 1), flops=LONG) for b in v_z]
    c_d = [swap(b, "row", 2 * t) for b in c_z for t in range(1, Y)]
    N = join("near_blocks", c16, *c_y, *c_z, v16, v_x, *v_z)
    N_k = hand_on("near_other", swap(N, "col", 1), flops=4 * LONG // 4)
    v_d = join("diagonal_clips", *v_d)
    vd_k = swap(v_d, "col", 1)

    def early_kernel(consts, labels, N, N_k, S1, p, q, loss):
        stack(S1, [N.at[:na], N_k.at[:na]])
        own = N[na:, :]
        loss[...] = strip(
            consts, near + up, 0, S1[:na, :], own, labels[:, :n3], n3, put_in(p)
        ) + strip(consts, near + up, 1, S1[na:, :], own, labels[:, :n3], n3, put_in(q))
        strip(
            consts, near + up, 0, S1[:na, :], N_k[na:, :], labels[:, n4:n7], 0, put_in(p, left=n3)
        )

    S1, p, q, loss_a = call(
        "early_pairs", early_kernel,
        [vm((2 * na, width)), vm((na, 2 * n3)), vm((na, n3)), vm((1, n3), F32)],
        [consts, labels, N, N_k],
        flops=2 * 27 * rows * rows * width, limit=limit,
    )

    def middle_kernel(consts, labels, N, N_k, vd, vdk, S1, p, q, VV, G1, coef, loss):
        stack(VV, [N.at[na:], vd, N_k.at[na:], vdk])
        coef[:, :n3] = p[:, :n3]
        coef[:, n4:n7] = p[:, n3:]
        G1[na:, :n3] = q[...]
        late = labels[:, n3:n4]
        loss[...] = strip(
            consts, near + up, 0, S1[:na, :], vd[...], late, n1, put_in(coef, left=n3)
        ) + strip(consts, near + up, 1, S1[na:, :], vd[...], late, n1, put_in(G1, na, n3))
        strip(consts, near + up, 0, S1[:na, :], vdk[...], labels[:, n7:], 0, put_in(coef, left=n7))
        G1[:na, :] = coef[:, :n4]

    VV, G1, coef_a, loss_m = call(
        "middle_pairs", middle_kernel,
        [vm((8 * n1, width)), vm((2 * na, n4)), vm((na, 8 * n1)), vm((1, n1), F32)],
        [consts, labels, N, N_k, v_d, vd_k, S1, p, q],
        flops=2 * 9 * rows * rows * width, limit=limit,
    )
    c_d = [hand_on("captions_d", b, loss_m, flops=3 * LONG) for b in c_d]
    D_k = [swap(b, "col", 1) for b in c_d]

    def far_captions_kernel(consts, labels, VV, *refs):
        n = len(diag)
        caps, (loss, p, *sums, D, coef) = refs[:n], refs[n:]
        stack(D, caps)
        loss[...] = strip(consts, diag, 0, D[...], VV[...], labels[...], n4, put_in(coef))
        p[...] = coef[:, :n4]
        for i in range(width // CHUNK):
            cols = pl.ds(i * CHUNK, CHUNK)
            part = dot_nn(coef[...], VV[:, cols])
            for j, ref in enumerate(sums):
                ref[:, cols] = part[j * half : (j + 1) * half].astype(BF16)

    loss_c, p_d, *dcd = call(
        "far_captions", far_captions_kernel,
        [vm((1, n4), F32), vm((nd, n4))] + [vm(hmat)] * (2 * len(diag)),
        [consts, labels, VV, *c_d],
        flops=2 * 16 * rows * rows * width, limit=limit,
        scratch=[pltpu.VMEM((nd, width), BF16), pltpu.VMEM((nd, 8 * n1), BF16)],
    )

    def far_clips_kernel(consts, labels, VV, S1, G1, p_d, *refs):
        n = len(diag)
        caps, (S2, G2, loss, dv) = refs[: 2 * n], refs[2 * n :]
        stack(S2, caps)
        G2[:nd, :] = p_d[...]
        loss[...] = strip(consts, diag, 1, S2[nd:, :], VV[:n4, :], labels[:, :n4], n4, put_in(G2, nd))
        for i in range(width // CHUNK):
            cols = pl.ds(i * CHUNK, CHUNK)
            dv[:, cols] = (dot_tn(G1[:, n3:], S1[:, cols]) + dot_tn(G2[:, n3:], S2[:, cols])).astype(BF16)

    S2, G2, loss_d, dv_d = call(
        "far_clips", far_clips_kernel,
        [vm((2 * nd, width)), vm((2 * nd, n4)), vm((1, n4), F32), vm(mat)],
        [consts, labels, VV, S1, G1, p_d, *c_d, *D_k],
        flops=2 * 12 * rows * rows * width, limit=limit,
    )
    far_v = swap(dv_d, "row", 1)

    def near_captions_kernel(coef, VV, after, dc0, *refs):
        dcy, dcz = refs[: Y - 1], refs[Y - 1 :]
        for i in range(width // CHUNK):
            cols = pl.ds(i * CHUNK, CHUNK)
            part = dot_nn(coef[...], VV[:, cols])
            for j, ref in enumerate((dc0, *dcy)):
                ref[:, cols] = part[j * rows : (j + 1) * rows].astype(ref.dtype)
            for j, ref in enumerate(dcz):
                ref[:, cols] = part[nn + j * half : nn + (j + 1) * half]

    dc0, *dcs = call(
        "near_captions", near_captions_kernel,
        [vm(mat, F32)] + [vm(mat)] * (Y - 1) + [vm(hmat, F32)] * (2 * (Z - 1)),
        [coef_a, VV, dv_d],
        flops=2 * 24 * rows * rows * width, limit=limit,
    )
    dcy, dcz = dcs[: Y - 1], dcs[Y - 1 :]

    def add_kernel(*refs):
        total = refs[0][...].astype(F32)
        for ref in refs[1:-1]:
            total += ref[...].astype(F32)
        refs[-1][...] = total.astype(BF16)

    def add(name, *terms):
        return call(name, add_kernel, [vm(terms[0].shape)], terms)[0]

    def captions_back(h, *after):
        sums = []
        for s in range(Z - 1):
            far = [
                hand_on("far_" + "ab"[h], swap(dcd[2 * (s * (Y - 1) + t - 1) + h], "row", 2 * t), *after, flops=(4, 0)[h] * LONG // 4)
                for t in range(1, Y)
            ]
            sums.append(add("add_" + "ab"[h], dcz[2 * s + h], *far))
        return sums, [swap(sums[s], "col", 4 * (s + 1)) for s in range(Z - 1)]

    sums_a, got_a = captions_back(0, dc0)
    dcd = [hand_on("far_b", b, dv_d) if i % 2 else b for i, b in enumerate(dcd)]
    def near_clips_kernel(S1, S2, G1, G2, after, dv0, dvx, dvz):
        for i in range(width // CHUNK):
            cols = pl.ds(i * CHUNK, CHUNK)
            part = dot_tn(G1[:, :n3], S1[:, cols]) + dot_tn(G2[:, :n3], S2[:, cols])
            for j, ref in enumerate((dv0, dvx, dvz)):
                ref[:, cols] = part[j * rows : (j + 1) * rows].astype(ref.dtype)

    dv0, dvx, dvz = call(
        "near_clips", near_clips_kernel, [vm(mat, F32), vm(mat), vm(mat, F32)], [S1, S2, G1, G2, sums_a[0]],
        flops=2 * 24 * rows * rows * width, limit=limit,
    )

    sums_b, got_b = captions_back(1, dvz)
    sum_v = add("add_clips", dvz, far_v)
    got_z = swap(sum_v, "col", 2)
    got_h = [[hand_on("captions_back", b, sum_v, flops=3 * LONG) for b in got] for got in (got_a, got_b)]
    dcy = [hand_on("near_y", b, sum_v) for b in dcy]
    dvx = hand_on("near_x", dvx, sum_v)
    got_y = [hand_on("captions_y", swap(dcy[t - 1], "row", 2 * t), sum_v, flops=LONG) for t in range(1, Y)]
    got_x = hand_on("clips_x", swap(dvx, "row", 1), sum_v, flops=4 * LONG)

    def losses_kernel(l_a, l_m, l_c, l_d, after, *refs):
        loss_0, loss_x, loss_z = refs[-3:]
        total = l_c[...] + l_d[...]
        own = total[:, :n3] + l_a[...]
        loss_0[...] = own[:, :n1]
        loss_x[0:1, :] = own[:, n1 : 2 * n1]
        loss_x[1:2, :] = total[:, n3:] + l_m[...]
        loss_z[...] = own[:, 2 * n1 :]

    def add_loss_kernel(loss_z, arrived, got, sum_v, out):
        out[...] = loss_z[...] + arrived[1:2, :]

    loss_0, loss_x, loss_z = call(
        "losses", losses_kernel, [vm((1, n1), F32), vm((2, n1), F32), vm((1, n1), F32)],
        [loss_a, loss_m, loss_c, loss_d, sums_a[0]],
    )
    far_loss = hand_on("losses_x", swap(loss_x, "row", 1), *sums_b)
    (sum_loss,) = call("add_loss", add_loss_kernel, [vm((1, n1), F32)], [loss_z, far_loss, got_b[0], sum_v])
    got_loss = swap(sum_loss, "col", 2)

    def finish(name, losses, consts, hat, inverse, own, whole, halves, *after):
        tail = 3 + bool(losses)

        def finish_kernel(consts, hat_ref, inverse_ref, *refs):
            adds, (grad, *loss, buf, sems) = refs[: -1 - tail - len(after)], refs[-1 - tail :]
            copies = []
            if not losses:
                loss[0][...] = jnp.zeros((8, 128), F32)
            if losses:
                out, lbuf = loss
                loss_0, far_loss, got_loss = adds[:3]
                lbuf[...] = loss_0[...] + far_loss[0:1, :] + got_loss[...]
                copies.append(pltpu.make_async_copy(lbuf, out, sems.at[2]))
                copies[-1].start()
            adds = adds[len(losses) :]
            for i in range(2):
                part = pl.ds(i * half, half)
                total = adds[0][part, :]
                for ref in adds[1 : 1 + len(whole)]:
                    total += ref[part, :].astype(F32)
                for ref in adds[1 + len(whole) :][i * len(halves[0]) : (i + 1) * len(halves[0])]:
                    total += ref[...].astype(F32)
                total = total * consts[0:1, 0:1]
                hat = hat_ref[part, :]
                along = jnp.sum(hat * total, axis=1, keepdims=True)
                buf[part, :] = inverse_ref[part, :] * (total - hat * along)
                copies.append(pltpu.make_async_copy(buf.at[part], grad.at[part], sems.at[i]))
                copies[-1].start()
            for copy in copies:
                copy.wait()

        return call(
            name, finish_kernel,
            [jax.ShapeDtypeStruct(mat, F32)]
            + ([jax.ShapeDtypeStruct((1, rows), F32)] if losses else [vm((8, 128), F32)]),
            [consts, hat, inverse, *losses, own, *whole, *halves[0], *halves[1], *after], out_spec="hh" if losses else "hv",
            scratch=[pltpu.VMEM((1, rows), F32)] * bool(losses)
            + [pltpu.VMEM(mat, F32), pltpu.SemaphoreType.DMA((3,))],
        )

    gc, done = finish("finish_captions", [], consts, chat, cinv, dc0, got_y, got_h, sum_loss)
    got_z = hand_on("clips_back", got_z, done, flops=3 * LONG)
    gv, clip_loss = finish(
        "finish_clips", [loss_0, far_loss, got_loss], consts, vhat, vinv, dv0, [got_x, got_z], ([], [])
    )
    return clip_loss.reshape(rows), gv, gc


def solution(mesh):
    return jax.shard_map(
        shards,
        mesh=mesh,
        in_specs=(P(("row", "col"), None), P(("col", "row"), None), P(), P(), P()),
        out_specs=(P(("row", "col")), P(("row", "col"), None), P(("col", "row"), None)),
        check_vma=False,
    )
```

```python
import jax
import jax.numpy as jnp
from jax import lax
from jax.experimental import pallas as pl
from jax.experimental.pallas import tpu as pltpu
from jax.sharding import PartitionSpec as P

F32, BF16 = jnp.float32, jnp.bfloat16
MIB = 1024 * 1024
CHUNK = 256
PARTS = 4
LONG = 10**10
SPECS = {
    "s": pl.BlockSpec(memory_space=pltpu.SMEM),
    "v": pl.BlockSpec(memory_space=pltpu.VMEM),
    "h": pl.BlockSpec(memory_space=pl.ANY),
}


def vm(shape, dtype=BF16):
    return pltpu.VMEM(shape, dtype)


def call(name, kernel, out_shape, args, spec="v", out_spec="v", limit=4, flops=0, scratch=(), aliases={}):
    space = {"v": pltpu.VMEM, "h": pltpu.HBM}
    if spec in space:
        args = [pltpu.with_memory_space_constraint(a, space[spec]) for a in args]
    return pl.pallas_call(
        kernel,
        name=name,
        out_shape=out_shape,
        in_specs=[SPECS[spec]] * len(args),
        out_specs=[SPECS[s] for s in (out_spec if len(out_spec) > 1 else out_spec * len(out_shape))],
        scratch_shapes=list(scratch),
        input_output_aliases=aliases,
        compiler_params=pltpu.CompilerParams(vmem_limit_bytes=limit * MIB),
        cost_estimate=pl.CostEstimate(flops=flops, bytes_accessed=0, transcendentals=0),
    )(*args)


def hand_on(name, block, *after, flops=0):
    return call(
        name, lambda *refs: None, [vm(block.shape, block.dtype)], [block, *after],
        aliases={0: 0}, flops=flops,
    )[0]


def unit_rows(rows):
    inverse = lax.rsqrt(jnp.sum(rows * rows, axis=1, keepdims=True) + 1e-06)
    return rows * inverse, inverse


def dot_nt(a, b):
    return lax.dot_general(a, b, (((1,), (1,)), ((), ())), preferred_element_type=F32)


def dot_tn(a, b):
    return lax.dot_general(a, b, (((0,), (0,)), ((), ())), preferred_element_type=F32)


def dot_nn(a, b):
    return jnp.dot(a, b, preferred_element_type=F32)


def log1p_sum(e):
    rows = e.shape[0]
    u = e
    for _ in range(3):
        rows //= 2
        a, b = u[:rows], u[rows:]
        u = a + b + a * b
    series = u * (1.0 - u * (0.5 - u * (1.0 / 3.0 - u * 0.25)))
    logs = jnp.where(u < 0.01, series, jnp.log(1.0 + u))
    return jnp.sum(logs, axis=0, keepdims=True)


def pairs(dots, scale, shift, base, labels, counted):
    logits = dots * scale + shift
    match = lax.broadcasted_iota(jnp.int32, logits.shape, 0) == labels - base
    e = jnp.exp(-jnp.abs(logits))
    whole = 1.0 + e
    over = pl.reciprocal(whole, approx=True)
    over = over * (2.0 - whole * over)
    sigmoid = jnp.where(logits >= 0.0, over, e * over)
    coef = (sigmoid - jnp.where(match, 1.0, 0.0)).astype(BF16)
    if not counted:
        return coef, None
    e, logits, match = e[:, :counted], logits[:, :counted], match[:, :counted]
    linear = jnp.maximum(jnp.where(match, -logits, logits), 0.0)
    return coef, jnp.sum(linear, axis=0, keepdims=True) + log1p_sum(e)


def stack(target, blocks):
    at = 0
    for b in blocks:
        target[pl.ds(at, b.shape[0]), :] = b[...]
        at += b.shape[0]


def shards(film, text, matched, sharpness, offset):
    rows, width = film.shape
    half = rows // 2
    R, C = lax.axis_size("row"), lax.axis_size("col")
    Y, Z = R // 2, C // 4
    mat, hmat = (rows, width), (half, width)
    limit = 6 + 2 * (Y * Z * 2 * rows) // 1024

    def swap(value, axis, bits):
        size = lax.axis_size(axis)
        return lax.ppermute(value, axis, [(i, i ^ bits) for i in range(size)])

    def first_caption(s, t, k):
        r, c = lax.axis_index("row"), lax.axis_index("col")
        return ((c ^ (4 * s + k)) * R + (r ^ (2 * t))) * rows

    def clip_index(x, z, k):
        r, c = lax.axis_index("row"), lax.axis_index("col")
        return (r ^ x) * C + (c ^ (2 * z + k))

    near = [(0, t) for t in range(Y)]
    up = [(s, 0) for s in range(1, Z)]
    diag = [(s, t) for s in range(1, Z) for t in range(1, Y)]
    clip_order = [(x, z, k) for k in range(2) for z in range(2) for x in range(2)]
    nn, na, nd = len(near) * rows, len(near + up) * rows, len(diag) * rows
    n1, n3, n4, n7 = rows, 3 * rows, 4 * rows, 7 * rows

    def strip(consts, blocks, k, captions, clips, labels, counted, put):
        scale, shift = consts[0:1, 0:1], consts[1:2, 0:1]
        losses = []
        for left in range(0, clips.shape[0], CHUNK):
            right = min(left + CHUNK, clips.shape[0])
            dots = dot_nt(captions, clips[left:right])
            count = max(0, min(counted - left, right - left))
            total = 0.0
            for i, (s, t) in enumerate(blocks):
                block = dots[i * rows : (i + 1) * rows]
                base = first_caption(s, t, k)
                coef, add = pairs(block, scale, shift, base, labels[:, left:right], count)
                put(i * rows, left, coef)
                total = total + add if count else None
            if count:
                losses.append(total)
        return jnp.concatenate(losses, axis=1) if losses else None

    def put_in(target, first=0, left=0):
        def put(at, column, coef):
            target[pl.ds(first + at, coef.shape[0]), pl.ds(left + column, coef.shape[1])] = coef
        return put

    def normalize_kernel(film, text, matched, v16, c16, va, vb, vhat, chat, vinv, cinv, labels, fbuf, tbuf, mbuf, sems):
        step = rows // PARTS
        get_matched = pltpu.make_async_copy(matched, mbuf, sems.at[2 * PARTS])
        copies = []
        for j, (src, buf) in enumerate(((film, fbuf), (text, tbuf))):
            for i in range(PARTS):
                part = pl.ds(i * step, step)
                copies.append(pltpu.make_async_copy(src.at[part], buf.at[part], sems.at[j * PARTS + i]))
        for copy in copies:
            copy.start()
        get_matched.start()
        for copy in copies[:PARTS]:
            copy.wait()
        hat, inverse = unit_rows(fbuf[...])
        vhat[...], vinv[...], v16[...] = hat, inverse, hat.astype(BF16)
        va[...] = hat[:half].astype(BF16)
        vb[...] = hat[half:].astype(BF16)
        for copy in copies[PARTS:]:
            copy.wait()
        hat, inverse = unit_rows(tbuf[...])
        chat[...], cinv[...], c16[...] = hat, inverse, hat.astype(BF16)
        get_matched.wait()
        labels[...] = jnp.concatenate(
            [mbuf[pl.ds(clip_index(*p), 1), :] for p in clip_order], axis=1
        )

    matched = matched.reshape(-1, rows)
    v16, c16, va, vb, vhat, chat, vinv, cinv, labels = call(
        "normalize", normalize_kernel,
        [vm(mat), vm(mat)] + [vm(hmat)] * 2 + [vm(mat, F32), vm(mat, F32), vm((rows, 1), F32), vm((rows, 1), F32),
         vm((1, 8 * rows), jnp.int32)],
        [film, text, matched], spec="h", limit=8,
        scratch=[pltpu.VMEM(mat, F32)] * 2
        + [pltpu.VMEM(matched.shape, jnp.int32), pltpu.SemaphoreType.DMA((2 * PARTS + 1,))],
    )

    def consts_kernel(scale, shift, out):
        out[0:1, :] = jnp.full((1, 128), scale[0], F32)
        out[1:2, :] = jnp.full((1, 128), shift[0], F32)

    (consts,) = call("consts", consts_kernel, [vm((2, 128), F32)], [sharpness, offset], spec="s")

    def join(name, *blocks):
        def join_kernel(*refs):
            stack(refs[-1], refs[:-1])

        return call(name, join_kernel, [vm((sum(b.shape[0] for b in blocks), width))], blocks)[0]

    v_z = [hand_on("clips_z", swap(b, "col", 2), flops=n * LONG // 4) for b, n in ((va, 4), (vb, 24))]
    c_z = [hand_on("captions_z", swap(c16, "col", 4 * s), consts, flops=4 * LONG // 4) for s in range(1, Z)]
    c_y = [swap(c16, "row", 2 * t) for t in range(1, Y)]
    v_x = swap(v16, "row", 1)
    v_d = [hand_on("clips_d", swap(b, "row", 1), flops=2 * LONG // 4) for b in v_z]
    c_d = [swap(b, "row", 2 * t) for b in c_z for t in range(1, Y)]
    N = join("near_blocks", c16, *c_y, v16, v_x, *v_z)
    N_k = hand_on("near_other", swap(N, "col", 1), flops=4 * LONG // 4)
    cz_k = [swap(b, "col", 1) for b in c_z]
    v_d = join("diagonal_clips", *v_d)
    vd_k = swap(v_d, "col", 1)

    def early_kernel(consts, labels, N, N_k, *refs):
        n = len(up)
        cz, czk, (S1, p, q, loss) = refs[:n], refs[n : 2 * n], refs[2 * n :]
        stack(S1, [N.at[:nn], *cz, N_k.at[:nn], *czk])
        own = N[nn:, :]
        loss[...] = strip(
            consts, near + up, 0, S1[:na, :], own, labels[:, :n3], n3, put_in(p)
        ) + strip(consts, near + up, 1, S1[na:, :], own, labels[:, :n3], n3, put_in(q))
        strip(
            consts, near + up, 0, S1[:na, :], N_k[nn:, :], labels[:, n4:n7], 0, put_in(p, left=n3)
        )

    S1, p, q, loss_a = call(
        "early_pairs", early_kernel,
        [vm((2 * na, width)), vm((na, 2 * n3)), vm((na, n3)), vm((1, n3), F32)],
        [consts, labels, N, N_k, *c_z, *cz_k],
        flops=2 * 27 * rows * rows * width, limit=limit,
    )

    def middle_kernel(consts, labels, N, N_k, vd, vdk, S1, p, q, VV, G1, coef, loss):
        stack(VV, [N.at[nn:], vd, N_k.at[nn:], vdk])
        coef[:, :n3] = p[:, :n3]
        coef[:, n4:n7] = p[:, n3:]
        G1[na:, :n3] = q[...]
        late = labels[:, n3:n4]
        loss[...] = strip(
            consts, near + up, 0, S1[:na, :], vd[...], late, n1, put_in(coef, left=n3)
        ) + strip(consts, near + up, 1, S1[na:, :], vd[...], late, n1, put_in(G1, na, n3))
        strip(consts, near + up, 0, S1[:na, :], vdk[...], labels[:, n7:], 0, put_in(coef, left=n7))
        G1[:na, :] = coef[:, :n4]

    VV, G1, coef_a, loss_m = call(
        "middle_pairs", middle_kernel,
        [vm((8 * n1, width)), vm((2 * na, n4)), vm((na, 8 * n1)), vm((1, n1), F32)],
        [consts, labels, N, N_k, v_d, vd_k, S1, p, q],
        flops=2 * 9 * rows * rows * width, limit=limit,
    )
    c_d = [hand_on("captions_d", b, loss_m, flops=3 * LONG) for b in c_d]
    D_k = [swap(b, "col", 1) for b in c_d]

    def far_captions_kernel(consts, labels, VV, *refs):
        n = len(diag)
        caps, (loss, p, *sums, D, coef) = refs[:n], refs[n:]
        stack(D, caps)
        loss[...] = strip(consts, diag, 0, D[...], VV[...], labels[...], n4, put_in(coef))
        p[...] = coef[:, :n4]
        for i in range(width // CHUNK):
            cols = pl.ds(i * CHUNK, CHUNK)
            part = dot_nn(coef[...], VV[:, cols])
            for j, ref in enumerate(sums):
                ref[:, cols] = part[j * half : (j + 1) * half].astype(BF16)

    loss_c, p_d, *dcd = call(
        "far_captions", far_captions_kernel,
        [vm((1, n4), F32), vm((nd, n4))] + [vm(hmat)] * (2 * len(diag)),
        [consts, labels, VV, *c_d],
        flops=2 * 16 * rows * rows * width, limit=limit,
        scratch=[pltpu.VMEM((nd, width), BF16), pltpu.VMEM((nd, 8 * n1), BF16)],
    )

    def far_clips_kernel(consts, labels, VV, S1, G1, p_d, *refs):
        n = len(diag)
        caps, (S2, G2, loss, dv) = refs[: 2 * n], refs[2 * n :]
        stack(S2, caps)
        G2[:nd, :] = p_d[...]
        loss[...] = strip(consts, diag, 1, S2[nd:, :], VV[:n4, :], labels[:, :n4], n4, put_in(G2, nd))
        for i in range(width // CHUNK):
            cols = pl.ds(i * CHUNK, CHUNK)
            dv[:, cols] = (dot_tn(G1[:, n3:], S1[:, cols]) + dot_tn(G2[:, n3:], S2[:, cols])).astype(BF16)

    S2, G2, loss_d, dv_d = call(
        "far_clips", far_clips_kernel,
        [vm((2 * nd, width)), vm((2 * nd, n4)), vm((1, n4), F32), vm(mat)],
        [consts, labels, VV, S1, G1, p_d, *c_d, *D_k],
        flops=2 * 12 * rows * rows * width, limit=limit,
    )
    far_v = swap(dv_d, "row", 1)

    def near_captions_kernel(coef, VV, after, dc0, *refs):
        dcy, dcz = refs[: Y - 1], refs[Y - 1 :]
        for i in range(width // CHUNK):
            cols = pl.ds(i * CHUNK, CHUNK)
            part = dot_nn(coef[...], VV[:, cols])
            for j, ref in enumerate((dc0, *dcy)):
                ref[:, cols] = part[j * rows : (j + 1) * rows].astype(ref.dtype)
            for j, ref in enumerate(dcz):
                ref[:, cols] = part[nn + j * half : nn + (j + 1) * half]

    dc0, *dcs = call(
        "near_captions", near_captions_kernel,
        [vm(mat, F32)] + [vm(mat)] * (Y - 1) + [vm(hmat, F32)] * (2 * (Z - 1)),
        [coef_a, VV, dv_d],
        flops=2 * 24 * rows * rows * width, limit=limit,
    )
    dcy, dcz = dcs[: Y - 1], dcs[Y - 1 :]

    def add_kernel(*refs):
        total = refs[0][...].astype(F32)
        for ref in refs[1:-1]:
            total += ref[...].astype(F32)
        refs[-1][...] = total.astype(BF16)

    def add(name, *terms):
        return call(name, add_kernel, [vm(terms[0].shape)], terms)[0]

    def captions_back(h, *after):
        sums = []
        for s in range(Z - 1):
            far = [
                hand_on("far_" + "ab"[h], swap(dcd[2 * (s * (Y - 1) + t - 1) + h], "row", 2 * t), *after, flops=(4, 0)[h] * LONG // 4)
                for t in range(1, Y)
            ]
            sums.append(add("add_" + "ab"[h], dcz[2 * s + h], *far))
        return sums, [swap(sums[s], "col", 4 * (s + 1)) for s in range(Z - 1)]

    sums_a, got_a = captions_back(0, dc0)
    dcd = [hand_on("far_b", b, dv_d) if i % 2 else b for i, b in enumerate(dcd)]
    def near_clips_kernel(S1, S2, G1, G2, after, dv0, dvx, dvz):
        for i in range(width // CHUNK):
            cols = pl.ds(i * CHUNK, CHUNK)
            part = dot_tn(G1[:, :n3], S1[:, cols]) + dot_tn(G2[:, :n3], S2[:, cols])
            for j, ref in enumerate((dv0, dvx, dvz)):
                ref[:, cols] = part[j * rows : (j + 1) * rows].astype(ref.dtype)

    dv0, dvx, dvz = call(
        "near_clips", near_clips_kernel, [vm(mat, F32), vm(mat), vm(mat, F32)], [S1, S2, G1, G2, sums_a[0]],
        flops=2 * 24 * rows * rows * width, limit=limit,
    )

    sums_b, got_b = captions_back(1, dvz)
    sum_v = add("add_clips", dvz, far_v)
    got_z = swap(sum_v, "col", 2)
    got_h = [[hand_on("captions_back", b, sum_v, flops=3 * LONG) for b in got] for got in (got_a, got_b)]
    dcy = [hand_on("near_y", b, sum_v) for b in dcy]
    dvx = hand_on("near_x", dvx, sum_v)
    got_y = [hand_on("captions_y", swap(dcy[t - 1], "row", 2 * t), sum_v, flops=LONG) for t in range(1, Y)]
    got_x = hand_on("clips_x", swap(dvx, "row", 1), sum_v, flops=4 * LONG)

    def losses_kernel(l_a, l_m, l_c, l_d, after, *refs):
        loss_0, loss_x, loss_z = refs[-3:]
        total = l_c[...] + l_d[...]
        own = total[:, :n3] + l_a[...]
        loss_0[...] = own[:, :n1]
        loss_x[0:1, :] = own[:, n1 : 2 * n1]
        loss_x[1:2, :] = total[:, n3:] + l_m[...]
        loss_z[...] = own[:, 2 * n1 :]

    def add_loss_kernel(loss_z, arrived, got, sum_v, out):
        out[...] = loss_z[...] + arrived[1:2, :]

    loss_0, loss_x, loss_z = call(
        "losses", losses_kernel, [vm((1, n1), F32), vm((2, n1), F32), vm((1, n1), F32)],
        [loss_a, loss_m, loss_c, loss_d, sums_a[0]],
    )
    far_loss = hand_on("losses_x", swap(loss_x, "row", 1), *sums_b)
    (sum_loss,) = call("add_loss", add_loss_kernel, [vm((1, n1), F32)], [loss_z, far_loss, got_b[0], sum_v])
    got_loss = swap(sum_loss, "col", 2)

    def finish(name, losses, consts, hat, inverse, own, whole, halves, *after):
        tail = 3 + bool(losses)

        def finish_kernel(consts, hat_ref, inverse_ref, *refs):
            adds, (grad, *loss, buf, sems) = refs[: -1 - tail - len(after)], refs[-1 - tail :]
            copies = []
            if not losses:
                loss[0][...] = jnp.zeros((8, 128), F32)
            if losses:
                out, lbuf = loss
                loss_0, far_loss, got_loss = adds[:3]
                lbuf[...] = loss_0[...] + far_loss[0:1, :] + got_loss[...]
                copies.append(pltpu.make_async_copy(lbuf, out, sems.at[2]))
                copies[-1].start()
            adds = adds[len(losses) :]
            for i in range(2):
                part = pl.ds(i * half, half)
                total = adds[0][part, :]
                for ref in adds[1 : 1 + len(whole)]:
                    total += ref[part, :].astype(F32)
                for ref in adds[1 + len(whole) :][i * len(halves[0]) : (i + 1) * len(halves[0])]:
                    total += ref[...].astype(F32)
                total = total * consts[0:1, 0:1]
                hat = hat_ref[part, :]
                along = jnp.sum(hat * total, axis=1, keepdims=True)
                buf[part, :] = inverse_ref[part, :] * (total - hat * along)
                copies.append(pltpu.make_async_copy(buf.at[part], grad.at[part], sems.at[i]))
                copies[-1].start()
            for copy in copies:
                copy.wait()

        return call(
            name, finish_kernel,
            [jax.ShapeDtypeStruct(mat, F32)]
            + ([jax.ShapeDtypeStruct((1, rows), F32)] if losses else [vm((8, 128), F32)]),
            [consts, hat, inverse, *losses, own, *whole, *halves[0], *halves[1], *after], out_spec="hh" if losses else "hv",
            scratch=[pltpu.VMEM((1, rows), F32)] * bool(losses)
            + [pltpu.VMEM(mat, F32), pltpu.SemaphoreType.DMA((3,))],
        )

    gc, done = finish("finish_captions", [], consts, chat, cinv, dc0, got_y, got_h, sum_loss)
    got_z = hand_on("clips_back", got_z, done, flops=3 * LONG)
    gv, clip_loss = finish(
        "finish_clips", [loss_0, far_loss, got_loss], consts, vhat, vinv, dv0, [got_x, got_z], ([], [])
    )
    return clip_loss.reshape(rows), gv, gc


def solution(mesh):
    return jax.shard_map(
        shards,
        mesh=mesh,
        in_specs=(P(("row", "col"), None), P(("col", "row"), None), P(), P(), P()),
        out_specs=(P(("row", "col")), P(("row", "col"), None), P(("col", "row"), None)),
        check_vma=False,
    )
```

```python
import jax
import jax.numpy as jnp
from jax import lax
from jax.experimental import pallas as pl
from jax.experimental.pallas import tpu as pltpu
from jax.sharding import PartitionSpec as P

F32, BF16 = jnp.float32, jnp.bfloat16
MIB = 1024 * 1024
CHUNK = 256
PARTS = 4
LONG = 10**10
SPECS = {
    "s": pl.BlockSpec(memory_space=pltpu.SMEM),
    "v": pl.BlockSpec(memory_space=pltpu.VMEM),
    "h": pl.BlockSpec(memory_space=pl.ANY),
}


def vm(shape, dtype=BF16):
    return pltpu.VMEM(shape, dtype)


def call(name, kernel, out_shape, args, spec="v", out_spec="v", limit=4, flops=0, scratch=(), aliases={}):
    space = {"v": pltpu.VMEM, "h": pltpu.HBM}
    if spec in space:
        args = [pltpu.with_memory_space_constraint(a, space[spec]) for a in args]
    return pl.pallas_call(
        kernel,
        name=name,
        out_shape=out_shape,
        in_specs=[SPECS[spec]] * len(args),
        out_specs=[SPECS[s] for s in (out_spec if len(out_spec) > 1 else out_spec * len(out_shape))],
        scratch_shapes=list(scratch),
        input_output_aliases=aliases,
        compiler_params=pltpu.CompilerParams(vmem_limit_bytes=limit * MIB),
        cost_estimate=pl.CostEstimate(flops=flops, bytes_accessed=0, transcendentals=0),
    )(*args)


def hand_on(name, block, *after, flops=0):
    return call(
        name, lambda *refs: None, [vm(block.shape, block.dtype)], [block, *after],
        aliases={0: 0}, flops=flops,
    )[0]


def unit_rows(rows):
    inverse = lax.rsqrt(jnp.sum(rows * rows, axis=1, keepdims=True) + 1e-06)
    return rows * inverse, inverse


def dot_nt(a, b):
    return lax.dot_general(a, b, (((1,), (1,)), ((), ())), preferred_element_type=F32)


def dot_tn(a, b):
    return lax.dot_general(a, b, (((0,), (0,)), ((), ())), preferred_element_type=F32)


def dot_nn(a, b):
    return jnp.dot(a, b, preferred_element_type=F32)


def log1p_sum(e):
    rows = e.shape[0]
    u = e
    for _ in range(3):
        rows //= 2
        a, b = u[:rows], u[rows:]
        u = a + b + a * b
    series = u * (1.0 - u * (0.5 - u * (1.0 / 3.0 - u * 0.25)))
    logs = jnp.where(u < 0.01, series, jnp.log(1.0 + u))
    return jnp.sum(logs, axis=0, keepdims=True)


def pairs(dots, scale, shift, base, labels, counted):
    logits = dots * scale + shift
    match = lax.broadcasted_iota(jnp.int32, logits.shape, 0) == labels - base
    e = jnp.exp(-jnp.abs(logits))
    whole = 1.0 + e
    over = pl.reciprocal(whole, approx=True)
    over = over * (2.0 - whole * over)
    sigmoid = jnp.where(logits >= 0.0, over, e * over)
    coef = (sigmoid - jnp.where(match, 1.0, 0.0)).astype(BF16)
    if not counted:
        return coef, None
    e, logits, match = e[:, :counted], logits[:, :counted], match[:, :counted]
    linear = jnp.maximum(jnp.where(match, -logits, logits), 0.0)
    return coef, jnp.sum(linear, axis=0, keepdims=True) + log1p_sum(e)


def stack(target, blocks):
    at = 0
    for b in blocks:
        target[pl.ds(at, b.shape[0]), :] = b[...]
        at += b.shape[0]


def shards(film, text, matched, sharpness, offset):
    rows, width = film.shape
    half = rows // 2
    R, C = lax.axis_size("row"), lax.axis_size("col")
    Y, Z = R // 2, C // 4
    mat, hmat = (rows, width), (half, width)
    limit = 6 + 2 * (Y * Z * 2 * rows) // 1024

    def swap(value, axis, bits):
        size = lax.axis_size(axis)
        return lax.ppermute(value, axis, [(i, i ^ bits) for i in range(size)])

    def first_caption(s, t, k):
        r, c = lax.axis_index("row"), lax.axis_index("col")
        return ((c ^ (4 * s + k)) * R + (r ^ (2 * t))) * rows

    def clip_index(x, z, k):
        r, c = lax.axis_index("row"), lax.axis_index("col")
        return (r ^ x) * C + (c ^ (2 * z + k))

    near = [(0, t) for t in range(Y)]
    up = [(s, 0) for s in range(1, Z)]
    diag = [(s, t) for s in range(1, Z) for t in range(1, Y)]
    clip_order = [(x, z, k) for k in range(2) for z in range(2) for x in range(2)]
    nn, na, nd = len(near) * rows, len(near + up) * rows, len(diag) * rows
    n1, n3, n4, n7 = rows, 3 * rows, 4 * rows, 7 * rows

    def strip(consts, blocks, k, captions, clips, labels, counted, put):
        scale, shift = consts[0:1, 0:1], consts[1:2, 0:1]
        losses = []
        for left in range(0, clips.shape[0], CHUNK):
            right = min(left + CHUNK, clips.shape[0])
            dots = dot_nt(captions, clips[left:right])
            count = max(0, min(counted - left, right - left))
            total = 0.0
            for i, (s, t) in enumerate(blocks):
                block = dots[i * rows : (i + 1) * rows]
                base = first_caption(s, t, k)
                coef, add = pairs(block, scale, shift, base, labels[:, left:right], count)
                put(i * rows, left, coef)
                total = total + add if count else None
            if count:
                losses.append(total)
        return jnp.concatenate(losses, axis=1) if losses else None

    def put_in(target, first=0, left=0):
        def put(at, column, coef):
            target[pl.ds(first + at, coef.shape[0]), pl.ds(left + column, coef.shape[1])] = coef
        return put

    def normalize_kernel(film, text, matched, v16, c16, va, vb, vhat, chat, vinv, cinv, labels, fbuf, tbuf, mbuf, sems):
        step = rows // PARTS
        get_matched = pltpu.make_async_copy(matched, mbuf, sems.at[2 * PARTS])
        copies = []
        for j, (src, buf) in enumerate(((film, fbuf), (text, tbuf))):
            for i in range(PARTS):
                part = pl.ds(i * step, step)
                copies.append(pltpu.make_async_copy(src.at[part], buf.at[part], sems.at[j * PARTS + i]))
        for copy in copies:
            copy.start()
        get_matched.start()
        for copy in copies[:PARTS]:
            copy.wait()
        hat, inverse = unit_rows(fbuf[...])
        vhat[...], vinv[...], v16[...] = hat, inverse, hat.astype(BF16)
        va[...] = hat[:half].astype(BF16)
        vb[...] = hat[half:].astype(BF16)
        for copy in copies[PARTS:]:
            copy.wait()
        hat, inverse = unit_rows(tbuf[...])
        chat[...], cinv[...], c16[...] = hat, inverse, hat.astype(BF16)
        get_matched.wait()
        labels[...] = jnp.concatenate(
            [mbuf[pl.ds(clip_index(*p), 1), :] for p in clip_order], axis=1
        )

    matched = matched.reshape(-1, rows)
    v16, c16, va, vb, vhat, chat, vinv, cinv, labels = call(
        "normalize", normalize_kernel,
        [vm(mat), vm(mat)] + [vm(hmat)] * 2 + [vm(mat, F32), vm(mat, F32), vm((rows, 1), F32), vm((rows, 1), F32),
         vm((1, 8 * rows), jnp.int32)],
        [film, text, matched], spec="h", limit=8,
        scratch=[pltpu.VMEM(mat, F32)] * 2
        + [pltpu.VMEM(matched.shape, jnp.int32), pltpu.SemaphoreType.DMA((2 * PARTS + 1,))],
    )

    def consts_kernel(scale, shift, out):
        out[0:1, :] = jnp.full((1, 128), scale[0], F32)
        out[1:2, :] = jnp.full((1, 128), shift[0], F32)

    (consts,) = call("consts", consts_kernel, [vm((2, 128), F32)], [sharpness, offset], spec="s")

    def join(name, *blocks):
        def join_kernel(*refs):
            stack(refs[-1], refs[:-1])

        return call(name, join_kernel, [vm((sum(b.shape[0] for b in blocks), width))], blocks)[0]

    v_z = [hand_on("clips_z", swap(b, "col", 2), flops=n * LONG // 4) for b, n in ((va, 4), (vb, 24))]
    c_z = [hand_on("captions_z", swap(c16, "col", 4 * s), consts, flops=4 * LONG // 4) for s in range(1, Z)]
    c_y = [swap(c16, "row", 2 * t) for t in range(1, Y)]
    v_x = swap(v16, "row", 1)
    v_d = [hand_on("clips_d", swap(b, "row", 1), flops=LONG) for b in v_z]
    c_d = [swap(b, "row", 2 * t) for b in c_z for t in range(1, Y)]
    c_y = [hand_on("captions_y", b, c_z[0]) for b in c_y]
    N = join("near_blocks", c16, *c_y, v16, v_x, *v_z)
    N_k = hand_on("near_other", swap(N, "col", 1), flops=4 * LONG // 4)
    cz_k = [swap(b, "col", 1) for b in c_z]
    v_d = join("diagonal_clips", *v_d)
    vd_k = swap(v_d, "col", 1)

    def early_kernel(consts, labels, N, N_k, *refs):
        n = len(up)
        cz, czk, (S1, p, q, loss) = refs[:n], refs[n : 2 * n], refs[2 * n :]
        stack(S1, [N.at[:nn], *cz, N_k.at[:nn], *czk])
        own = N[nn:, :]
        loss[...] = strip(
            consts, near + up, 0, S1[:na, :], own, labels[:, :n3], n3, put_in(p)
        ) + strip(consts, near + up, 1, S1[na:, :], own, labels[:, :n3], n3, put_in(q))
        strip(
            consts, near + up, 0, S1[:na, :], N_k[nn:, :], labels[:, n4:n7], 0, put_in(p, left=n3)
        )

    S1, p, q, loss_a = call(
        "early_pairs", early_kernel,
        [vm((2 * na, width)), vm((na, 2 * n3)), vm((na, n3)), vm((1, n3), F32)],
        [consts, labels, N, N_k, *c_z, *cz_k],
        flops=2 * 27 * rows * rows * width, limit=limit,
    )

    def middle_kernel(consts, labels, N, N_k, vd, vdk, S1, p, q, VV, G1, coef, loss):
        stack(VV, [N.at[nn:], vd, N_k.at[nn:], vdk])
        coef[:, :n3] = p[:, :n3]
        coef[:, n4:n7] = p[:, n3:]
        G1[na:, :n3] = q[...]
        late = labels[:, n3:n4]
        loss[...] = strip(
            consts, near + up, 0, S1[:na, :], vd[...], late, n1, put_in(coef, left=n3)
        ) + strip(consts, near + up, 1, S1[na:, :], vd[...], late, n1, put_in(G1, na, n3))
        strip(consts, near + up, 0, S1[:na, :], vdk[...], labels[:, n7:], 0, put_in(coef, left=n7))
        G1[:na, :] = coef[:, :n4]

    VV, G1, coef_a, loss_m = call(
        "middle_pairs", middle_kernel,
        [vm((8 * n1, width)), vm((2 * na, n4)), vm((na, 8 * n1)), vm((1, n1), F32)],
        [consts, labels, N, N_k, v_d, vd_k, S1, p, q],
        flops=2 * 9 * rows * rows * width, limit=limit,
    )
    c_d = [hand_on("captions_d", b, loss_m, flops=3 * LONG) for b in c_d]
    D_k = [swap(b, "col", 1) for b in c_d]

    def far_captions_kernel(consts, labels, VV, *refs):
        n = len(diag)
        caps, (loss, p, *sums, D, coef) = refs[:n], refs[n:]
        stack(D, caps)
        loss[...] = strip(consts, diag, 0, D[...], VV[...], labels[...], n4, put_in(coef))
        p[...] = coef[:, :n4]
        for i in range(width // CHUNK):
            cols = pl.ds(i * CHUNK, CHUNK)
            part = dot_nn(coef[...], VV[:, cols])
            for j, ref in enumerate(sums):
                ref[:, cols] = part[j * half : (j + 1) * half].astype(BF16)

    loss_c, p_d, *dcd = call(
        "far_captions", far_captions_kernel,
        [vm((1, n4), F32), vm((nd, n4))] + [vm(hmat)] * (2 * len(diag)),
        [consts, labels, VV, *c_d],
        flops=2 * 16 * rows * rows * width, limit=limit,
        scratch=[pltpu.VMEM((nd, width), BF16), pltpu.VMEM((nd, 8 * n1), BF16)],
    )

    def far_clips_kernel(consts, labels, VV, S1, G1, p_d, *refs):
        n = len(diag)
        caps, (S2, G2, loss, dv) = refs[: 2 * n], refs[2 * n :]
        stack(S2, caps)
        G2[:nd, :] = p_d[...]
        loss[...] = strip(consts, diag, 1, S2[nd:, :], VV[:n4, :], labels[:, :n4], n4, put_in(G2, nd))
        for i in range(width // CHUNK):
            cols = pl.ds(i * CHUNK, CHUNK)
            dv[:, cols] = (dot_tn(G1[:, n3:], S1[:, cols]) + dot_tn(G2[:, n3:], S2[:, cols])).astype(BF16)

    S2, G2, loss_d, dv_d = call(
        "far_clips", far_clips_kernel,
        [vm((2 * nd, width)), vm((2 * nd, n4)), vm((1, n4), F32), vm(mat)],
        [consts, labels, VV, S1, G1, p_d, *c_d, *D_k],
        flops=2 * 12 * rows * rows * width, limit=limit,
    )
    far_v = swap(dv_d, "row", 1)

    def near_captions_kernel(coef, VV, after, dc0, *refs):
        dcy, dcz = refs[: Y - 1], refs[Y - 1 :]
        for i in range(width // CHUNK):
            cols = pl.ds(i * CHUNK, CHUNK)
            part = dot_nn(coef[...], VV[:, cols])
            for j, ref in enumerate((dc0, *dcy)):
                ref[:, cols] = part[j * rows : (j + 1) * rows].astype(ref.dtype)
            for j, ref in enumerate(dcz):
                ref[:, cols] = part[nn + j * half : nn + (j + 1) * half]

    dc0, *dcs = call(
        "near_captions", near_captions_kernel,
        [vm(mat, F32)] + [vm(mat)] * (Y - 1) + [vm(hmat, F32)] * (2 * (Z - 1)),
        [coef_a, VV, dv_d],
        flops=2 * 24 * rows * rows * width, limit=limit,
    )
    dcy, dcz = dcs[: Y - 1], dcs[Y - 1 :]

    def add_kernel(*refs):
        total = refs[0][...].astype(F32)
        for ref in refs[1:-1]:
            total += ref[...].astype(F32)
        refs[-1][...] = total.astype(BF16)

    def add(name, *terms):
        return call(name, add_kernel, [vm(terms[0].shape)], terms)[0]

    def captions_back(h, *after):
        sums = []
        for s in range(Z - 1):
            far = [
                hand_on("far_" + "ab"[h], swap(dcd[2 * (s * (Y - 1) + t - 1) + h], "row", 2 * t), *after, flops=(4, 0)[h] * LONG // 4)
                for t in range(1, Y)
            ]
            sums.append(add("add_" + "ab"[h], dcz[2 * s + h], *far))
        return sums, [swap(sums[s], "col", 4 * (s + 1)) for s in range(Z - 1)]

    sums_a, got_a = captions_back(0, dc0)
    dcd = [hand_on("far_b", b, dv_d) if i % 2 else b for i, b in enumerate(dcd)]
    def near_clips_kernel(S1, S2, G1, G2, after, dv0, dvx, dvz):
        for i in range(width // CHUNK):
            cols = pl.ds(i * CHUNK, CHUNK)
            part = dot_tn(G1[:, :n3], S1[:, cols]) + dot_tn(G2[:, :n3], S2[:, cols])
            for j, ref in enumerate((dv0, dvx, dvz)):
                ref[:, cols] = part[j * rows : (j + 1) * rows].astype(ref.dtype)

    dv0, dvx, dvz = call(
        "near_clips", near_clips_kernel, [vm(mat, F32), vm(mat), vm(mat, F32)], [S1, S2, G1, G2, sums_a[0]],
        flops=2 * 24 * rows * rows * width, limit=limit,
    )

    sums_b, got_b = captions_back(1, dvz)
    sum_v = add("add_clips", dvz, far_v)
    got_z = swap(sum_v, "col", 2)
    got_h = [[hand_on("captions_back", b, sum_v, flops=3 * LONG) for b in got] for got in (got_a, got_b)]
    dcy = [hand_on("near_y", b, sum_v) for b in dcy]
    dvx = hand_on("near_x", dvx, sum_v)
    got_y = [hand_on("captions_y", swap(dcy[t - 1], "row", 2 * t), sum_v, flops=LONG) for t in range(1, Y)]
    got_x = hand_on("clips_x", swap(dvx, "row", 1), sum_v, flops=4 * LONG)

    def losses_kernel(l_a, l_m, l_c, l_d, after, *refs):
        loss_0, loss_x, loss_z = refs[-3:]
        total = l_c[...] + l_d[...]
        own = total[:, :n3] + l_a[...]
        loss_0[...] = own[:, :n1]
        loss_x[0:1, :] = own[:, n1 : 2 * n1]
        loss_x[1:2, :] = total[:, n3:] + l_m[...]
        loss_z[...] = own[:, 2 * n1 :]

    def add_loss_kernel(loss_z, arrived, got, sum_v, out):
        out[...] = loss_z[...] + arrived[1:2, :]

    loss_0, loss_x, loss_z = call(
        "losses", losses_kernel, [vm((1, n1), F32), vm((2, n1), F32), vm((1, n1), F32)],
        [loss_a, loss_m, loss_c, loss_d, sums_a[0]],
    )
    far_loss = hand_on("losses_x", swap(loss_x, "row", 1), *sums_b)
    (sum_loss,) = call("add_loss", add_loss_kernel, [vm((1, n1), F32)], [loss_z, far_loss, got_b[0], sum_v])
    got_loss = swap(sum_loss, "col", 2)

    def finish(name, losses, consts, hat, inverse, own, whole, halves, *after):
        tail = 3 + bool(losses)

        def finish_kernel(consts, hat_ref, inverse_ref, *refs):
            adds, (grad, *loss, buf, sems) = refs[: -1 - tail - len(after)], refs[-1 - tail :]
            copies = []
            if not losses:
                loss[0][...] = jnp.zeros((8, 128), F32)
            if losses:
                out, lbuf = loss
                loss_0, far_loss, got_loss = adds[:3]
                lbuf[...] = loss_0[...] + far_loss[0:1, :] + got_loss[...]
                copies.append(pltpu.make_async_copy(lbuf, out, sems.at[2]))
                copies[-1].start()
            adds = adds[len(losses) :]
            for i in range(2):
                part = pl.ds(i * half, half)
                total = adds[0][part, :]
                for ref in adds[1 : 1 + len(whole)]:
                    total += ref[part, :].astype(F32)
                for ref in adds[1 + len(whole) :][i * len(halves[0]) : (i + 1) * len(halves[0])]:
                    total += ref[...].astype(F32)
                total = total * consts[0:1, 0:1]
                hat = hat_ref[part, :]
                along = jnp.sum(hat * total, axis=1, keepdims=True)
                buf[part, :] = inverse_ref[part, :] * (total - hat * along)
                copies.append(pltpu.make_async_copy(buf.at[part], grad.at[part], sems.at[i]))
                copies[-1].start()
            for copy in copies:
                copy.wait()

        return call(
            name, finish_kernel,
            [jax.ShapeDtypeStruct(mat, F32)]
            + ([jax.ShapeDtypeStruct((1, rows), F32)] if losses else [vm((8, 128), F32)]),
            [consts, hat, inverse, *losses, own, *whole, *halves[0], *halves[1], *after], out_spec="hh" if losses else "hv",
            scratch=[pltpu.VMEM((1, rows), F32)] * bool(losses)
            + [pltpu.VMEM(mat, F32), pltpu.SemaphoreType.DMA((3,))],
        )

    gc, done = finish("finish_captions", [], consts, chat, cinv, dc0, got_y, got_h, sum_loss)
    got_z = hand_on("clips_back", got_z, done, flops=3 * LONG)
    gv, clip_loss = finish(
        "finish_clips", [loss_0, far_loss, got_loss], consts, vhat, vinv, dv0, [got_x, got_z], ([], [])
    )
    return clip_loss.reshape(rows), gv, gc


def solution(mesh):
    return jax.shard_map(
        shards,
        mesh=mesh,
        in_specs=(P(("row", "col"), None), P(("col", "row"), None), P(), P(), P()),
        out_specs=(P(("row", "col")), P(("row", "col"), None), P(("col", "row"), None)),
        check_vma=False,
    )
```

```python
import jax
import jax.numpy as jnp
from jax import lax
from jax.experimental import pallas as pl
from jax.experimental.pallas import tpu as pltpu
from jax.sharding import PartitionSpec as P

F32, BF16 = jnp.float32, jnp.bfloat16
MIB = 1024 * 1024
CHUNK = 256
PARTS = 8
LONG = 10**10
SPECS = {
    "s": pl.BlockSpec(memory_space=pltpu.SMEM),
    "v": pl.BlockSpec(memory_space=pltpu.VMEM),
    "h": pl.BlockSpec(memory_space=pl.ANY),
}


def vm(shape, dtype=BF16):
    return pltpu.VMEM(shape, dtype)


def call(name, kernel, out_shape, args, spec="v", out_spec="v", limit=4, flops=0, scratch=(), aliases={}):
    space = {"v": pltpu.VMEM, "h": pltpu.HBM}
    if spec in space:
        args = [pltpu.with_memory_space_constraint(a, space[spec]) for a in args]
    return pl.pallas_call(
        kernel,
        name=name,
        out_shape=out_shape,
        in_specs=[SPECS[spec]] * len(args),
        out_specs=[SPECS[s] for s in (out_spec if len(out_spec) > 1 else out_spec * len(out_shape))],
        scratch_shapes=list(scratch),
        input_output_aliases=aliases,
        compiler_params=pltpu.CompilerParams(vmem_limit_bytes=limit * MIB),
        cost_estimate=pl.CostEstimate(flops=flops, bytes_accessed=0, transcendentals=0),
    )(*args)


def hand_on(name, block, *after, flops=0):
    return call(
        name, lambda *refs: None, [vm(block.shape, block.dtype)], [block, *after],
        aliases={0: 0}, flops=flops,
    )[0]


def unit_rows(rows):
    inverse = lax.rsqrt(jnp.sum(rows * rows, axis=1, keepdims=True) + 1e-06)
    return rows * inverse, inverse


def dot_nt(a, b):
    return lax.dot_general(a, b, (((1,), (1,)), ((), ())), preferred_element_type=F32)


def dot_tn(a, b):
    return lax.dot_general(a, b, (((0,), (0,)), ((), ())), preferred_element_type=F32)


def dot_nn(a, b):
    return jnp.dot(a, b, preferred_element_type=F32)


def log1p_sum(e):
    rows = e.shape[0]
    u = e
    for _ in range(3):
        rows //= 2
        a, b = u[:rows], u[rows:]
        u = a + b + a * b
    series = u * (1.0 - u * (0.5 - u * (1.0 / 3.0 - u * 0.25)))
    logs = jnp.where(u < 0.01, series, jnp.log(1.0 + u))
    return jnp.sum(logs, axis=0, keepdims=True)


def pairs(dots, scale, shift, base, labels, counted):
    logits = dots * scale + shift
    match = lax.broadcasted_iota(jnp.int32, logits.shape, 0) == labels - base
    e = jnp.exp(-jnp.abs(logits))
    whole = 1.0 + e
    over = pl.reciprocal(whole, approx=True)
    over = over * (2.0 - whole * over)
    sigmoid = jnp.where(logits >= 0.0, over, e * over)
    coef = (sigmoid - jnp.where(match, 1.0, 0.0)).astype(BF16)
    if not counted:
        return coef, None
    e, logits, match = e[:, :counted], logits[:, :counted], match[:, :counted]
    linear = jnp.maximum(jnp.where(match, -logits, logits), 0.0)
    return coef, jnp.sum(linear, axis=0, keepdims=True) + log1p_sum(e)


def stack(target, blocks):
    at = 0
    for b in blocks:
        target[pl.ds(at, b.shape[0]), :] = b[...]
        at += b.shape[0]


def shards(film, text, matched, sharpness, offset):
    rows, width = film.shape
    half = rows // 2
    R, C = lax.axis_size("row"), lax.axis_size("col")
    Y, Z = R // 2, C // 4
    mat, hmat = (rows, width), (half, width)
    limit = 6 + 2 * (Y * Z * 2 * rows) // 1024

    def swap(value, axis, bits):
        size = lax.axis_size(axis)
        return lax.ppermute(value, axis, [(i, i ^ bits) for i in range(size)])

    def first_caption(s, t, k):
        r, c = lax.axis_index("row"), lax.axis_index("col")
        return ((c ^ (4 * s + k)) * R + (r ^ (2 * t))) * rows

    def clip_index(x, z, k):
        r, c = lax.axis_index("row"), lax.axis_index("col")
        return (r ^ x) * C + (c ^ (2 * z + k))

    near = [(0, t) for t in range(Y)]
    up = [(s, 0) for s in range(1, Z)]
    diag = [(s, t) for s in range(1, Z) for t in range(1, Y)]
    clip_order = [(x, z, k) for k in range(2) for z in range(2) for x in range(2)]
    nn, na, nd = len(near) * rows, len(near + up) * rows, len(diag) * rows
    n1, n3, n4, n7 = rows, 3 * rows, 4 * rows, 7 * rows

    def strip(consts, blocks, k, captions, clips, labels, counted, put):
        scale, shift = consts[0:1, 0:1], consts[1:2, 0:1]
        losses = []
        for left in range(0, clips.shape[0], CHUNK):
            right = min(left + CHUNK, clips.shape[0])
            dots = dot_nt(captions, clips[left:right])
            count = max(0, min(counted - left, right - left))
            total = 0.0
            for i, (s, t) in enumerate(blocks):
                block = dots[i * rows : (i + 1) * rows]
                base = first_caption(s, t, k)
                coef, add = pairs(block, scale, shift, base, labels[:, left:right], count)
                put(i * rows, left, coef)
                total = total + add if count else None
            if count:
                losses.append(total)
        return jnp.concatenate(losses, axis=1) if losses else None

    def put_in(target, first=0, left=0):
        def put(at, column, coef):
            target[pl.ds(first + at, coef.shape[0]), pl.ds(left + column, coef.shape[1])] = coef
        return put

    def normalize_kernel(film, text, matched, v16, c16, va, vb, vhat, chat, vinv, cinv, labels, fbuf, tbuf, mbuf, sems):
        step = rows // PARTS
        get_matched = pltpu.make_async_copy(matched, mbuf, sems.at[2 * PARTS])
        copies = []
        for j, (src, buf) in enumerate(((film, fbuf), (text, tbuf))):
            for i in range(PARTS):
                part = pl.ds(i * step, step)
                copies.append(pltpu.make_async_copy(src.at[part], buf.at[part], sems.at[j * PARTS + i]))
        for copy in copies:
            copy.start()
        get_matched.start()
        for copy in copies[:PARTS]:
            copy.wait()
        hat, inverse = unit_rows(fbuf[...])
        vhat[...], vinv[...], v16[...] = hat, inverse, hat.astype(BF16)
        va[...] = hat[:half].astype(BF16)
        vb[...] = hat[half:].astype(BF16)
        for copy in copies[PARTS:]:
            copy.wait()
        hat, inverse = unit_rows(tbuf[...])
        chat[...], cinv[...], c16[...] = hat, inverse, hat.astype(BF16)
        get_matched.wait()
        labels[...] = jnp.concatenate(
            [mbuf[pl.ds(clip_index(*p), 1), :] for p in clip_order], axis=1
        )

    matched = matched.reshape(-1, rows)
    v16, c16, va, vb, vhat, chat, vinv, cinv, labels = call(
        "normalize", normalize_kernel,
        [vm(mat), vm(mat)] + [vm(hmat)] * 2 + [vm(mat, F32), vm(mat, F32), vm((rows, 1), F32), vm((rows, 1), F32),
         vm((1, 8 * rows), jnp.int32)],
        [film, text, matched], spec="h", limit=8,
        scratch=[pltpu.VMEM(mat, F32)] * 2
        + [pltpu.VMEM(matched.shape, jnp.int32), pltpu.SemaphoreType.DMA((2 * PARTS + 1,))],
    )

    def consts_kernel(scale, shift, out):
        out[0:1, :] = jnp.full((1, 128), scale[0], F32)
        out[1:2, :] = jnp.full((1, 128), shift[0], F32)

    (consts,) = call("consts", consts_kernel, [vm((2, 128), F32)], [sharpness, offset], spec="s")

    def join(name, *blocks):
        def join_kernel(*refs):
            stack(refs[-1], refs[:-1])

        return call(name, join_kernel, [vm((sum(b.shape[0] for b in blocks), width))], blocks)[0]

    v_z = [hand_on("clips_z", swap(b, "col", 2), flops=n * LONG // 4) for b, n in ((va, 4), (vb, 24))]
    c_z = [hand_on("captions_z", swap(c16, "col", 4 * s), consts, flops=4 * LONG // 4) for s in range(1, Z)]
    c_y = [swap(c16, "row", 2 * t) for t in range(1, Y)]
    v_x = swap(v16, "row", 1)
    v_d = [hand_on("clips_d", swap(b, "row", 1), flops=2 * LONG // 4) for b in v_z]
    c_d = [swap(b, "row", 2 * t) for b in c_z for t in range(1, Y)]
    N = join("near_blocks", c16, *c_y, v16, v_x, *v_z)
    N_k = hand_on("near_other", swap(N, "col", 1), flops=4 * LONG // 4)
    cz_k = [swap(b, "col", 1) for b in c_z]
    v_d = join("diagonal_clips", *v_d)
    vd_k = swap(v_d, "col", 1)

    def early_kernel(consts, labels, N, N_k, *refs):
        n = len(up)
        cz, czk, (S1, p, q, loss) = refs[:n], refs[n : 2 * n], refs[2 * n :]
        stack(S1, [N.at[:nn], *cz, N_k.at[:nn], *czk])
        own = N[nn:, :]
        loss[...] = strip(
            consts, near + up, 0, S1[:na, :], own, labels[:, :n3], n3, put_in(p)
        ) + strip(consts, near + up, 1, S1[na:, :], own, labels[:, :n3], n3, put_in(q))
        strip(
            consts, near + up, 0, S1[:na, :], N_k[nn:, :], labels[:, n4:n7], 0, put_in(p, left=n3)
        )

    S1, p, q, loss_a = call(
        "early_pairs", early_kernel,
        [vm((2 * na, width)), vm((na, 2 * n3)), vm((na, n3)), vm((1, n3), F32)],
        [consts, labels, N, N_k, *c_z, *cz_k],
        flops=2 * 27 * rows * rows * width, limit=limit,
    )

    def middle_kernel(consts, labels, N, N_k, vd, vdk, S1, p, q, VV, G1, coef, loss):
        stack(VV, [N.at[nn:], vd, N_k.at[nn:], vdk])
        coef[:, :n3] = p[:, :n3]
        coef[:, n4:n7] = p[:, n3:]
        G1[na:, :n3] = q[...]
        late = labels[:, n3:n4]
        loss[...] = strip(
            consts, near + up, 0, S1[:na, :], vd[...], late, n1, put_in(coef, left=n3)
        ) + strip(consts, near + up, 1, S1[na:, :], vd[...], late, n1, put_in(G1, na, n3))
        strip(consts, near + up, 0, S1[:na, :], vdk[...], labels[:, n7:], 0, put_in(coef, left=n7))
        G1[:na, :] = coef[:, :n4]

    VV, G1, coef_a, loss_m = call(
        "middle_pairs", middle_kernel,
        [vm((8 * n1, width)), vm((2 * na, n4)), vm((na, 8 * n1)), vm((1, n1), F32)],
        [consts, labels, N, N_k, v_d, vd_k, S1, p, q],
        flops=2 * 9 * rows * rows * width, limit=limit,
    )
    c_d = [hand_on("captions_d", b, loss_m, flops=3 * LONG) for b in c_d]
    D_k = [swap(b, "col", 1) for b in c_d]

    def far_captions_kernel(consts, labels, VV, *refs):
        n = len(diag)
        caps, (loss, p, *sums, D, coef) = refs[:n], refs[n:]
        stack(D, caps)
        loss[...] = strip(consts, diag, 0, D[...], VV[...], labels[...], n4, put_in(coef))
        p[...] = coef[:, :n4]
        for i in range(width // CHUNK):
            cols = pl.ds(i * CHUNK, CHUNK)
            part = dot_nn(coef[...], VV[:, cols])
            for j, ref in enumerate(sums):
                ref[:, cols] = part[j * half : (j + 1) * half].astype(BF16)

    loss_c, p_d, *dcd = call(
        "far_captions", far_captions_kernel,
        [vm((1, n4), F32), vm((nd, n4))] + [vm(hmat)] * (2 * len(diag)),
        [consts, labels, VV, *c_d],
        flops=2 * 16 * rows * rows * width, limit=limit,
        scratch=[pltpu.VMEM((nd, width), BF16), pltpu.VMEM((nd, 8 * n1), BF16)],
    )

    def far_clips_kernel(consts, labels, VV, S1, G1, p_d, *refs):
        n = len(diag)
        caps, (S2, G2, loss, dv) = refs[: 2 * n], refs[2 * n :]
        stack(S2, caps)
        G2[:nd, :] = p_d[...]
        loss[...] = strip(consts, diag, 1, S2[nd:, :], VV[:n4, :], labels[:, :n4], n4, put_in(G2, nd))
        for i in range(width // CHUNK):
            cols = pl.ds(i * CHUNK, CHUNK)
            dv[:, cols] = (dot_tn(G1[:, n3:], S1[:, cols]) + dot_tn(G2[:, n3:], S2[:, cols])).astype(BF16)

    S2, G2, loss_d, dv_d = call(
        "far_clips", far_clips_kernel,
        [vm((2 * nd, width)), vm((2 * nd, n4)), vm((1, n4), F32), vm(mat)],
        [consts, labels, VV, S1, G1, p_d, *c_d, *D_k],
        flops=2 * 12 * rows * rows * width, limit=limit,
    )
    far_v = swap(dv_d, "row", 1)

    def near_captions_kernel(coef, VV, after, dc0, *refs):
        dcy, dcz = refs[: Y - 1], refs[Y - 1 :]
        for i in range(width // CHUNK):
            cols = pl.ds(i * CHUNK, CHUNK)
            part = dot_nn(coef[...], VV[:, cols])
            for j, ref in enumerate((dc0, *dcy)):
                ref[:, cols] = part[j * rows : (j + 1) * rows].astype(ref.dtype)
            for j, ref in enumerate(dcz):
                ref[:, cols] = part[nn + j * half : nn + (j + 1) * half]

    dc0, *dcs = call(
        "near_captions", near_captions_kernel,
        [vm(mat, F32)] + [vm(mat)] * (Y - 1) + [vm(hmat, F32)] * (2 * (Z - 1)),
        [coef_a, VV, dv_d],
        flops=2 * 24 * rows * rows * width, limit=limit,
    )
    dcy, dcz = dcs[: Y - 1], dcs[Y - 1 :]

    def add_kernel(*refs):
        total = refs[0][...].astype(F32)
        for ref in refs[1:-1]:
            total += ref[...].astype(F32)
        refs[-1][...] = total.astype(BF16)

    def add(name, *terms):
        return call(name, add_kernel, [vm(terms[0].shape)], terms)[0]

    def captions_back(h, *after):
        sums = []
        for s in range(Z - 1):
            far = [
                hand_on("far_" + "ab"[h], swap(dcd[2 * (s * (Y - 1) + t - 1) + h], "row", 2 * t), *after, flops=(4, 0)[h] * LONG // 4)
                for t in range(1, Y)
            ]
            sums.append(add("add_" + "ab"[h], dcz[2 * s + h], *far))
        return sums, [swap(sums[s], "col", 4 * (s + 1)) for s in range(Z - 1)]

    sums_a, got_a = captions_back(0, dc0)
    dcd = [hand_on("far_b", b, dv_d) if i % 2 else b for i, b in enumerate(dcd)]
    def near_clips_kernel(S1, S2, G1, G2, after, dv0, dvx, dvz):
        for i in range(width // CHUNK):
            cols = pl.ds(i * CHUNK, CHUNK)
            part = dot_tn(G1[:, :n3], S1[:, cols]) + dot_tn(G2[:, :n3], S2[:, cols])
            for j, ref in enumerate((dv0, dvx, dvz)):
                ref[:, cols] = part[j * rows : (j + 1) * rows].astype(ref.dtype)

    dv0, dvx, dvz = call(
        "near_clips", near_clips_kernel, [vm(mat, F32), vm(mat), vm(mat, F32)], [S1, S2, G1, G2, sums_a[0]],
        flops=2 * 24 * rows * rows * width, limit=limit,
    )

    sums_b, got_b = captions_back(1, dvz)
    sum_v = add("add_clips", dvz, far_v)
    got_z = swap(sum_v, "col", 2)
    got_h = [[hand_on("captions_back", b, sum_v, flops=3 * LONG) for b in got] for got in (got_a, got_b)]
    dcy = [hand_on("near_y", b, sum_v) for b in dcy]
    dvx = hand_on("near_x", dvx, sum_v)
    got_y = [hand_on("captions_y", swap(dcy[t - 1], "row", 2 * t), sum_v, flops=LONG) for t in range(1, Y)]
    got_x = hand_on("clips_x", swap(dvx, "row", 1), sum_v, flops=4 * LONG)

    def losses_kernel(l_a, l_m, l_c, l_d, after, *refs):
        loss_0, loss_x, loss_z = refs[-3:]
        total = l_c[...] + l_d[...]
        own = total[:, :n3] + l_a[...]
        loss_0[...] = own[:, :n1]
        loss_x[0:1, :] = own[:, n1 : 2 * n1]
        loss_x[1:2, :] = total[:, n3:] + l_m[...]
        loss_z[...] = own[:, 2 * n1 :]

    def add_loss_kernel(loss_z, arrived, got, sum_v, out):
        out[...] = loss_z[...] + arrived[1:2, :]

    loss_0, loss_x, loss_z = call(
        "losses", losses_kernel, [vm((1, n1), F32), vm((2, n1), F32), vm((1, n1), F32)],
        [loss_a, loss_m, loss_c, loss_d, sums_a[0]],
    )
    far_loss = hand_on("losses_x", swap(loss_x, "row", 1), *sums_b)
    (sum_loss,) = call("add_loss", add_loss_kernel, [vm((1, n1), F32)], [loss_z, far_loss, got_b[0], sum_v])
    got_loss = swap(sum_loss, "col", 2)

    def finish(name, losses, consts, hat, inverse, own, whole, halves, *after):
        tail = 3 + bool(losses)

        def finish_kernel(consts, hat_ref, inverse_ref, *refs):
            adds, (grad, *loss, buf, sems) = refs[: -1 - tail - len(after)], refs[-1 - tail :]
            copies = []
            if not losses:
                loss[0][...] = jnp.zeros((8, 128), F32)
            if losses:
                out, lbuf = loss
                loss_0, far_loss, got_loss = adds[:3]
                lbuf[...] = loss_0[...] + far_loss[0:1, :] + got_loss[...]
                copies.append(pltpu.make_async_copy(lbuf, out, sems.at[2]))
                copies[-1].start()
            adds = adds[len(losses) :]
            for i in range(2):
                part = pl.ds(i * half, half)
                total = adds[0][part, :]
                for ref in adds[1 : 1 + len(whole)]:
                    total += ref[part, :].astype(F32)
                for ref in adds[1 + len(whole) :][i * len(halves[0]) : (i + 1) * len(halves[0])]:
                    total += ref[...].astype(F32)
                total = total * consts[0:1, 0:1]
                hat = hat_ref[part, :]
                along = jnp.sum(hat * total, axis=1, keepdims=True)
                buf[part, :] = inverse_ref[part, :] * (total - hat * along)
                copies.append(pltpu.make_async_copy(buf.at[part], grad.at[part], sems.at[i]))
                copies[-1].start()
            for copy in copies:
                copy.wait()

        return call(
            name, finish_kernel,
            [jax.ShapeDtypeStruct(mat, F32)]
            + ([jax.ShapeDtypeStruct((1, rows), F32)] if losses else [vm((8, 128), F32)]),
            [consts, hat, inverse, *losses, own, *whole, *halves[0], *halves[1], *after], out_spec="hh" if losses else "hv",
            scratch=[pltpu.VMEM((1, rows), F32)] * bool(losses)
            + [pltpu.VMEM(mat, F32), pltpu.SemaphoreType.DMA((3,))],
        )

    gc, done = finish("finish_captions", [], consts, chat, cinv, dc0, got_y, got_h, sum_loss)
    got_z = hand_on("clips_back", got_z, done, flops=3 * LONG)
    gv, clip_loss = finish(
        "finish_clips", [loss_0, far_loss, got_loss], consts, vhat, vinv, dv0, [got_x, got_z], ([], [])
    )
    return clip_loss.reshape(rows), gv, gc


def solution(mesh):
    return jax.shard_map(
        shards,
        mesh=mesh,
        in_specs=(P(("row", "col"), None), P(("col", "row"), None), P(), P(), P()),
        out_specs=(P(("row", "col")), P(("row", "col"), None), P(("col", "row"), None)),
        check_vma=False,
    )
```
